32 devices in a mesh: fsdp: 4 (over y, x), ctx: 4 (over z), blk: 2 (over core).
Axes of the slice: x: 2, y: 2, z: 4, core: 2. Of those that a mesh axis runs over, the one named last changes fastest.
Arguments:
- latents: bfloat16 [4, 1024, 1152], P('fsdp', ('ctx', 'blk')), may hold values from -6 to 6
- text_embed: bfloat16 [4, 120, 1152], P('fsdp'), may hold values from -6 to 6
- timestep: float32 [4, 6912], P('fsdp'), may hold values from -1.5 to 1.5
- ada_table: bfloat16 [6, 1152], P(None, 'fsdp'), may hold values from -1.5 to 1.5
- w_attn_in: bfloat16 [1152, 3456], P('fsdp'), may hold values from -0.1875 to 0.1875
- w_attn_out: bfloat16 [1152, 1152], P('fsdp'), may hold values from -2 to 2
- w_cross_q: bfloat16 [1152, 1152], P('fsdp'), may hold values from -0.1875 to 0.1875
- w_cross_kv: bfloat16 [1152, 2304], P('fsdp'), may hold values from -0.1875 to 0.1875
- w_cross_out: bfloat16 [1152, 1152], P('fsdp'), may hold values from -0.75 to 0.75
- w_mlp_up: bfloat16 [1152, 4608], P('fsdp'), may hold values from -0.1875 to 0.1875
- w_mlp_down: bfloat16 [4608, 1152], P('fsdp'), may hold values from -0.09375 to 0.09375
- grad_out: bfloat16 [4, 1024, 1152], P('fsdp', ('ctx', 'blk')), may hold values from -6 to 6
Outputs:
- block_out: bfloat16 [4, 1024, 1152], P('fsdp', ('ctx', 'blk'))
- grad_latents: float32 [4, 1024, 1152], P('fsdp', ('ctx', 'blk'))
- grad_text: float32 [4, 120, 1152], P('fsdp')
- grad_timestep: float32 [4, 6912], P('fsdp')
- grad_table: float32 [6, 1152], P(None, ('fsdp', 'ctx', 'blk'))
- grad_attn_in: float32 [1152, 3456], P(('fsdp', 'ctx', 'blk'))
- grad_attn_out: float32 [1152, 1152], P(('fsdp', 'ctx', 'blk'))
- grad_cross_q: float32 [1152, 1152], P(('fsdp', 'ctx', 'blk'))
- grad_cross_kv: float32 [1152, 2304], P(('fsdp', 'ctx', 'blk'))
- grad_cross_out: float32 [1152, 1152], P(('fsdp', 'ctx', 'blk'))
- grad_mlp_up: float32 [1152, 4608], P(('fsdp', 'ctx', 'blk'))
- grad_mlp_down: float32 [4608, 1152], P(('fsdp', 'ctx', 'blk'))
- grad_shift_mlp: float32 [1152], P(('fsdp', 'ctx', 'blk'))
The draws below stay inside these ranges and needn't reach their ends.
All inputs are finite; a program needn't handle non-finite values.
Results may differ from the reference program's by a relative error of at most 0.023.
Values may be sent and summed in bfloat16 or wider, within the bound.
No kernel may reach another device: no remote copies, remote signals or barrier semaphores. Data moves between devices by JAX's collectives and lax.ppermute only.
A program may use at most 256 MiB of HBM per device.

```python
import jax
import jax.numpy as jnp
from jax import lax

D = 1152
HEADS = 16
HEAD = 72
FF = 4608
TEXT = 120
SEQ = 1024
LATENTS = 4


def block_levels(own_key, extent, pieces, low, high):
    loudness = 1.0
    for position, parts in pieces:
        heights = jax.random.uniform(jax.random.fold_in(jax.random.fold_in(own_key, 6), position), (parts,), jnp.float32, low / len(pieces), high / len(pieces))
        loudness = loudness * jnp.repeat(jnp.exp(heights), extent[position] // parts).reshape((-1,) + (1,) * (len(extent) - 1 - position))
    return loudness


def bell_draw(key, extent, deviation, limit, cuts=(), held_as=jnp.bfloat16):
    gain = block_levels(key, extent, cuts, -0.22, 0.18) if cuts else 1.0
    values = jax.random.normal(key, extent, jnp.float32) * deviation * gain
    return jnp.minimum(jnp.maximum(values, -limit), limit).astype(held_as)


def setup_inputs(seed: int = 0) -> dict:
    key_of = jax.random.split(jax.random.key(seed), 13)
    return {
        "latents": bell_draw(key_of[0], (LATENTS, SEQ, D), 1.0, 6.0, ((0, 4), (1, 8))),
        "text_embed": bell_draw(key_of[1], (LATENTS, TEXT, D), 1.0, 6.0, ((0, 4),)),
        "timestep": bell_draw(key_of[2], (LATENTS, 6 * D), 0.25, 1.5, ((0, 4),), jnp.float32),
        "ada_table": bell_draw(key_of[3], (6, D), 0.25, 1.5, ((1, 4),)),
        "w_attn_in": bell_draw(key_of[4], (D, 3 * D), D ** -0.5, 0.1875, ((0, 4),)),
        "w_attn_out": bell_draw(key_of[5], (D, D), (max(8, 8 * D // SEQ)) ** -0.5, 2.0, ((0, 4),)),
        "w_cross_q": bell_draw(key_of[6], (D, D), D ** -0.5, 0.1875, ((0, 4),)),
        "w_cross_kv": bell_draw(key_of[7], (D, 2 * D), D ** -0.5, 0.1875, ((0, 4),)),
        "w_cross_out": bell_draw(key_of[8], (D, D), (D // 16) ** -0.5, 0.75, ((0, 4),)),
        "w_mlp_up": bell_draw(key_of[9], (D, FF), D ** -0.5, 0.1875, ((0, 4),)),
        "w_mlp_down": bell_draw(key_of[10], (FF, D), FF ** -0.5, 0.09375, ((0, 4),)),
        "grad_out": bell_draw(key_of[11], (LATENTS, SEQ, D), 1.0, 6.0, ((0, 4), (1, 8))),
    }


@jax.custom_vjp
def low(v):
    return lax.optimization_barrier(v.astype(jnp.bfloat16)).astype(jnp.float32)

@jax.custom_vjp
def low_back(v):
    return v

def low_keep(v):
    return (low(v), None)

def low_pass(kept, grad):
    return (grad,)

def back_keep(v):
    return (v, None)

def back_low(kept, grad):
    return (low(grad),)
low.defvjp(low_keep, low_pass)
low_back.defvjp(back_keep, back_low)
highest = lax.Precision.HIGHEST
epsilon = 1e-06

def matmul(left, right):
    return jnp.matmul(left, right, precision=highest)

def layer_norm(values):
    centred = values - lax.optimization_barrier(jnp.mean(values, axis=-1, keepdims=True))
    variance = lax.optimization_barrier(jnp.mean(centred * centred, axis=-1, keepdims=True))
    return centred * lax.rsqrt(variance + epsilon)

def self_attention(queries, keys_all, values_all):
    row_block = min(512, queries.shape[0])
    blocks = queries.shape[0] // row_block
    scaling = HEAD ** (-0.5)

    def one_block(query_block):
        scores = low_back(scaling * jnp.einsum('qhe,khe->hqk', query_block, keys_all, precision=highest))
        weights = jax.nn.softmax(scores, axis=-1)
        mixed = jnp.einsum('hqk,khe->qhe', low(weights), values_all, precision=highest)
        return low_back(low(mixed))
    outputs = lax.map(jax.checkpoint(one_block), queries.reshape(blocks, row_block, HEADS, HEAD))
    return outputs.reshape(-1, HEADS * HEAD)

def forward_one(latent, text_one, stamp_one, table_f32, w_attn_in, w_attn_out, w_cross_q, w_cross_kv, w_cross_out, w_mlp_up, w_mlp_down):
    modulation = table_f32 + stamp_one.reshape(6, -1)
    shift_one = modulation[0]
    scale_one = modulation[1]
    gate_one = modulation[2]
    shift_two = modulation[3]
    scale_two = modulation[4]
    gate_two = modulation[5]
    scaling = HEAD ** (-0.5)
    normed_one = layer_norm(latent)
    modulated_one = low(normed_one * (1.0 + scale_one) + shift_one)
    packed = low_back(low(matmul(modulated_one, w_attn_in)))
    triple = packed.reshape(-1, 3, HEADS, HEAD)
    mixed = self_attention(triple[:, 0], triple[:, 1], triple[:, 2])
    branch_one = low_back(matmul(mixed, w_attn_out))
    first = latent + gate_one * branch_one
    cross_query = low_back(low(matmul(low(first), w_cross_q))).reshape(-1, HEADS, HEAD)
    cross_pairs = low_back(low(matmul(text_one, w_cross_kv))).reshape(-1, 2, HEADS, HEAD)
    cross_scores = low_back(scaling * jnp.einsum('qhe,khe->hqk', cross_query, cross_pairs[:, 0], precision=highest))
    cross_weights = jax.nn.softmax(cross_scores, axis=-1)
    cross_mixed = jnp.einsum('hqk,khe->qhe', low(cross_weights), cross_pairs[:, 1], precision=highest)
    cross_mixed = low_back(low(cross_mixed)).reshape(-1, HEADS * HEAD)
    second = first + low_back(matmul(cross_mixed, w_cross_out))
    normed_two = layer_norm(second)
    modulated_two = low(normed_two * (1.0 + scale_two) + shift_two)
    hidden_pre = low_back(matmul(modulated_two, w_mlp_up))
    hidden = low(jax.nn.gelu(hidden_pre, approximate=True))
    mlp_branch = low_back(matmul(hidden, w_mlp_down))
    return second + gate_two * mlp_branch

def reference(latents, text_embed, timestep, ada_table, w_attn_in, w_attn_out, w_cross_q, w_cross_kv, w_cross_out, w_mlp_up, w_mlp_down, grad_out):
    table_f32 = ada_table.astype(jnp.float32)
    weights = (w_attn_in.astype(jnp.float32), w_attn_out.astype(jnp.float32), w_cross_q.astype(jnp.float32), w_cross_kv.astype(jnp.float32), w_cross_out.astype(jnp.float32), w_mlp_up.astype(jnp.float32), w_mlp_down.astype(jnp.float32))

    def per_latent(totals_in, inputs_one):
        latent, text_one, stamp_one, cotangent = inputs_one
        result, pullback = jax.vjp(forward_one, latent.astype(jnp.float32), text_one.astype(jnp.float32), stamp_one, table_f32, *weights)
        gradients = pullback(cotangent.astype(jnp.float32))
        totals_out = tuple((running + gradient for running, gradient in zip(totals_in, gradients[3:])))
        return (totals_out, (result.astype(jnp.bfloat16), gradients[0], gradients[1], gradients[2]))
    initial = tuple((jnp.zeros_like(member) for member in (table_f32,) + weights))
    totals, outputs = lax.scan(per_latent, initial, (latents, text_embed, timestep, grad_out))
    return (outputs[0], outputs[1], outputs[2], outputs[3], totals[0], totals[1], totals[2], totals[3], totals[4], totals[5], totals[6], totals[7], totals[0][3])
```

```python
import jax
import jax.numpy as jnp
from jax import lax
from jax.sharding import PartitionSpec as P

D = 1152
HEADS = 16
HEAD = 72
TEXT = 120

epsilon = 1e-06
bfloat = jnp.bfloat16
single = jnp.float32


def layer_norm(values):
    centred = values - jnp.mean(values, axis=-1, keepdims=True)
    variance = jnp.mean(centred * centred, axis=-1, keepdims=True)
    inverse = lax.rsqrt(variance + epsilon)
    return (centred * inverse, inverse)


def norm_back(grad_normed, normed, inverse):
    first_mean = jnp.mean(grad_normed, axis=-1, keepdims=True)
    second_mean = jnp.mean(grad_normed * normed, axis=-1, keepdims=True)
    return inverse * (grad_normed - first_mean - normed * second_mean)


def product(left, right, pattern):
    return jnp.einsum(pattern, left, right, preferred_element_type=single)


def swap(values, axis, step):
    size = lax.axis_size(axis)
    return lax.ppermute(values, axis, [(i, i ^ step) for i in range(size)])


def tree_sum(parts):
    while len(parts) > 1:
        parts = [parts[i] + parts[i + 1] for i in range(0, len(parts), 2)]
    return parts[0]


def pick(values, index):
    return lax.dynamic_index_in_dim(values, index, 0, keepdims=False)


def reorder(parts, index):
    count = len(parts)
    bit = 1
    parts = list(parts)
    while bit < count:
        flag = (index & bit) != 0
        parts = [jnp.where(flag, parts[i ^ bit], parts[i]) for i in range(count)]
        bit *= 2
    return parts


def gather_relative(values, axis):
    size = lax.axis_size(axis)
    return [values] + [swap(values, axis, step) for step in range(1, size)]


def scatter_sum(chunks, axis, own):
    size = lax.axis_size(axis)
    parts = [own] + [swap(chunks(step), axis, step).astype(single) for step in range(1, size)]
    return tree_sum(parts)


def exchange_zb(values):
    z = lax.axis_index("ctx")
    b = lax.axis_index("blk")
    size = values.shape[0]
    by_core = jnp.moveaxis(values, 1, 0)
    keep = pick(by_core, b)
    taken = swap(pick(by_core, 1 - b), "blk", 1)
    pair = jnp.stack([keep, taken], axis=1)
    parts = [pick(pair, z)] + [swap(pick(pair, z ^ step), "ctx", step) for step in range(1, size)]
    nat = jnp.stack(reorder(parts, z), 0)
    return jnp.stack(reorder([nat[:, 0], nat[:, 1]], b), 1)


def rows_permuted(values, f_size, z_size):
    piece = D // (f_size * z_size * 2)
    return (
        values.T.reshape(f_size * z_size, 2, piece, -1).transpose(1, 0, 2, 3).reshape(2, D // 2, -1)
    )


def core_sum(left_t, right):
    b = lax.axis_index("blk")
    send = product(pick(left_t, 1 - b), right, "kt,tn->kn").astype(bfloat)
    keep = product(pick(left_t, b), right, "kt,tn->kn")
    return keep + swap(send, "blk", 1).astype(single)


def plane_sum(half):
    f = lax.axis_index("fsdp")
    f_size = lax.axis_size("fsdp")
    rows = half.reshape(f_size, half.shape[0] // f_size, half.shape[1])
    low = rows.astype(bfloat)
    return scatter_sum(lambda step: pick(low, f ^ step), "fsdp", pick(rows, f))


def depth_sum(rows):
    z = lax.axis_index("ctx")
    low = rows.astype(bfloat)
    return scatter_sum(lambda step: pick(low, z ^ step), "ctx", pick(rows, z))


def shards(
    latents,
    text_embed,
    timestep,
    ada_table,
    w_attn_in,
    w_attn_out,
    w_cross_q,
    w_cross_kv,
    w_cross_out,
    w_mlp_up,
    w_mlp_down,
    grad_out,
):
    f_size = lax.axis_size("fsdp")
    z_size = lax.axis_size("ctx")
    group = 2 * z_size
    f = lax.axis_index("fsdp")
    z = lax.axis_index("ctx")
    b = lax.axis_index("blk")
    g = 2 * z + b
    tok = latents.shape[1]
    total = tok * group
    heads_here = HEADS // group
    wide = heads_here * HEAD
    kv_wide = 2 * D // group
    rows_f = D // f_size
    scaling = HEAD ** (-0.5)

    x = latents[0].astype(single)
    cotangent = grad_out[0].astype(single)
    text = text_embed[0]

    table = jnp.concatenate(reorder(gather_relative(ada_table, "fsdp"), f), axis=1)
    modulation = table.astype(single) + timestep.reshape(6, D)
    shift_one, scale_one, gate_one, shift_two, scale_two, gate_two = [
        modulation[i][None] for i in range(6)
    ]
    normed_one, inverse_one = layer_norm(x)
    modulated_one = (normed_one * (1.0 + scale_one) + shift_one).astype(bfloat)

    own_in = jnp.concatenate(
        [
            lax.dynamic_slice(w_attn_in, (0, i * D + g * wide), (rows_f, wide)) for i in range(3)
        ]
        + [lax.dynamic_slice(w_cross_kv, (0, g * kv_wide), (rows_f, kv_wide))],
        axis=1,
    )
    proj = jnp.concatenate(reorder(gather_relative(own_in, "fsdp"), f), axis=0)
    w_in = proj[:, : 3 * wide]
    w_kv = proj[:, 3 * wide :]

    near = jnp.stack(gather_relative(modulated_one, "ctx"), 0)
    x_all = jnp.stack([near, swap(near, "blk", 1)], 0).reshape(total, D)

    squares = jnp.stack([w_attn_out, w_cross_q, w_cross_out], 0).reshape(3, 2, rows_f // 2, D)
    half = lax.dynamic_index_in_dim(squares, b, 1, keepdims=False)
    square_full = jnp.zeros((3, f_size, 2, rows_f // 2, D), bfloat)
    square_full = lax.dynamic_update_slice(square_full, squares[:, None], (0, f, 0, 0, 0))
    for step in range(1, f_size):
        got = swap(half, "fsdp", step)
        other = swap(got, "blk", 1)
        square_full = lax.dynamic_update_slice(
            square_full, got[:, None, None], (0, f ^ step, b, 0, 0)
        )
        square_full = lax.dynamic_update_slice(
            square_full, other[:, None, None], (0, f ^ step, 1 - b, 0, 0)
        )
    attn_out, cross_q, cross_out = [square_full[i].reshape(D, D) for i in range(3)]

    ff = w_mlp_up.shape[1] // f_size
    up_half = lax.dynamic_slice(w_mlp_up, (b * (rows_f // 2), 0), (rows_f // 2, f_size * ff))
    up_full = jnp.zeros((f_size, 2, rows_f // 2, ff), bfloat)
    up_own = lax.dynamic_slice(w_mlp_up, (0, f * ff), (rows_f, ff)).reshape(1, 2, rows_f // 2, ff)
    up_full = lax.dynamic_update_slice(up_full, up_own, (f, 0, 0, 0))
    for step in range(1, f_size):
        got = swap(
            lax.dynamic_slice(up_half, (0, (f ^ step) * ff), (rows_f // 2, ff)), "fsdp", step
        )
        other = swap(got, "blk", 1)
        up_full = lax.dynamic_update_slice(up_full, got[None, None], (f ^ step, b, 0, 0))
        up_full = lax.dynamic_update_slice(up_full, other[None, None], (f ^ step, 1 - b, 0, 0))
    mlp_up = up_full.reshape(D, ff)
    mlp_down = w_mlp_down

    branch_two_grad = (gate_two * cotangent).astype(bfloat)
    branch_two_all = jnp.concatenate(gather_relative(branch_two_grad, "fsdp"), axis=0)

    pairs_here = product(w_kv, text, "dn,sd->ns").astype(bfloat)
    pairs_near = jnp.stack(reorder(gather_relative(pairs_here, "ctx"), z), 0)
    pairs_all = jnp.stack(reorder([pairs_near, swap(pairs_near, "blk", 1)], b), 1)
    pairs_all = pairs_all.reshape(2, HEADS, HEAD, TEXT)
    text_keys, text_values = pairs_all[0], pairs_all[1]

    packed = product(x_all, w_in, "td,de->te").astype(bfloat)
    packed = packed.reshape(total, 3, heads_here, HEAD)
    query, key, value = packed[:, 0], packed[:, 1], packed[:, 2]
    scores = scaling * product(query, key, "qhe,khe->hqk")
    top = jnp.max(scores, axis=-1, keepdims=True)
    exponent = jnp.exp(scores - top)
    weights = exponent / jnp.sum(exponent, axis=-1, keepdims=True)
    weights_low = weights.astype(bfloat)
    mixed_here = product(weights_low, value, "hqk,khe->heq").astype(bfloat)

    def tokens_to_owner(values):
        n = values.shape[0]
        parts = values.reshape(n, 2, z_size, tok).transpose(1, 2, 0, 3)
        taken = swap(parts[1], "blk", 1)
        pair = jnp.stack([parts[0], taken], axis=1)
        got = [pair[0]] + [swap(pair[step], "ctx", step) for step in range(1, z_size)]
        nat = jnp.stack(reorder(got, z), 0)
        return jnp.stack(reorder([nat[:, 0], nat[:, 1]], b), 1).reshape(group * n, tok)

    def tokens_to_heads(values):
        n = values.shape[0] // group
        parts = values.reshape(z_size, 2, n, tok)
        nat = jnp.stack(reorder([parts[i] for i in range(z_size)], z), 0)
        near = [nat[0]] + [swap(nat[step], "ctx", step) for step in range(1, z_size)]
        near = jnp.stack(near, 0)
        keep, send = reorder([near[:, 0], near[:, 1]], b)
        both = jnp.stack([keep, swap(send, "blk", 1)], 0)
        return both.transpose(2, 0, 1, 3).reshape(n, total)

    mixed_t = tokens_to_owner(mixed_here.reshape(wide, total))
    branch_one = product(mixed_t, attn_out, "dt,de->te")
    first = x + gate_one * branch_one
    first_low = first.astype(bfloat)
    cross_query = product(first_low, cross_q, "td,de->te").astype(bfloat).reshape(tok, HEADS, HEAD)
    cross_scores = scaling * product(cross_query, text_keys, "qhe,hek->hqk")
    cross_max = jnp.max(cross_scores, axis=-1, keepdims=True)
    cross_exp = jnp.exp(cross_scores - cross_max)
    cross_weights = cross_exp / jnp.sum(cross_exp, axis=-1, keepdims=True)
    cross_low = cross_weights.astype(bfloat)
    cross_mixed = product(cross_low, text_values, "hqk,hek->qhe").astype(bfloat).reshape(tok, D)
    second = first + product(cross_mixed, cross_out, "td,de->te")
    normed_two, inverse_two = layer_norm(second)
    modulated_two = (normed_two * (1.0 + scale_two) + shift_two).astype(bfloat)

    x_two_all = jnp.concatenate(gather_relative(modulated_two, "fsdp"), axis=0)
    hidden_pre = product(x_two_all, mlp_up, "td,df->tf")
    hidden, gelu_back = jax.vjp(lambda values: jax.nn.gelu(values, approximate=True), hidden_pre)
    hidden_low = hidden.astype(bfloat)
    grad_hidden = product(branch_two_all, mlp_down, "td,fd->tf")
    grad_pre = gelu_back(grad_hidden)[0].astype(bfloat)

    def from_plane(partial):
        parts = partial.reshape(f_size, tok, D)
        low = parts.astype(bfloat)
        return scatter_sum(lambda step: low[step], "fsdp", parts[0])

    grad_mod_two = from_plane(product(grad_pre, mlp_up, "tf,df->td"))
    mlp_branch = from_plane(product(hidden_low, mlp_down, "tf,fd->td"))
    block_out = (second + gate_two * mlp_branch).astype(bfloat)
    grad_gate_two = jnp.sum(cotangent * mlp_branch, axis=0)

    grad_scale_two = jnp.sum(grad_mod_two * normed_two, axis=0)
    grad_shift_two = jnp.sum(grad_mod_two, axis=0)
    grad_second = cotangent + norm_back(grad_mod_two * (1.0 + scale_two), normed_two, inverse_two)
    grad_cross_branch = grad_second.astype(bfloat)
    grad_cross_mixed = (
        product(grad_cross_branch, cross_out, "te,de->td").astype(bfloat).reshape(tok, HEADS, HEAD)
    )
    grad_cross_weights = product(grad_cross_mixed, text_values, "qhe,hek->hqk")
    grad_cross_values = product(grad_cross_mixed, cross_low, "qhe,hqk->hek")
    inner_cross = jnp.sum(cross_weights * grad_cross_weights, axis=-1, keepdims=True)
    grad_cross_scores = (cross_weights * (grad_cross_weights - inner_cross)).astype(bfloat)
    grad_cross_query = (
        (scaling * product(grad_cross_scores, text_keys, "hqk,hek->qhe"))
        .astype(bfloat)
        .reshape(tok, D)
    )
    grad_cross_keys = scaling * product(cross_query, grad_cross_scores, "qhe,hqk->hek")
    grad_first = grad_second + product(grad_cross_query, cross_q, "te,de->td")
    grad_gate_one = jnp.sum(grad_first * branch_one, axis=0)
    grad_branch_one = (gate_one * grad_first).astype(bfloat)
    grad_mixed_t = product(attn_out, grad_branch_one, "de,te->dt").astype(bfloat)

    grad_mixed = tokens_to_heads(grad_mixed_t).reshape(heads_here, HEAD, total)
    grad_weights = product(grad_mixed, value, "heq,khe->hqk")
    grad_values = product(weights_low, grad_mixed, "hqk,heq->khe")
    inner = jnp.sum(weights * grad_weights, axis=-1, keepdims=True)
    grad_scores = (weights * (grad_weights - inner)).astype(bfloat)
    grad_query = scaling * product(grad_scores, key, "hqk,khe->qhe")
    grad_keys = scaling * product(grad_scores, query, "hqk,qhe->khe")
    grad_packed = (
        jnp.stack([grad_query, grad_keys, grad_values], 1).astype(bfloat).reshape(total, 3 * wide)
    )

    grad_part = product(grad_packed, w_in, "te,de->td").reshape(2, z_size, tok, D)
    grad_near = grad_part[0] + swap(grad_part[1].astype(bfloat), "blk", 1).astype(single)
    grad_near_low = grad_near.astype(bfloat)
    grad_mod_one = scatter_sum(lambda step: grad_near_low[step], "ctx", grad_near[0])
    grad_scale_one = jnp.sum(grad_mod_one * normed_one, axis=0)
    grad_shift_one = jnp.sum(grad_mod_one, axis=0)
    grad_latents = grad_first + norm_back(grad_mod_one * (1.0 + scale_one), normed_one, inverse_one)

    stamp = jnp.stack(
        [
            grad_shift_one,
            grad_scale_one,
            grad_gate_one,
            grad_shift_two,
            grad_scale_two,
            grad_gate_two,
        ],
        axis=0,
    )
    stamp = stamp + swap(stamp, "blk", 1)
    stamp = tree_sum(gather_relative(stamp, "ctx"))
    grad_timestep = stamp.reshape(1, 6 * D)
    table_sum = tree_sum(gather_relative(stamp, "fsdp"))
    own = D // (f_size * group)
    grad_table = lax.dynamic_slice(table_sum, (0, (f * group + g) * own), (6, own))

    pair_grads = jnp.concatenate([grad_cross_keys, grad_cross_values], 0)
    pair_grads = pair_grads.reshape(z_size, 2, kv_wide, TEXT).transpose(1, 0, 2, 3)
    pair_near = pick(pair_grads, b) + swap(pick(pair_grads, 1 - b).astype(bfloat), "blk", 1).astype(single)
    grad_pairs = depth_sum(pair_near).astype(bfloat)
    grad_text_part = product(w_kv, grad_pairs, "dn,ns->ds").reshape(2, D // 2, TEXT)
    text_near = pick(grad_text_part, b) + swap(
        pick(grad_text_part, 1 - b).astype(bfloat), "blk", 1
    ).astype(single)
    text_rows = depth_sum(text_near.reshape(z_size, D // group, TEXT))
    text_rows = jnp.concatenate(reorder(gather_relative(text_rows, "ctx"), z), 0)
    text_rows = jnp.concatenate(reorder([text_rows, swap(text_rows, "blk", 1)], b), 0)
    grad_text = text_rows.T[None]

    def column_parallel(partial):
        rows = partial.reshape(f_size, rows_f, -1)
        low = rows.astype(bfloat)
        mine = scatter_sum(lambda step: pick(low, f ^ step), "fsdp", pick(rows, f)).astype(bfloat)
        got = exchange_zb(mine.reshape(z_size, 2, own, -1)).astype(single)
        return got.reshape(group, own, -1).transpose(1, 0, 2)

    grad_attn_in = column_parallel(product(x_all, grad_packed, "td,te->de"))
    grad_attn_in = (
        grad_attn_in.reshape(own, group, 3, wide).transpose(0, 2, 1, 3).reshape(own, 3 * D)
    )
    grad_cross_kv = column_parallel(product(text, grad_pairs, "sd,ns->dn")).reshape(own, 2 * D)

    def square(left_t, right):
        rows = plane_sum(core_sum(left_t, right))
        return depth_sum(rows.reshape(z_size, own, D))

    grad_attn_out = square(rows_permuted(mixed_t.T, f_size, z_size), grad_branch_one)
    grad_cross_q = square(rows_permuted(first_low, f_size, z_size), grad_cross_query)
    grad_cross_out = square(rows_permuted(cross_mixed, f_size, z_size), grad_cross_branch)

    up_rows = core_sum(rows_permuted(x_two_all, f_size, z_size), grad_pre)
    up_rows = up_rows.astype(bfloat).reshape(f_size, z_size * own, ff)
    up_got = [pick(up_rows, f)] + [
        swap(pick(up_rows, f ^ step), "fsdp", step) for step in range(1, f_size)
    ]
    up_got = jnp.stack(up_got, 0).reshape(f_size, z_size, own, ff).transpose(1, 0, 2, 3)
    up_sum = depth_sum(up_got.astype(single).reshape(z_size, f_size * own, ff))
    up_sum = up_sum.reshape(f_size, own, ff)
    grad_mlp_up = jnp.concatenate(reorder([up_sum[i] for i in range(f_size)], f), axis=1)

    own_down = w_mlp_down.shape[0] // group
    down_t = hidden_low.T.reshape(z_size, 2, own_down, -1).transpose(1, 0, 2, 3)
    down_t = down_t.reshape(2, z_size * own_down, -1)
    down_rows = core_sum(down_t, branch_two_all)
    grad_mlp_down = depth_sum(down_rows.reshape(z_size, own_down, D))

    return (
        block_out[None],
        grad_latents[None],
        grad_text,
        grad_timestep,
        grad_table,
        grad_attn_in,
        grad_attn_out,
        grad_cross_q,
        grad_cross_kv,
        grad_cross_out,
        grad_mlp_up,
        grad_mlp_down,
        grad_table[3],
    )


def solution(mesh):
    placed = (
        P("fsdp", ("ctx", "blk"), None),
        P("fsdp", None, None),
        P("fsdp", None),
        P(None, "fsdp"),
        P("fsdp", None),
        P("fsdp", None),
        P("fsdp", None),
        P("fsdp", None),
        P("fsdp", None),
        P("fsdp", None),
        P("fsdp", None),
        P("fsdp", ("ctx", "blk"), None),
    )
    owned = P(("fsdp", "ctx", "blk"), None)
    return jax.shard_map(
        shards,
        mesh=mesh,
        in_specs=placed,
        out_specs=(
            P("fsdp", ("ctx", "blk"), None),
            P("fsdp", ("ctx", "blk"), None),
            P("fsdp", None, None),
            P("fsdp", None),
            P(None, ("fsdp", "ctx", "blk")),
            owned,
            owned,
            owned,
            owned,
            owned,
            owned,
            owned,
            P(("fsdp", "ctx", "blk")),
        ),
        check_vma=False,
    )
```

```python
import functools

import jax
import jax.numpy as jnp
from jax import lax
from jax.experimental import pallas as pl
from jax.experimental.pallas import tpu as pltpu
from jax.sharding import PartitionSpec as P

D = 1152
HEADS = 16
HEAD = 72
TEXT = 120

epsilon = 1e-06
bfloat = jnp.bfloat16
single = jnp.float32
scaling = HEAD ** (-0.5)

VMEM = pl.BlockSpec(memory_space=pltpu.VMEM)
SMEM = pl.BlockSpec(memory_space=pltpu.SMEM)
ANY = pl.BlockSpec(memory_space=pl.ANY)


def layer_norm(values):
    centred = values - jnp.mean(values, axis=-1, keepdims=True)
    variance = jnp.mean(centred * centred, axis=-1, keepdims=True)
    inverse = lax.rsqrt(variance + epsilon)
    return (centred * inverse, inverse)


def norm_back(grad_normed, normed, inverse):
    first_mean = jnp.mean(grad_normed, axis=-1, keepdims=True)
    second_mean = jnp.mean(grad_normed * normed, axis=-1, keepdims=True)
    return inverse * (grad_normed - first_mean - normed * second_mean)


def dot(left, right, axes=(1, 0)):
    return lax.dot_general(
        left, right, (((axes[0],), (axes[1],)), ((), ())), preferred_element_type=single
    )


def shape(dims, dtype=bfloat):
    return jax.ShapeDtypeStruct(tuple(dims), dtype)


def call(body, outs, args, specs, scratch=(), megabytes=40, micros=2):
    return pl.pallas_call(
        body,
        out_shape=tuple(outs),
        in_specs=list(specs),
        out_specs=tuple(VMEM for _ in outs),
        scratch_shapes=list(scratch),
        compiler_params=pltpu.CompilerParams(vmem_limit_bytes=megabytes * 2**20),
        cost_estimate=pl.CostEstimate(
            flops=int(micros * 1.15e9), bytes_accessed=1, transcendentals=0
        ),
    )(*args)


def swap(values, axis, step):
    size = lax.axis_size(axis)
    return lax.ppermute(values, axis, [(i, i ^ step) for i in range(size)])


def bits_of(size):
    return size.bit_length() - 1


def step_of(place, core, size):
    bits = bits_of(size)
    back = sum(((place >> j) & 1) << (bits - 1 - j) for j in range(bits))
    return jnp.where(core == 0, place, back)


def cross(values, axis, stage):
    size = lax.axis_size(axis)
    pairs = []
    for i in range(size):
        for core in range(2):
            step = 1 << stage if core == 0 else 1 << (bits_of(size) - 1 - stage)
            pairs.append((2 * i + core, 2 * (i ^ step) + core))
    return lax.ppermute(values, (axis, "blk"), pairs)


def doubling(values, axis):
    held = [values]
    found = []
    for stage in range(bits_of(lax.axis_size(axis))):
        message = held[0][None] if stage == 0 else jnp.stack(held, 0)
        got = cross(message, axis, stage)
        found += [(got, i) for i in range(len(held))]
        held = held + [got[i] for i in range(len(held))]
    return found


def halving(keep, send, axis):
    for stage in reversed(range(bits_of(lax.axis_size(axis)))):
        got = cross(send, axis, stage)
        if stage == 0:
            return keep[0], got[0]
        half = keep.shape[0] // 2
        send = (keep[half:] + got[half:].astype(single)).astype(bfloat)
        keep = keep[:half] + got[:half].astype(single)


def half_sum(keep, send, axis):
    own, got = halving(keep, send, axis)
    return own + got.astype(single)


def tree_sum(parts):
    while len(parts) > 1:
        parts = [parts[i] + parts[i + 1] for i in range(0, len(parts), 2)]
    return parts[0]


def reorder(parts, index):
    count = len(parts)
    bit = 1
    parts = list(parts)
    while bit < count:
        flag = (index & bit) != 0
        parts = [jnp.where(flag, parts[i ^ bit], parts[i]) for i in range(count)]
        bit *= 2
    return parts


def partners(values, axis):
    return [swap(values[step], axis, step) for step in range(1, lax.axis_size(axis))]


def unique(found):
    arrays = []
    for got, _ in found:
        if all(got is not other for other in arrays):
            arrays.append(got)
    return arrays


def after(values, *earlier):
    return lax.optimization_barrier((values,) + earlier)[0]


def aligned(index, unit):
    return pl.multiple_of(index, unit)


def project_text(ids, own_part, parts, text, own_wide, kv_wide, f_size):
    rows, cols = own_part.shape
    count = f_size
    n_parts = len(parts)

    def body(*refs):
        ids_ref, text_ref = refs[0], refs[1]
        own_ref = refs[2]
        part_refs = refs[3 : 3 + n_parts]
        w_ref, kv_ref, pairs_ref, table_ref = refs[3 + n_parts : 7 + n_parts]
        full, sems = refs[7 + n_parts :]
        f, b = ids_ref[0], ids_ref[2]
        sources = [own_ref] + [ref.at[i] for ref in part_refs for i in range(ref.shape[0])]
        copies = []
        for q, source in enumerate(sources):
            place = pl.ds(aligned((f ^ step_of(q, b, count)) * rows, 16), rows)
            copies.append(pltpu.make_async_copy(source, full.at[place, :], sems.at[q]))
        for copy in copies:
            copy.start()
        for copy in copies:
            copy.wait()
        turned = full[...].T
        w_ref[...] = turned[:own_wide]
        kv = turned[own_wide : own_wide + kv_wide]
        kv_ref[...] = kv
        pairs_ref[...] = dot(kv, text_ref[...], (1, 1)).astype(bfloat)
        table_ref[...] = turned[own_wide + kv_wide :].astype(single)

    return call(
        body,
        [
            shape((own_wide, D)),
            shape((kv_wide, D)),
            shape((kv_wide, TEXT)),
            shape((cols - own_wide - kv_wide, D), single),
        ],
        [ids, text, own_part] + list(parts),
        [SMEM, VMEM] + [ANY] * (1 + n_parts),
        [pltpu.VMEM((count * rows, cols), bfloat), pltpu.SemaphoreType.DMA((count,))],
        megabytes=16,
        micros=2.6,
    )


def attend_forward(ids, w_t, modulation, x_parts, x_kinds, heads_here, z_size):
    tok = x_parts[0].shape[-2]
    count = 2 * z_size
    total = count * tok
    width = 256 if total % 256 == 0 else tok
    per = width // tok
    n_parts = len(x_parts)

    def body(*refs):
        ids_ref, w_ref, mod_ref = refs[:3]
        x_refs = refs[3 : 3 + n_parts]
        near_ref, far_ref, qkv_ref, norm_ref, x_all = refs[3 + n_parts : 8 + n_parts]
        raw, sems = refs[8 + n_parts :]
        b = ids_ref[2]
        copies = []
        for ref, chunks in zip(x_refs, x_kinds):
            for i, chunk in enumerate(chunks):
                source = ref if len(ref.shape) == 2 else ref.at[i]
                target = raw.at[pl.ds(chunk * tok, tok), :]
                copies.append(pltpu.make_async_copy(source, target, sems.at[chunk]))
        for copy in copies:
            copy.start()
        for copy in copies:
            copy.wait()

        def project(j, carry):
            place = pl.ds(aligned(j * width, width), width)
            normed, _ = layer_norm(raw[place, :].astype(single))
            modulated = (normed * (1.0 + mod_ref[1:2]) + mod_ref[0:1]).astype(bfloat)
            x_all[place, :] = modulated
            got = dot(w_ref[...], modulated, (1, 1))
            for i in range(3 * heads_here):
                qkv_ref[i, :, place] = got[i * HEAD : (i + 1) * HEAD].astype(bfloat)
            return carry

        lax.fori_loop(0, total // width, project, 0)

        for h in range(heads_here):
            keys = qkv_ref[heads_here + h]
            values = qkv_ref[2 * heads_here + h]

            for j in range(total // width):
                place = pl.ds(j * width, width)
                scores = dot(keys, qkv_ref[h, :, place], (0, 0)) * scaling
                top = jnp.max(scores, axis=0, keepdims=True)
                exponent = jnp.exp(scores - top)
                summed = jnp.sum(exponent, axis=0, keepdims=True)
                weights = (exponent * (1.0 / summed)).astype(bfloat)
                mixed = dot(values, weights).astype(bfloat)
                norm_ref[h, :, place] = top + jnp.log(summed)
                for i in range(per):
                    chunk = j * per + i
                    piece = mixed[:, i * tok : (i + 1) * tok]
                    if chunk < z_size:
                        near_ref[step_of(chunk, b, z_size), h] = piece
                    else:
                        far_ref[step_of(chunk - z_size, 1 - b, z_size), h] = piece

    wide = heads_here * HEAD
    return call(
        body,
        [
            shape((z_size, heads_here, HEAD, tok)),
            shape((z_size, heads_here, HEAD, tok)),
            shape((3 * heads_here, HEAD, total)),
            shape((heads_here, 1, total), single),
            shape((total, D)),
        ],
        [ids, w_t, modulation] + list(x_parts),
        [SMEM, VMEM, VMEM] + [ANY] * n_parts,
        [pltpu.VMEM((total, D), bfloat), pltpu.SemaphoreType.DMA((count,))],
        megabytes=24,
        micros=12,
    )


def weight_copies(piece_refs, kinds, full, sems, f, b, rows):
    copies = []
    half = rows // 2
    for i, (ref, kind) in enumerate(zip(piece_refs, kinds)):
        sem = sems.at[i]
        if kind[0] == "whole":
            copies.append(pltpu.make_async_copy(ref, full, sem))
        elif kind[0] == "own":
            place = pl.ds(aligned(f * rows, 16), rows)
            copies.append(pltpu.make_async_copy(ref, full.at[kind[1], place, :], sem))
        else:
            core = b if kind[0] == "near" else 1 - b
            source = f ^ kind[2](core)
            place = pl.ds(aligned(source * rows + core * half, 16), half)
            target = full.at[:, place, :]
            ref = ref if kind[1] is None else ref.at[kind[1]]
            copies.append(pltpu.make_async_copy(ref, target, sem))
    return copies


def permute_rows(source, target, count, piece):
    for k in range(count):
        for core in range(2):
            target[core, pl.ds(k * piece, piece), :] = source[
                pl.ds((2 * k + core) * piece, piece), :
            ]


def token_forward(ids, near, far, got, x, modulation, pair_parts, pieces, kinds, f_size, z_size):
    tok = x.shape[0]
    heads_here = near.shape[1]
    rows = D // f_size
    own = D // (2 * f_size * z_size)
    kv_wide = D // z_size
    n_got, n_pieces, n_pairs = len(got), len(pieces), len(pair_parts)

    def body(*refs):
        ids_ref, near_ref, far_ref, x_ref, mod_ref = refs[:5]
        got_refs = refs[5 : 5 + n_got]
        pair_refs = refs[5 + n_got : 5 + n_got + n_pairs]
        at = 5 + n_got + n_pairs
        piece_refs = refs[at : at + n_pieces]
        rest = refs[at + n_pieces :]
        x_two_ref, second_ref, branch_ref, p_ref, cq_ref, keep_ref, send_ref, pairs_ref = rest[:8]
        full, mixed, pair_s, turned, left, sems = rest[8:]
        f, z, b = ids_ref[0], ids_ref[1], ids_ref[2]
        copies = weight_copies(piece_refs, kinds, full, sems, f, b, rows)
        for copy in copies:
            copy.start()

        def place(step, core, h):
            g = 2 * (z ^ step) + (b ^ core)
            return pl.ds(aligned((g * heads_here + h) * HEAD, 8), HEAD)

        for h in range(heads_here):
            mixed[place(0, 0, h), :] = near_ref[0, h].astype(single)
            mixed[place(0, 1, h), :] = far_ref[0, h].astype(single)
            for step in range(1, z_size):
                for core in range(2):
                    mixed[place(step, core, h), :] = got_refs[step - 1][core, h].astype(single)
        sources = [pair_refs[0]] + [ref.at[i] for ref in pair_refs[1:] for i in range(ref.shape[0])]
        for q, source in enumerate(sources):
            for core in range(2):
                g = 2 * (z ^ step_of(q, b, z_size)) + (b ^ core)
                pair_s[pl.ds(aligned(g * kv_wide, 8), kv_wide), :] = source[core].astype(single)
        pairs_ref[...] = pair_s[...]

        def keep_left(i, source):
            permute_rows(source, left, f_size * z_size, own)
            keep_ref[i] = left[b].astype(bfloat)
            send_ref[i] = left[1 - b].astype(bfloat)

        keep_left(0, mixed)
        shift_two, scale_two, gate_one = mod_ref[3:4], mod_ref[4:5], mod_ref[2:3]
        for copy in copies:
            copy.wait()
        branch = dot(mixed[...].T.astype(bfloat), full[0])
        branch_ref[...] = branch
        first = x_ref[...].astype(single) + gate_one * branch
        first_low = first.astype(bfloat)
        turned[...] = first_low.astype(single).T
        keep_left(1, turned)
        turned[...] = dot(first_low, full[1]).T
        cq_ref[...] = turned[...].astype(bfloat)
        for h in range(HEADS):
            rows_h = pl.ds(h * HEAD, HEAD)
            keys = pair_s[rows_h, :].astype(bfloat)
            values = pair_s[pl.ds(D + h * HEAD, HEAD), :].astype(bfloat)
            scores = dot(keys, turned[rows_h, :].astype(bfloat), (0, 0)) * scaling
            top = jnp.max(scores, axis=0, keepdims=True)
            exponent = jnp.exp(scores - top)
            weights = exponent * (1.0 / jnp.sum(exponent, axis=0, keepdims=True))
            p_ref[h] = weights
            mixed[rows_h, :] = dot(values, weights.astype(bfloat)).astype(bfloat).astype(single)
        second = first + dot(mixed[...].T.astype(bfloat), full[2])
        second_ref[...] = second
        normed, _ = layer_norm(second)
        x_two_ref[...] = (normed * (1.0 + scale_two) + shift_two).astype(bfloat)
        keep_left(2, mixed)

    return call(
        body,
        [
            shape((tok, D)),
            shape((tok, D), single),
            shape((tok, D), single),
            shape((HEADS, TEXT, tok), single),
            shape((D, tok)),
            shape((3, D // 2, tok)),
            shape((3, D // 2, tok)),
            shape((2 * D, TEXT), single),
        ],
        [ids, near, far, x, modulation] + list(got) + list(pair_parts) + list(pieces),
        [SMEM] + [VMEM] * (4 + n_got + n_pairs) + [ANY] * n_pieces,
        [
            pltpu.VMEM((3, D, D), bfloat),
            pltpu.VMEM((D, tok), single),
            pltpu.VMEM((2 * D, TEXT), single),
            pltpu.VMEM((D, tok), single),
            pltpu.VMEM((2, D // 2, tok), single),
            pltpu.SemaphoreType.DMA((n_pieces,)),
        ],
        megabytes=28,
        micros=7,
    )


def feed_forward(ids, x_parts, grad_hidden, pieces, kinds, ff, f_size):
    count = f_size
    n_parts = len(x_parts)
    tok = x_parts[0].shape[0]
    tile = 384 if ff % 384 == 0 else ff
    rows = D // f_size
    n_pieces = len(pieces)

    def body(*refs):
        ids_ref = refs[0]
        x_refs = refs[1 : 1 + n_parts]
        gh_ref = refs[1 + n_parts]
        piece_refs = refs[2 + n_parts : 2 + n_parts + n_pieces]
        rest = refs[2 + n_parts + n_pieces :]
        hidden_ref, pre_ref, keep_ref, send_ref = rest[:4]
        x_all, full, sems = rest[4:]
        up_ref = full.at[0]
        copies = weight_copies(piece_refs, kinds, full, sems, ids_ref[0], ids_ref[2], rows)
        for copy in copies:
            copy.start()
        x_all[0:tok, :] = x_refs[0][...]
        at = tok
        for ref in x_refs[1:]:
            for i in range(ref.shape[0]):
                x_all[at : at + tok, :] = ref[i]
                at += tok
        for copy in copies:
            copy.wait()

        def step(j, carry):
            place = pl.ds(aligned(j * tile, 128), tile) if ff > tile else pl.ds(0, tile)
            u = dot(x_all[...], up_ref[:, place])
            square = u * u
            t = jnp.tanh(0.7978845608028654 * u * (1.0 + 0.044715 * square))
            half = 0.5 * (1.0 + t)
            hidden_ref[:, place] = (u * half).astype(bfloat)
            slope = half + 0.5 * u * (1.0 - t * t) * (
                0.7978845608028654 * (1.0 + 0.134145 * square)
            )
            pre_ref[:, place] = (gh_ref[:, place] * slope).astype(bfloat)
            return carry

        if ff > tile:
            lax.fori_loop(0, ff // tile, step, 0)
        else:
            step(0, 0)
        part = dot(pre_ref[...], up_ref[...], (1, 1))
        for i in range(count):
            piece = part[i * tok : (i + 1) * tok]
            if i < count // 2:
                keep_ref[i] = piece
            else:
                send_ref[i - count // 2] = piece.astype(bfloat)

    total = count * tok
    return call(
        body,
        [
            shape((total, ff)),
            shape((total, ff)),
            shape((count // 2, tok, D), single),
            shape((count // 2, tok, D)),
        ],
        [ids] + list(x_parts) + [grad_hidden] + list(pieces),
        [SMEM] + [VMEM] * (n_parts + 1) + [ANY] * n_pieces,
        [
            pltpu.VMEM((total, D), bfloat),
            pltpu.VMEM((1, D, ff), bfloat),
            pltpu.SemaphoreType.DMA((n_pieces,)),
        ],
        megabytes=24,
        micros=7,
    )


def feed_forward_rest(ids, x_parts, hidden, pre, branch_grad, down, f_size, z_size):
    count = f_size
    n_parts = len(x_parts)
    tok = x_parts[0].shape[0]
    total = count * tok
    ff = hidden.shape[1]
    own = D // (2 * f_size * z_size)
    own_down = ff // (2 * z_size)
    merged = ff == D

    def body(*refs):
        ids_ref = refs[0]
        x_refs = refs[1 : 1 + n_parts]
        hidden_ref, pre_ref, grad_ref, down_ref = refs[1 + n_parts : 5 + n_parts]
        out = refs[5 + n_parts :]
        branch_keep, branch_send = out[:2]
        if merged:
            send_ref, dk_ref, uk_ref = out[2:5]
            ds_ref, us_ref = send_ref.at[0], send_ref.at[1]
        else:
            ds_ref, us_ref, dk_ref, uk_ref = out[2:6]
        flat, halves, flat_down, halves_down = out[-4:]
        b = ids_ref[2]
        part = dot(hidden_ref[...], down_ref[...])
        for i in range(count):
            piece = part[i * tok : (i + 1) * tok]
            if i < count // 2:
                branch_keep[i] = piece
            else:
                branch_send[i - count // 2] = piece.astype(bfloat)
        flat_down[...] = hidden_ref[...].T.astype(single)
        permute_rows(flat_down, halves_down, z_size, own_down)
        ds_ref[...] = dot(halves_down[1 - b].astype(bfloat), grad_ref[...]).astype(bfloat)
        dk_ref[...] = dot(halves_down[b].astype(bfloat), grad_ref[...])
        flat[:, 0:tok] = x_refs[0][...].T.astype(single)
        at = tok
        for ref in x_refs[1:]:
            for i in range(ref.shape[0]):
                flat[:, at : at + tok] = ref[i].T.astype(single)
                at += tok
        permute_rows(flat, halves, f_size * z_size, own)
        us_ref[...] = dot(halves[1 - b].astype(bfloat), pre_ref[...]).astype(bfloat)
        uk_ref[...] = dot(halves[b].astype(bfloat), pre_ref[...])

    outs = call(
        body,
        [shape((count // 2, tok, D), single), shape((count // 2, tok, D))]
        + ([shape((2, D // 2, D))] if merged else [shape((ff // 2, D)), shape((D // 2, ff))])
        + [shape((ff // 2, D), single), shape((D // 2, ff), single)],
        [ids] + list(x_parts) + [hidden, pre, branch_grad, down],
        [SMEM] + [VMEM] * (n_parts + 4),
        [
            pltpu.VMEM((D, total), single),
            pltpu.VMEM((2, D // 2, total), single),
            pltpu.VMEM((ff, total), single),
            pltpu.VMEM((2, ff // 2, total), single),
        ],
        megabytes=32,
        micros=6.6,
    )
    return outs[:2], outs[2:-2], outs[-2:]


def token_backward(
    ids, own, got, second, branch, cotangent, modulation, p, cq, pairs, pieces, kinds, f_size, z_size
):
    tok = second.shape[0]
    heads_here = HEADS // (2 * z_size)
    rows = D // f_size
    kv_wide = D // z_size
    n_got, n_pieces = len(got), len(pieces)

    def body(*refs):
        ids_ref, own_ref, second_ref, branch_ref, cot_ref, mod_ref, p_ref, cq_ref, pairs_ref = refs[:9]
        got_refs = refs[9 : 9 + n_got]
        piece_refs = refs[9 + n_got : 9 + n_got + n_pieces]
        rest = refs[9 + n_got + n_pieces :]
        near_ref, far_ref, right_ref, first_ref, stat_ref, pair_ref = rest[:6]
        full, turned, grads, low, sems = rest[6:]
        pair_s = pairs_ref
        f, z, b = ids_ref[0], ids_ref[1], ids_ref[2]
        copies = weight_copies(piece_refs, kinds, full, sems, f, b, rows)
        for copy in copies:
            copy.start()
        gate_one, scale_two = mod_ref[2:3], mod_ref[4:5]
        grad_mod = own_ref[...]
        for ref in got_refs:
            grad_mod = grad_mod + ref[...].astype(single)
        normed, inverse = layer_norm(second_ref[...])
        stat_ref[1:2] = jnp.sum(grad_mod, axis=0, keepdims=True)
        stat_ref[2:3] = jnp.sum(grad_mod * normed, axis=0, keepdims=True)
        grad_second = cot_ref[...].astype(single) + norm_back(
            grad_mod * (1.0 + scale_two), normed, inverse
        )
        grad_low = grad_second.astype(bfloat)
        right_ref[2] = grad_low
        for copy in copies:
            copy.wait()
        turned[...] = dot(full[2], grad_low, (1, 1))
        low[...] = cq_ref[...].astype(single)
        for h in range(HEADS):
            rows_h = pl.ds(h * HEAD, HEAD)
            keys = pair_s[rows_h, :].astype(bfloat)
            values = pair_s[pl.ds(D + h * HEAD, HEAD), :].astype(bfloat)
            grad_h = turned[rows_h, :].astype(bfloat)
            weights = p_ref[h]
            grad_weights = dot(values, grad_h, (0, 0))
            grads[pl.ds(D + h * HEAD, HEAD), :] = dot(grad_h, weights.astype(bfloat), (1, 1))
            inner = jnp.sum(weights * grad_weights, axis=0, keepdims=True)
            grad_scores = (weights * (grad_weights - inner)).astype(bfloat)
            turned[rows_h, :] = scaling * dot(keys, grad_scores)
            grads[rows_h, :] = scaling * dot(low[rows_h, :].astype(bfloat), grad_scores, (1, 1))
        pair_ref[...] = grads[...].astype(bfloat)
        grad_query = turned[...].T.astype(bfloat)
        right_ref[1] = grad_query
        grad_first = grad_second + dot(grad_query, full[1], (1, 1))
        first_ref[...] = grad_first
        stat_ref[0:1] = jnp.sum(grad_first * branch_ref[...], axis=0, keepdims=True)
        grad_branch = (gate_one * grad_first).astype(bfloat)
        right_ref[0] = grad_branch
        turned[...] = dot(full[0], grad_branch, (1, 1))
        for step in range(z_size):
            for core in range(2):
                target = near_ref if core == 0 else far_ref
                g = 2 * (z ^ step) + (b ^ core)
                for h in range(heads_here):
                    place = pl.ds(aligned((g * heads_here + h) * HEAD, 8), HEAD)
                    target[step, h] = turned[place, :].astype(bfloat)

    return call(
        body,
        [
            shape((z_size, heads_here, HEAD, tok)),
            shape((z_size, heads_here, HEAD, tok)),
            shape((3, tok, D)),
            shape((tok, D), single),
            shape((3, D), single),
            shape((2 * D, TEXT)),
        ],
        [ids, own, second, branch, cotangent, modulation, p, cq, pairs] + list(got) + list(pieces),
        [SMEM] + [VMEM] * (8 + n_got) + [ANY] * n_pieces,
        [
            pltpu.VMEM((3, D, D), bfloat),
            pltpu.VMEM((D, tok), single),
            pltpu.VMEM((2 * D, TEXT), single),
            pltpu.VMEM((D, tok), single),
            pltpu.SemaphoreType.DMA((n_pieces,)),
        ],
        megabytes=28,
        micros=8.5,
    )


def square_grads(ids, left, left_far, right, right_far, f_size):
    count, half, tok = left.shape
    part = half // f_size

    def body(*refs):
        ids_ref, left_ref, lf_ref, right_ref, rf_ref, keep_ref, send_ref = refs[:7]
        left_s, right_s, flat = refs[7:]
        f, b = ids_ref[0], ids_ref[2]
        for i in range(count):
            left_s[:, 0:tok] = left_ref[i]
            left_s[:, tok : 2 * tok] = lf_ref[i]
            right_s[0:tok, :] = right_ref[i]
            right_s[tok : 2 * tok, :] = rf_ref[i]
            value = dot(left_s[...], right_s[...])
            for k in range(f_size):
                flat[k] = value[k * part : (k + 1) * part]
            for q in range(f_size):
                value = flat[f ^ step_of(q, b, f_size)]
                if q < f_size // 2:
                    keep_ref[q, i] = value
                else:
                    send_ref[q - f_size // 2, i] = value.astype(bfloat)

    return call(
        body,
        [
            shape((f_size // 2, count, part, D), single),
            shape((f_size // 2, count, part, D)),
        ],
        [ids, left, left_far, right, right_far],
        [SMEM] + [VMEM] * 4,
        [
            pltpu.VMEM((half, 2 * tok), bfloat),
            pltpu.VMEM((2 * tok, D), bfloat),
            pltpu.VMEM((f_size, part, D), single),
        ],
        megabytes=20,
        micros=4,
    )


def split_sum(ids, index, keep, recv, count, direct):
    rows, cols = keep.shape
    part = rows // count
    unit = 16 if part % 16 == 0 else 8

    def body(ids_ref, keep_ref, recv_ref, own_ref, send_ref):
        i, b = ids_ref[index], ids_ref[2]
        for q in range(count):
            step = q if direct else step_of(q, b, count)
            place = pl.ds(aligned((i ^ step) * part, unit), part)
            value = keep_ref[place, :] + recv_ref[place, :].astype(single)
            if q < held:
                own_ref[q] = value
            else:
                send_ref[q - held] = value.astype(bfloat)

    held = 1 if direct else count // 2
    if part % 8:
        chunks = (keep + recv.astype(single)).reshape(count, part, cols)
        order = [
            lax.dynamic_index_in_dim(
                chunks, ids[index] ^ (q if direct else step_of(q, ids[2], count)), 0, keepdims=False
            )
            for q in range(count)
        ]
        return jnp.stack(order[:held], 0), jnp.stack(order[held:], 0).astype(bfloat)
    return call(
        body,
        [shape((held, part, cols), single), shape((count - held, part, cols))],
        [ids, keep, recv],
        [SMEM, VMEM, VMEM],
        megabytes=20,
        micros=1,
    )


def sum_split(ids, index, own, got, count, add):
    lead, rows, cols = own.shape
    part = rows // count
    n_got = len(got)
    groups = lead if add else lead * (1 + n_got)

    def body(*refs):
        ids_ref, own_ref = refs[:2]
        got_refs = refs[2 : 2 + n_got]
        keep_ref, send_ref, flat, chunks = refs[2 + n_got :]
        i, b = ids_ref[index], ids_ref[2]
        for k in range(lead):
            if add:
                value = own_ref[k]
                for ref in got_refs:
                    value = value + ref[k].astype(single)
                flat[k] = value
            else:
                flat[k] = own_ref[k]
                for j, ref in enumerate(got_refs):
                    flat[(j + 1) * lead + k] = ref[k].astype(single)
        for k in range(groups):
            for c in range(count):
                chunks[c, k] = flat[k, pl.ds(c * part, part), :]
        for q in range(count):
            value = chunks[i ^ step_of(q, b, count)]
            if q < count // 2:
                keep_ref[q] = value
            else:
                send_ref[q - count // 2] = value.astype(bfloat)

    return call(
        body,
        [
            shape((count // 2, groups, part, cols), single),
            shape((count // 2, groups, part, cols)),
        ],
        [ids, own] + list(got),
        [SMEM] + [VMEM] * (1 + n_got),
        [
            pltpu.VMEM((groups, rows, cols), single),
            pltpu.VMEM((count, groups, part, cols), single),
        ],
        megabytes=24,
        micros=2,
    )


def attend_backward(ids, qkv, norm, w_t, near, far, got, x_all, z_size):
    heads_here = near.shape[1]
    tok = near.shape[3]
    total = x_all.shape[0]
    count = total // tok
    width = 256 if total % 256 == 0 else tok
    wide3 = 3 * heads_here * HEAD
    n_got = len(got)

    def body(*refs):
        ids_ref, qkv_ref, norm_ref, w_ref, near_ref, far_ref = refs[:6]
        got_refs = refs[6 : 6 + n_got]
        x_ref, close_ref, away_ref, turned_ref = refs[6 + n_got : 10 + n_got]
        x_s, by_step, grad, flat, low, sem = refs[10 + n_got :]
        copy = pltpu.make_async_copy(x_ref, x_s, sem)
        copy.start()
        b = ids_ref[2]
        for h in range(heads_here):
            by_step[0, 0, h] = near_ref[0, h]
            by_step[1, 0, h] = far_ref[0, h]
            for step in range(1, z_size):
                for core in range(2):
                    by_step[core, step, h] = got_refs[step - 1][core, h]
            for core in range(2):
                for q in range(z_size):
                    at = (core * z_size + q) * tok
                    step = step_of(q, b ^ core, z_size)
                    grad[h, :, at : at + tok] = by_step[core, step, h]
        flat[...] = jnp.zeros_like(flat)
        for h in range(heads_here):
            keys = qkv_ref[heads_here + h]
            values = qkv_ref[2 * heads_here + h]
            rows_k = pl.ds((heads_here + h) * HEAD, HEAD)
            rows_v = pl.ds((2 * heads_here + h) * HEAD, HEAD)

            def block(j, carry):
                place = pl.ds(aligned(j * width, width), width)
                query = qkv_ref[h, :, place]
                grad_h = grad[h, :, place]
                scores = dot(keys, query, (0, 0)) * scaling
                weights = jnp.exp(scores - norm_ref[h, :, place])
                grad_weights = dot(values, grad_h, (0, 0))
                inner = jnp.sum(weights * grad_weights, axis=0, keepdims=True)
                grad_scores = (weights * (grad_weights - inner)).astype(bfloat)
                flat[rows_v, :] += dot(grad_h, weights.astype(bfloat), (1, 1))
                flat[pl.ds(h * HEAD, HEAD), place] = scaling * dot(keys, grad_scores)
                flat[rows_k, :] += scaling * dot(query, grad_scores, (1, 1))
                return carry

            lax.fori_loop(0, total // width, block, 0)
        low[...] = flat[...].astype(bfloat)

        def tokens(j, carry):
            place = pl.ds(aligned(j * tok, tok), tok)
            part = dot(low[:, place], w_ref[...], (0, 0))

            @pl.when(j < z_size)
            def _():
                close_ref[j] = part

            @pl.when(j >= z_size)
            def _():
                away_ref[j - z_size] = part.astype(bfloat)

            return carry

        lax.fori_loop(0, count, tokens, 0)
        copy.wait()
        turned_ref[...] = dot(low[...], x_s[...]).T

    return call(
        body,
        [
            shape((z_size, tok, D), single),
            shape((z_size, tok, D)),
            shape((D, wide3), single),
        ],
        [ids, qkv, norm, w_t, near, far] + list(got) + [x_all],
        [SMEM] + [VMEM] * (5 + n_got) + [ANY],
        [
            pltpu.VMEM((total, D), bfloat),
            pltpu.VMEM((2, z_size, heads_here, HEAD, tok), bfloat),
            pltpu.VMEM((heads_here, HEAD, total), bfloat),
            pltpu.VMEM((wide3, total), single),
            pltpu.VMEM((wide3, total), bfloat),
            pltpu.SemaphoreType.DMA,
        ],
        megabytes=28,
        micros=13.6,
    )


def column_grads(ids, turned, text, grad_pairs, kv_t, f_size):
    wide3 = turned.shape[1]
    kv_wide = grad_pairs.shape[0]
    rows = D // f_size
    cols = wide3 + kv_wide

    def body(*refs):
        ids_ref, turned_ref, text_ref, pairs_ref, kv_ref, keep_ref, send_ref = refs[:7]
        text_out, kv_s = refs[7:]
        f, b = ids_ref[0], ids_ref[2]
        pairs = pairs_ref[...]
        kv_s[...] = dot(text_ref[...], pairs, (0, 1))
        held = f_size // 2
        for q in range(f_size):
            place = pl.ds(aligned((f ^ step_of(q, b, f_size)) * rows, 8), rows)
            if q < held:
                keep_ref[q, :, 0:wide3] = turned_ref[place, :]
                keep_ref[q, :, wide3:cols] = kv_s[place, :]
            else:
                send_ref[q - held, :, 0:wide3] = turned_ref[place, :].astype(bfloat)
                send_ref[q - held, :, wide3:cols] = kv_s[place, :].astype(bfloat)
        text_out[...] = dot(pairs, kv_ref[...], (0, 0))

    return call(
        body,
        [
            shape((f_size // 2, rows, cols), single),
            shape((f_size // 2, rows, cols)),
            shape((TEXT, D), single),
        ],
        [ids, turned, text, grad_pairs, kv_t],
        [SMEM] + [VMEM] * 4,
        [pltpu.VMEM((D, kv_wide), single)],
        megabytes=20,
        micros=2.4,
    )


def finish(own, got, x, modulation, grad_first):
    tok = x.shape[0]
    n_got = len(got)

    def body(*refs):
        own_ref, x_ref, mod_ref, first_ref = refs[:4]
        got_refs = refs[4 : 4 + n_got]
        out_ref, stat_ref = refs[4 + n_got :]
        grad_mod = own_ref[...]
        for ref in got_refs:
            grad_mod = grad_mod + ref[...].astype(single)
        normed, inverse = layer_norm(x_ref[...].astype(single))
        stat_ref[0:1] = jnp.sum(grad_mod, axis=0, keepdims=True)
        stat_ref[1:2] = jnp.sum(grad_mod * normed, axis=0, keepdims=True)
        out_ref[...] = first_ref[...] + norm_back(grad_mod * (1.0 + mod_ref[1:2]), normed, inverse)

    return call(
        body,
        [shape((tok, D), single), shape((2, D), single)],
        [own, x, modulation, grad_first] + list(got),
        [VMEM] * (4 + n_got),
        micros=2,
    )


def shards(
    latents,
    text_embed,
    timestep,
    ada_table,
    w_attn_in,
    w_attn_out,
    w_cross_q,
    w_cross_kv,
    w_cross_out,
    w_mlp_up,
    w_mlp_down,
    grad_out,
):
    f_size = lax.axis_size("fsdp")
    z_size = lax.axis_size("ctx")
    group = 2 * z_size
    f = lax.axis_index("fsdp")
    z = lax.axis_index("ctx")
    b = lax.axis_index("blk")
    g = 2 * z + b
    ids = jnp.stack([f, z, b]).astype(jnp.int32)
    tok = latents.shape[1]
    heads_here = HEADS // group
    wide = heads_here * HEAD
    kv_wide = 2 * D // group
    rows_f = D // f_size
    half_f = rows_f // 2
    own = D // (f_size * group)
    ff = w_mlp_up.shape[1] // f_size
    own_down = w_mlp_down.shape[0] // group

    x = latents[0]
    cotangent = grad_out[0]
    text = text_embed[0]

    x_near = [x] + unique(doubling(x, "ctx"))
    x_far = [swap(part, "blk", 1) for part in x_near]
    x_parts = x_near + x_far
    x_kinds, at = [], 0
    for part in x_parts:
        n = 1 if part.ndim == 2 else part.shape[0]
        x_kinds.append(list(range(at, at + n)))
        at += n

    own_in = jnp.concatenate(
        [lax.dynamic_slice(w_attn_in, (0, i * D + g * wide), (rows_f, wide)) for i in range(3)]
        + [lax.dynamic_slice(w_cross_kv, (0, g * kv_wide), (rows_f, kv_wide)), ada_table.T],
        axis=1,
    )
    in_found = unique(doubling(own_in, "fsdp"))
    w_t, kv_t, pairs_here, table = project_text(
        ids, own_in, in_found, text, 3 * wide, kv_wide, f_size
    )
    modulation = table + timestep.reshape(6, D)
    pair_both = jnp.stack([pairs_here, swap(pairs_here, "blk", 1)], 0)
    pair_parts = [pair_both] + unique(doubling(after(pair_both, x_far[-1]), "ctx"))

    def assemble(pieces, kinds):
        if half_f % 16 == 0:
            return pieces, kinds
        count = sum(kind[0] == "own" for kind in kinds)
        whole = jnp.zeros((count, f_size, rows_f, pieces[0].shape[-1]), bfloat)
        for part, kind in zip(pieces, kinds):
            if kind[0] == "own":
                whole = lax.dynamic_update_slice(whole, part[None, None], (kind[1], f, 0, 0))
            else:
                core = b if kind[0] == "near" else 1 - b
                part = part if kind[1] is None else part[kind[1]]
                whole = lax.dynamic_update_slice(
                    whole, part[:, None], (0, f ^ kind[2](core), core * half_f, 0)
                )
        return [whole.reshape(count, D, -1)], [("whole",)]

    squares = [w_attn_out, w_cross_q, w_cross_out]
    half = jnp.stack([lax.dynamic_slice(w, (b * half_f, 0), (half_f, D)) for w in squares], 0)
    found = doubling(after(half, in_found[0]), "fsdp")
    arrays = unique(found)
    swapped = [swap(part, "blk", 1) for part in arrays]
    pieces, kinds = list(squares), [("own", i) for i in range(3)]
    for name in ("near", "far"):
        for q, (got, i) in enumerate(found):
            at = [other is got for other in arrays].index(True)
            pieces.append(got if name == "near" else swapped[at])
            kinds.append((name, i, functools.partial(step_of, q + 1, size=f_size)))
    pieces, kinds = assemble(pieces, kinds)

    near, far, qkv, norm, x_all = attend_forward(
        ids, w_t, modulation, x_parts, x_kinds, heads_here, z_size
    )

    up_half = lax.dynamic_slice(after(w_mlp_up, near), (b * half_f, 0), (half_f, f_size * ff))
    up_pieces = [lax.dynamic_slice(w_mlp_up, (0, f * ff), (rows_f, ff))]
    up_kinds = [("own", 0)]
    up_near = [
        swap(lax.dynamic_slice(up_half, (0, (f ^ step) * ff), (half_f, ff)), "fsdp", step)
        for step in range(1, f_size)
    ]
    up_far = swap(jnp.stack(up_near, 0)[:, None], "blk", 1)
    for step in range(1, f_size):
        up_pieces += [up_near[step - 1][None], up_far]
        up_kinds += [
            ("near", None, lambda core, step=step: step),
            ("far", step - 1, lambda core, step=step: step),
        ]
    up_pieces, up_kinds = assemble(up_pieces, up_kinds)

    branch_two_grad = (modulation[5:6] * cotangent.astype(single)).astype(bfloat)
    branch_two_grad = after(branch_two_grad, near)
    branch_found = [got[i] for got, i in doubling(branch_two_grad, "fsdp")]
    branch_two_all = jnp.concatenate([branch_two_grad] + branch_found, axis=0)
    grad_hidden = dot(branch_two_all, w_mlp_down, (1, 1))

    def exchange(near, far):
        far = swap(far, "blk", 1)
        got = [
            swap(jnp.stack([near[step], far[step]], 0), "ctx", step) for step in range(1, z_size)
        ]
        return far, got

    far, got = exchange(near, far)
    x_two, second, branch_one, p, cq, left, left_far, pairs = token_forward(
        ids, near, far, got, x, modulation, pair_parts, pieces, kinds, f_size, z_size
    )
    x_two_parts = [x_two] + unique(doubling(x_two, "fsdp"))
    left_far = swap(after(left_far, x_two_parts[-1]), "blk", 1)
    hidden, pre, gm_keep, gm_send = feed_forward(
        ids, x_two_parts, grad_hidden, up_pieces, up_kinds, ff, f_size
    )
    gm_own, gm_got = halving(gm_keep, gm_send, "fsdp")
    branch_terms, core_send, (dk, uk) = feed_forward_rest(
        after(ids, gm_keep), x_two_parts, hidden, pre, branch_two_all, w_mlp_down, f_size, z_size
    )
    core_got = [swap(part, "blk", 1) for part in core_send]
    d_far, u_far = (core_got[0][0], core_got[0][1]) if len(core_got) == 1 else core_got
    near, far, right, grad_first, stat_mid, pair_grads = token_backward(
        after(ids, dk),
        gm_own,
        [gm_got],
        second,
        branch_one,
        cotangent,
        modulation,
        p,
        cq,
        pairs,
        pieces,
        kinds,
        f_size,
        z_size,
    )
    far, got = exchange(near, far)
    right_far = swap(right, "blk", 1)
    d_terms = split_sum(after(ids, near), 1, dk, d_far, z_size, False)
    u_own, u_send = split_sum(after(ids, d_terms[0]), 0, uk, u_far, f_size, True)
    s_terms = square_grads(after(ids, u_own), left, left_far, right, right_far, f_size)
    close, away, turned = attend_backward(
        after(ids, s_terms[0]), qkv, norm, w_t, near, far, got, x_all, z_size
    )
    m_sum = close + swap(away, "blk", 1).astype(single)
    m_half = z_size // 2
    m_own, m_got = halving(m_sum[:m_half], m_sum[m_half:].astype(bfloat), "ctx")

    mlp_branch = half_sum(*branch_terms, "fsdp")
    block_out = (second + modulation[5:6] * mlp_branch).astype(bfloat)
    stat_gate = jnp.sum(cotangent.astype(single) * mlp_branch, axis=0, keepdims=True)

    d_own, d_got = halving(*d_terms, "ctx")
    u_got = [swap(u_send[step - 1], "fsdp", step)[None] for step in range(1, f_size)]
    s_own, s_got = halving(*s_terms, "fsdp")

    grad_pairs = lax.psum_scatter(pair_grads, ("ctx", "blk"), scatter_dimension=0, tiled=True)
    c_keep, c_send, text_part = column_grads(
        after(ids, m_sum), turned, text, grad_pairs, kv_t, f_size
    )
    grad_text = lax.psum(text_part.astype(bfloat), ("ctx", "blk"))

    u_terms = sum_split(after(ids, m_sum), 1, u_own, u_got, z_size, False)
    u_own, u_got = halving(*u_terms, "ctx")
    s_terms = sum_split(after(ids, u_terms[0]), 1, s_own, [s_got], z_size, True)
    s_own, s_got = halving(*s_terms, "ctx")

    grad_latents, stat_last = finish(m_own, [m_got], x, modulation, grad_first)

    stamp = jnp.concatenate([stat_last, stat_mid, stat_gate], axis=0)
    stamp = stamp + swap(stamp, "blk", 1)
    for stage in range(bits_of(z_size)):
        stamp = stamp + swap(stamp, "ctx", 1 << stage)
    grad_timestep = stamp.reshape(1, 6 * D)
    table_sum = stamp
    for stage in range(bits_of(f_size)):
        table_sum = table_sum + swap(table_sum, "fsdp", 1 << stage)
    grad_table = lax.dynamic_slice(table_sum, (0, (f * group + g) * own), (6, own))

    cols = 3 * wide + kv_wide
    mine = half_sum(c_keep, c_send, "fsdp").astype(bfloat)
    mine = mine.reshape(z_size, 2, own, cols)
    keep, send = reorder([mine[:, 0], mine[:, 1]], b)
    pair = jnp.stack([keep, swap(send, "blk", 1)], 1)
    pair = reorder([pair[i] for i in range(z_size)], z)
    parts = [pair[0]] + partners(pair, "ctx")
    nat = jnp.stack(reorder(parts, z), 0)
    nat = jnp.stack(reorder([nat[:, 0], nat[:, 1]], b), 1).astype(single)
    nat = nat.reshape(group, own, cols).transpose(1, 0, 2)
    grad_attn_in = nat[:, :, : 3 * wide].reshape(own, group, 3, wide).transpose(0, 2, 1, 3)
    grad_attn_in = grad_attn_in.reshape(own, 3 * D)
    grad_cross_kv = nat[:, :, 3 * wide :].reshape(own, 2 * D)

    square_sum = s_own + s_got.astype(single)
    grad_mlp_down = d_own + d_got.astype(single)
    u_sum = u_own + u_got.astype(single)
    grad_mlp_up = jnp.concatenate(reorder([u_sum[i] for i in range(f_size)], f), axis=1)

    grad_text = after(grad_text, grad_table, grad_attn_in).astype(single)

    return (
        block_out[None],
        grad_latents[None],
        grad_text[None],
        grad_timestep,
        grad_table,
        grad_attn_in,
        square_sum[0],
        square_sum[1],
        grad_cross_kv,
        square_sum[2],
        grad_mlp_up,
        grad_mlp_down,
        grad_table[3],
    )


def solution(mesh):
    placed = (
        P("fsdp", ("ctx", "blk"), None),
        P("fsdp", None, None),
        P("fsdp", None),
        P(None, "fsdp"),
        P("fsdp", None),
        P("fsdp", None),
        P("fsdp", None),
        P("fsdp", None),
        P("fsdp", None),
        P("fsdp", None),
        P("fsdp", None),
        P("fsdp", ("ctx", "blk"), None),
    )
    owned = P(("fsdp", "ctx", "blk"), None)
    return jax.shard_map(
        shards,
        mesh=mesh,
        in_specs=placed,
        out_specs=(
            P("fsdp", ("ctx", "blk"), None),
            P("fsdp", ("ctx", "blk"), None),
            P("fsdp", None, None),
            P("fsdp", None),
            P(None, ("fsdp", "ctx", "blk")),
            owned,
            owned,
            owned,
            owned,
            owned,
            owned,
            owned,
            P(("fsdp", "ctx", "blk")),
        ),
        check_vma=False,
    )
```

```python
import functools

import jax
import jax.numpy as jnp
from jax import lax
from jax.experimental import pallas as pl
from jax.experimental.pallas import tpu as pltpu
from jax.sharding import PartitionSpec as P

D = 1152
HEADS = 16
HEAD = 72
TEXT = 120

epsilon = 1e-06
bfloat = jnp.bfloat16
single = jnp.float32
scaling = HEAD ** (-0.5)

VMEM = pl.BlockSpec(memory_space=pltpu.VMEM)
SMEM = pl.BlockSpec(memory_space=pltpu.SMEM)
ANY = pl.BlockSpec(memory_space=pl.ANY)
HBM = pl.BlockSpec(memory_space=pltpu.HBM)


def layer_norm(values):
    centred = values - jnp.mean(values, axis=-1, keepdims=True)
    variance = jnp.mean(centred * centred, axis=-1, keepdims=True)
    inverse = lax.rsqrt(variance + epsilon)
    return (centred * inverse, inverse)


def norm_back(grad_normed, normed, inverse):
    first_mean = jnp.mean(grad_normed, axis=-1, keepdims=True)
    second_mean = jnp.mean(grad_normed * normed, axis=-1, keepdims=True)
    return inverse * (grad_normed - first_mean - normed * second_mean)


def dot(left, right, axes=(1, 0)):
    return lax.dot_general(
        left, right, (((axes[0],), (axes[1],)), ((), ())), preferred_element_type=single
    )


def shape(dims, dtype=bfloat):
    return jax.ShapeDtypeStruct(tuple(dims), dtype)


def call(body, outs, args, specs, scratch=(), megabytes=40, micros=2):
    return pl.pallas_call(
        body,
        out_shape=tuple(outs),
        in_specs=list(specs),
        out_specs=tuple(VMEM for _ in outs),
        scratch_shapes=list(scratch),
        compiler_params=pltpu.CompilerParams(vmem_limit_bytes=megabytes * 2**20),
        cost_estimate=pl.CostEstimate(
            flops=int(micros * 1.15e9), bytes_accessed=1, transcendentals=0
        ),
    )(*args)


def swap(values, axis, step):
    size = lax.axis_size(axis)
    return lax.ppermute(values, axis, [(i, i ^ step) for i in range(size)])


def bits_of(size):
    return size.bit_length() - 1


def back_of(place, size):
    bits = bits_of(size)
    return sum(((place >> j) & 1) << (bits - 1 - j) for j in range(bits))


def step_of(place, core, size):
    return jnp.where(core == 0, place, back_of(place, size))


def cross(values, axis, stage):
    size = lax.axis_size(axis)
    pairs = []
    for i in range(size):
        for core in range(2):
            step = 1 << stage if core == 0 else 1 << (bits_of(size) - 1 - stage)
            pairs.append((2 * i + core, 2 * (i ^ step) + core))
    return lax.ppermute(values, (axis, "blk"), pairs)


class Clock:
    def __init__(self, ids):
        self.ids = ids
        self.token = ids

    def gate(self, values):
        return after(values, self.token)

    def wait(self, *values):
        out = lax.optimization_barrier(values + (self.token,))
        self.token = out[-1]
        return out[0] if len(values) == 1 else out[:-1]

    def run(self, kernel, *args, **named):
        outs = kernel(self.gate(self.ids), *args, **named)
        self.token = after(self.token, outs[0])
        return outs

    def swap(self, values, axis, step):
        return swap(self.gate(values), axis, step)


class Doubling:
    def __init__(self, clock, values, axis):
        self.clock, self.axis = clock, axis
        self.pieces = [values]
        self.arrays = []
        self.bits = bits_of(lax.axis_size(axis))
        self.stage = 0
        self.got = None

    def start(self):
        message = self.pieces[0][None] if self.stage == 0 else jnp.stack(self.pieces, 0)
        self.got = cross(self.clock.gate(message), self.axis, self.stage)
        self.stage += 1

    def wait(self):
        got = self.clock.wait(self.got)
        self.arrays.append(got)
        self.pieces += [got[i] for i in range(len(self.pieces))]

    def finish(self):
        self.wait()
        while self.stage < self.bits:
            self.start()
            self.wait()


class Transposing:
    def __init__(self, clock, chunks, axis):
        self.clock, self.axis = clock, axis
        self.pieces = list(chunks)
        self.bits = bits_of(lax.axis_size(axis))
        self.stage = 0
        self.found = {}

    def moved(self):
        return [q for q in range(len(self.pieces)) if (q >> (self.stage - 1)) & 1]

    def start(self):
        self.stage += 1
        message = jnp.stack([self.pieces[q] for q in self.moved()], 0)
        self.got = cross(self.clock.gate(message), self.axis, self.stage - 1)

    def wait(self):
        self.got = self.clock.wait(self.got)
        for i, q in enumerate(self.moved()):
            self.pieces[q] = self.got[i]
            self.found[q] = (self.got, i)

    def finish(self):
        self.wait()
        while self.stage < self.bits:
            self.start()
            self.wait()


class Halving:
    def __init__(self, clock, keep, send, axis):
        self.clock, self.axis = clock, axis
        self.keep, self.send = keep, send
        self.stage = bits_of(lax.axis_size(axis)) - 1
        self.got = None

    def start(self):
        self.got = cross(self.clock.gate(self.send), self.axis, self.stage)
        self.stage -= 1

    def wait(self):
        got = self.clock.wait(self.got)
        if self.stage < 0:
            self.own, self.last = self.keep[0], got[0]
            return
        half = self.keep.shape[0] // 2
        self.send = (self.keep[half:] + got[half:].astype(single)).astype(bfloat)
        self.keep = self.keep[:half] + got[:half].astype(single)

    def finish(self):
        self.wait()
        while self.stage >= 0:
            self.start()
            self.wait()

    def sum(self):
        return self.own + self.last.astype(single)


class Exchange:
    def __init__(self, clock, near, far):
        self.clock, self.near = clock, near
        self.far = clock.swap(far, "blk", 1)

    def cross(self):
        self.far = self.clock.wait(self.far)
        self.got = [
            self.clock.swap(jnp.stack([self.near[step], self.far[step]], 0), "ctx", step)
            for step in range(1, self.near.shape[0])
        ]

    def finish(self):
        self.got = list(self.clock.wait(*self.got, self.near)[:-1])


def tree_sum(parts):
    while len(parts) > 1:
        parts = [parts[i] + parts[i + 1] for i in range(0, len(parts), 2)]
    return parts[0]


def reorder(parts, index):
    count = len(parts)
    bit = 1
    parts = list(parts)
    while bit < count:
        flag = (index & bit) != 0
        parts = [jnp.where(flag, parts[i ^ bit], parts[i]) for i in range(count)]
        bit *= 2
    return parts


def after(values, *earlier):
    return lax.optimization_barrier((values,) + earlier)[0]


def aligned(index, unit):
    return pl.multiple_of(index, unit)


def project_text(ids, own_part, parts, text, own_wide, kv_wide, f_size):
    rows, cols = own_part.shape
    count = f_size
    n_parts = len(parts)

    def body(*refs):
        ids_ref, text_ref = refs[0], refs[1]
        own_ref = refs[2]
        part_refs = refs[3 : 3 + n_parts]
        w_ref, kv_ref, pairs_ref, table_ref = refs[3 + n_parts : 7 + n_parts]
        full, sems = refs[7 + n_parts :]
        f, b = ids_ref[0], ids_ref[2]
        sources = [own_ref] + [ref.at[i] for ref in part_refs for i in range(ref.shape[0])]
        copies = []
        for q, source in enumerate(sources):
            place = pl.ds(aligned((f ^ step_of(q, b, count)) * rows, 16), rows)
            copies.append(pltpu.make_async_copy(source, full.at[place, :], sems.at[q]))
        for copy in copies:
            copy.start()
        for copy in copies:
            copy.wait()
        turned = full[...].T
        w_ref[...] = turned[:own_wide]
        kv = turned[own_wide : own_wide + kv_wide]
        kv_ref[...] = kv
        pairs_ref[...] = dot(kv, text_ref[...], (1, 1)).astype(bfloat)
        table_ref[...] = turned[own_wide + kv_wide :].astype(single)

    return call(
        body,
        [
            shape((own_wide, D)),
            shape((kv_wide, D)),
            shape((kv_wide, TEXT)),
            shape((cols - own_wide - kv_wide, D), single),
        ],
        [ids, text, own_part] + list(parts),
        [SMEM, VMEM] + [ANY] * (1 + n_parts),
        [pltpu.VMEM((count * rows, cols), bfloat), pltpu.SemaphoreType.DMA((count,))],
        megabytes=16,
        micros=2.6,
    )


def attend_forward(ids, w_t, modulation, x_parts, x_kinds, heads_here, z_size):
    tok = x_parts[0].shape[-2]
    count = 2 * z_size
    total = count * tok
    width = 256 if total % 256 == 0 else tok
    per = width // tok
    n_parts = len(x_parts)

    def body(*refs):
        ids_ref, w_ref, mod_ref = refs[:3]
        x_refs = refs[3 : 3 + n_parts]
        near_ref, far_ref, qkv_ref, norm_ref, x_all = refs[3 + n_parts : 8 + n_parts]
        raw, sems = refs[8 + n_parts :]
        b = ids_ref[2]
        copies = []
        for ref, chunks in zip(x_refs, x_kinds):
            for i, chunk in enumerate(chunks):
                source = ref if len(ref.shape) == 2 else ref.at[i]
                target = raw.at[pl.ds(chunk * tok, tok), :]
                copies.append(pltpu.make_async_copy(source, target, sems.at[chunk]))
        for copy in copies:
            copy.start()
        for copy in copies:
            copy.wait()

        def project(j, carry):
            place = pl.ds(aligned(j * width, width), width)
            normed, _ = layer_norm(raw[place, :].astype(single))
            modulated = (normed * (1.0 + mod_ref[1:2]) + mod_ref[0:1]).astype(bfloat)
            x_all[place, :] = modulated
            got = dot(w_ref[...], modulated, (1, 1))
            for i in range(3 * heads_here):
                qkv_ref[i, :, place] = got[i * HEAD : (i + 1) * HEAD].astype(bfloat)
            return carry

        lax.fori_loop(0, total // width, project, 0)

        for h in range(heads_here):
            keys = qkv_ref[heads_here + h]
            values = qkv_ref[2 * heads_here + h]

            for j in range(total // width):
                place = pl.ds(j * width, width)
                scores = dot(keys, qkv_ref[h, :, place], (0, 0)) * scaling
                top = jnp.max(scores, axis=0, keepdims=True)
                exponent = jnp.exp(scores - top)
                summed = jnp.sum(exponent, axis=0, keepdims=True)
                weights = (exponent * (1.0 / summed)).astype(bfloat)
                mixed = dot(values, weights).astype(bfloat)
                norm_ref[h, :, place] = top + jnp.log(summed)
                for i in range(per):
                    chunk = j * per + i
                    piece = mixed[:, i * tok : (i + 1) * tok]
                    if chunk < z_size:
                        near_ref[step_of(chunk, b, z_size), h] = piece
                    else:
                        far_ref[step_of(chunk - z_size, 1 - b, z_size), h] = piece

    wide = heads_here * HEAD
    return call(
        body,
        [
            shape((z_size, heads_here, HEAD, tok)),
            shape((z_size, heads_here, HEAD, tok)),
            shape((3 * heads_here, HEAD, total)),
            shape((heads_here, 1, total), single),
            shape((total, D)),
        ],
        [ids, w_t, modulation] + list(x_parts),
        [SMEM, VMEM, VMEM] + [ANY] * n_parts,
        [pltpu.VMEM((total, D), bfloat), pltpu.SemaphoreType.DMA((count,))],
        megabytes=24,
        micros=12,
    )


def weight_copies(piece_refs, kinds, full, sems, f, b, rows):
    copies = []
    half = rows // 2
    for i, (ref, kind) in enumerate(zip(piece_refs, kinds)):
        sem = sems.at[i]
        if kind[0] == "whole":
            copies.append(pltpu.make_async_copy(ref, full, sem))
        elif kind[0] == "own":
            place = pl.ds(aligned(f * rows, 16), rows)
            copies.append(pltpu.make_async_copy(ref, full.at[kind[1], place, :], sem))
        else:
            core = b if kind[0] == "near" else 1 - b
            source = f ^ kind[2](core)
            place = pl.ds(aligned(source * rows + core * half, 16), half)
            target = full.at[:, place, :]
            ref = ref if kind[1] is None else ref.at[kind[1]]
            copies.append(pltpu.make_async_copy(ref, target, sem))
    return copies


def piece_specs(kinds):
    return [HBM if kind[0] == "own" else ANY for kind in kinds]


def permute_rows(source, target, count, piece):
    for k in range(count):
        for core in range(2):
            target[core, pl.ds(k * piece, piece), :] = source[
                pl.ds((2 * k + core) * piece, piece), :
            ]


def token_forward(ids, near, far, got, x, modulation, pair_parts, pieces, kinds, f_size, z_size):
    tok = x.shape[0]
    heads_here = near.shape[1]
    rows = D // f_size
    own = D // (2 * f_size * z_size)
    kv_wide = D // z_size
    n_got, n_pieces, n_pairs = len(got), len(pieces), len(pair_parts)

    def body(*refs):
        ids_ref, near_ref, far_ref, x_ref, mod_ref = refs[:5]
        got_refs = refs[5 : 5 + n_got]
        pair_refs = refs[5 + n_got : 5 + n_got + n_pairs]
        at = 5 + n_got + n_pairs
        piece_refs = refs[at : at + n_pieces]
        rest = refs[at + n_pieces :]
        x_two_ref, second_ref, branch_ref, p_ref, cq_ref, keep_ref, send_ref, pairs_ref = rest[:8]
        full, mixed, pair_s, turned, left, sems = rest[8:]
        f, z, b = ids_ref[0], ids_ref[1], ids_ref[2]
        copies = weight_copies(piece_refs, kinds, full, sems, f, b, rows)
        for copy in copies:
            copy.start()

        def place(step, core, h):
            g = 2 * (z ^ step) + (b ^ core)
            return pl.ds(aligned((g * heads_here + h) * HEAD, 8), HEAD)

        for h in range(heads_here):
            mixed[place(0, 0, h), :] = near_ref[0, h].astype(single)
            mixed[place(0, 1, h), :] = far_ref[0, h].astype(single)
            for step in range(1, z_size):
                for core in range(2):
                    mixed[place(step, core, h), :] = got_refs[step - 1][core, h].astype(single)
        for core in range(2):
            q = 0
            for ref in pair_refs[core * (n_pairs // 2) : (core + 1) * (n_pairs // 2)]:
                for source in [ref] if len(ref.shape) == 2 else [ref.at[i] for i in range(ref.shape[0])]:
                    g = 2 * (z ^ step_of(q, b ^ core, z_size)) + (b ^ core)
                    place = pl.ds(aligned(g * kv_wide, 8), kv_wide)
                    pair_s[place, :] = source[...].astype(single)
                    q += 1
        pairs_ref[...] = pair_s[...]

        def keep_left(i, source):
            permute_rows(source, left, f_size * z_size, own)
            keep_ref[i] = left[b].astype(bfloat)
            send_ref[i] = left[1 - b].astype(bfloat)

        keep_left(0, mixed)
        shift_two, scale_two, gate_one = mod_ref[3:4], mod_ref[4:5], mod_ref[2:3]
        for copy in copies:
            copy.wait()
        branch = dot(mixed[...].T.astype(bfloat), full[0])
        branch_ref[...] = branch
        first = x_ref[...].astype(single) + gate_one * branch
        first_low = first.astype(bfloat)
        turned[...] = first_low.astype(single).T
        keep_left(1, turned)
        turned[...] = dot(first_low, full[1]).T
        cq_ref[...] = turned[...].astype(bfloat)
        for h in range(HEADS):
            rows_h = pl.ds(h * HEAD, HEAD)
            keys = pair_s[rows_h, :].astype(bfloat)
            values = pair_s[pl.ds(D + h * HEAD, HEAD), :].astype(bfloat)
            scores = dot(keys, turned[rows_h, :].astype(bfloat), (0, 0)) * scaling
            top = jnp.max(scores, axis=0, keepdims=True)
            exponent = jnp.exp(scores - top)
            weights = exponent * (1.0 / jnp.sum(exponent, axis=0, keepdims=True))
            p_ref[h] = weights
            mixed[rows_h, :] = dot(values, weights.astype(bfloat)).astype(bfloat).astype(single)
        second = first + dot(mixed[...].T.astype(bfloat), full[2])
        second_ref[...] = second
        normed, _ = layer_norm(second)
        x_two_ref[...] = (normed * (1.0 + scale_two) + shift_two).astype(bfloat)
        keep_left(2, mixed)

    return call(
        body,
        [
            shape((tok, D)),
            shape((tok, D), single),
            shape((tok, D), single),
            shape((HEADS, TEXT, tok), single),
            shape((D, tok)),
            shape((3, D // 2, tok)),
            shape((3, D // 2, tok)),
            shape((2 * D, TEXT), single),
        ],
        [ids, near, far, x, modulation] + list(got) + list(pair_parts) + list(pieces),
        [SMEM] + [VMEM] * (4 + n_got + n_pairs) + piece_specs(kinds),
        [
            pltpu.VMEM((3, D, D), bfloat),
            pltpu.VMEM((D, tok), single),
            pltpu.VMEM((2 * D, TEXT), single),
            pltpu.VMEM((D, tok), single),
            pltpu.VMEM((2, D // 2, tok), single),
            pltpu.SemaphoreType.DMA((n_pieces,)),
        ],
        megabytes=28,
        micros=7,
    )


def feed_forward(ids, x_parts, grad_hidden, pieces, kinds, ff, f_size):
    count = f_size
    n_parts = len(x_parts)
    tok = x_parts[0].shape[0]
    tile = 384 if ff % 384 == 0 else ff
    rows = D // f_size
    n_pieces = len(pieces)

    def body(*refs):
        ids_ref = refs[0]
        x_refs = refs[1 : 1 + n_parts]
        gh_ref = refs[1 + n_parts]
        piece_refs = refs[2 + n_parts : 2 + n_parts + n_pieces]
        rest = refs[2 + n_parts + n_pieces :]
        hidden_ref, pre_ref, keep_ref, send_ref = rest[:4]
        x_all, full, sems = rest[4:]
        up_ref = full.at[0]
        copies = weight_copies(piece_refs, kinds, full, sems, ids_ref[0], ids_ref[2], rows)
        for copy in copies:
            copy.start()
        x_all[0:tok, :] = x_refs[0][...]
        at = tok
        for ref in x_refs[1:]:
            for i in range(ref.shape[0]):
                x_all[at : at + tok, :] = ref[i]
                at += tok
        for copy in copies:
            copy.wait()

        def step(j, carry):
            place = pl.ds(aligned(j * tile, 128), tile) if ff > tile else pl.ds(0, tile)
            u = dot(x_all[...], up_ref[:, place])
            square = u * u
            t = jnp.tanh(0.7978845608028654 * u * (1.0 + 0.044715 * square))
            half = 0.5 * (1.0 + t)
            hidden_ref[:, place] = (u * half).astype(bfloat)
            slope = half + 0.5 * u * (1.0 - t * t) * (
                0.7978845608028654 * (1.0 + 0.134145 * square)
            )
            pre_ref[:, place] = (gh_ref[:, place] * slope).astype(bfloat)
            return carry

        if ff > tile:
            lax.fori_loop(0, ff // tile, step, 0)
        else:
            step(0, 0)
        part = dot(pre_ref[...], up_ref[...], (1, 1))
        for i in range(count):
            piece = part[i * tok : (i + 1) * tok]
            if i < count // 2:
                keep_ref[i] = piece
            else:
                send_ref[i - count // 2] = piece.astype(bfloat)

    total = count * tok
    return call(
        body,
        [
            shape((total, ff)),
            shape((total, ff)),
            shape((count // 2, tok, D), single),
            shape((count // 2, tok, D)),
        ],
        [ids] + list(x_parts) + [grad_hidden] + list(pieces),
        [SMEM] + [VMEM] * (n_parts + 1) + piece_specs(kinds),
        [
            pltpu.VMEM((total, D), bfloat),
            pltpu.VMEM((1, D, ff), bfloat),
            pltpu.SemaphoreType.DMA((n_pieces,)),
        ],
        megabytes=24,
        micros=7,
    )


def feed_forward_turn(ids, x_parts, hidden, f_size, z_size):
    n_parts = len(x_parts)
    tok = x_parts[0].shape[0]
    total, ff = hidden.shape
    own = D // (2 * f_size * z_size)
    own_down = ff // (2 * z_size)

    def body(*refs):
        ids_ref, hidden_ref = refs[:2]
        x_refs = refs[2 : 2 + n_parts]
        hk_ref, hs_ref, xk_ref, xs_ref, flat, halves, flat_down, halves_down = refs[2 + n_parts :]
        b = ids_ref[2]
        flat_down[...] = hidden_ref[...].T.astype(single)
        permute_rows(flat_down, halves_down, z_size, own_down)
        hk_ref[...] = halves_down[b].astype(bfloat)
        hs_ref[...] = halves_down[1 - b].astype(bfloat)
        flat[:, 0:tok] = x_refs[0][...].T.astype(single)
        at = tok
        for ref in x_refs[1:]:
            for i in range(ref.shape[0]):
                flat[:, at : at + tok] = ref[i].T.astype(single)
                at += tok
        permute_rows(flat, halves, f_size * z_size, own)
        xk_ref[...] = halves[b].astype(bfloat)
        xs_ref[...] = halves[1 - b].astype(bfloat)

    return call(
        body,
        [shape((ff // 2, total))] * 2 + [shape((D // 2, total))] * 2,
        [ids, hidden] + list(x_parts),
        [SMEM] + [VMEM] * (1 + n_parts),
        [
            pltpu.VMEM((D, total), single),
            pltpu.VMEM((2, D // 2, total), single),
            pltpu.VMEM((ff, total), single),
            pltpu.VMEM((2, ff // 2, total), single),
        ],
        megabytes=20,
        micros=0.1,
    )


def feed_forward_out(ids, hidden, down, count):
    total = hidden.shape[0]
    tok = total // count

    def body(_, hidden_ref, down_ref, keep_ref, send_ref):
        part = dot(hidden_ref[...], down_ref[...])
        for i in range(count):
            piece = part[i * tok : (i + 1) * tok]
            if i < count // 2:
                keep_ref[i] = piece
            else:
                send_ref[i - count // 2] = piece.astype(bfloat)

    return call(
        body,
        [shape((count // 2, tok, D), single), shape((count // 2, tok, D))],
        [ids, hidden, down],
        [SMEM, VMEM, VMEM],
        megabytes=12,
        micros=0.1,
    )


def chip_grads(ids, index, left, left_far, right, right_far, count, direct):
    rows, tok = left.shape
    cols = right.shape[1]
    part = rows // count
    held = 1 if direct else count // 2

    def body(*refs):
        ids_ref, left_ref, lf_ref, right_ref, rf_ref, keep_ref, send_ref = refs[:7]
        left_s, right_s, flat = refs[7:]
        i, b = ids_ref[index], ids_ref[2]
        left_s[:, 0:tok] = left_ref[...]
        left_s[:, tok : 2 * tok] = lf_ref[...]
        right_s[0:tok, :] = right_ref[...]
        right_s[tok : 2 * tok, :] = rf_ref[...]
        value = dot(left_s[...], right_s[...])
        for k in range(count):
            flat[k] = value[k * part : (k + 1) * part]
        for q in range(count):
            piece = flat[i ^ step_of(q, b, count)]
            if q < held:
                keep_ref[q] = piece
            else:
                send_ref[q - held] = piece.astype(bfloat)

    return call(
        body,
        [shape((held, part, cols), single), shape((count - held, part, cols))],
        [ids, left, left_far, right, right_far],
        [SMEM] + [VMEM] * 4,
        [
            pltpu.VMEM((rows, 2 * tok), bfloat),
            pltpu.VMEM((2 * tok, cols), bfloat),
            pltpu.VMEM((count, part, cols), single),
        ],
        megabytes=24,
        micros=0.1,
    )


def token_backward(
    ids, own, got, second, branch, cotangent, modulation, p, cq, pairs, pieces, kinds, f_size, z_size
):
    tok = second.shape[0]
    heads_here = HEADS // (2 * z_size)
    rows = D // f_size
    kv_wide = D // z_size
    n_got, n_pieces = len(got), len(pieces)

    def body(*refs):
        ids_ref, own_ref, second_ref, branch_ref, cot_ref, mod_ref, p_ref, cq_ref, pairs_ref = refs[:9]
        got_refs = refs[9 : 9 + n_got]
        piece_refs = refs[9 + n_got : 9 + n_got + n_pieces]
        rest = refs[9 + n_got + n_pieces :]
        near_ref, far_ref, right_ref, first_ref, stat_ref, pair_keep, pair_send = rest[:7]
        full, turned, grads, low, sems = rest[7:]
        pair_s = pairs_ref
        f, z, b = ids_ref[0], ids_ref[1], ids_ref[2]
        copies = weight_copies(piece_refs, kinds, full, sems, f, b, rows)
        for copy in copies:
            copy.start()
        gate_one, scale_two = mod_ref[2:3], mod_ref[4:5]
        grad_mod = own_ref[...]
        for ref in got_refs:
            grad_mod = grad_mod + ref[...].astype(single)
        normed, inverse = layer_norm(second_ref[...])
        stat_ref[1:2] = jnp.sum(grad_mod, axis=0, keepdims=True)
        stat_ref[2:3] = jnp.sum(grad_mod * normed, axis=0, keepdims=True)
        grad_second = cot_ref[...].astype(single) + norm_back(
            grad_mod * (1.0 + scale_two), normed, inverse
        )
        grad_low = grad_second.astype(bfloat)
        right_ref[2] = grad_low
        for copy in copies:
            copy.wait()
        turned[...] = dot(full[2], grad_low, (1, 1))
        low[...] = cq_ref[...].astype(single)
        for h in range(HEADS):
            rows_h = pl.ds(h * HEAD, HEAD)
            keys = pair_s[rows_h, :].astype(bfloat)
            values = pair_s[pl.ds(D + h * HEAD, HEAD), :].astype(bfloat)
            grad_h = turned[rows_h, :].astype(bfloat)
            weights = p_ref[h]
            grad_weights = dot(values, grad_h, (0, 0))
            grads[pl.ds(D + h * HEAD, HEAD), :] = dot(grad_h, weights.astype(bfloat), (1, 1))
            inner = jnp.sum(weights * grad_weights, axis=0, keepdims=True)
            grad_scores = (weights * (grad_weights - inner)).astype(bfloat)
            turned[rows_h, :] = scaling * dot(keys, grad_scores)
            grads[rows_h, :] = scaling * dot(low[rows_h, :].astype(bfloat), grad_scores, (1, 1))
        for q in range(z_size):
            here = 2 * (z ^ step_of(q, b, z_size)) + b
            there = 2 * (z ^ step_of(q, 1 - b, z_size)) + 1 - b
            pair_keep[q] = grads[pl.ds(aligned(here * kv_wide, 8), kv_wide), :]
            place = pl.ds(aligned(there * kv_wide, 8), kv_wide)
            pair_send[q] = grads[place, :].astype(bfloat)
        grad_query = turned[...].T.astype(bfloat)
        right_ref[1] = grad_query
        grad_first = grad_second + dot(grad_query, full[1], (1, 1))
        first_ref[...] = grad_first
        stat_ref[0:1] = jnp.sum(grad_first * branch_ref[...], axis=0, keepdims=True)
        grad_branch = (gate_one * grad_first).astype(bfloat)
        right_ref[0] = grad_branch
        turned[...] = dot(full[0], grad_branch, (1, 1))
        for step in range(z_size):
            for core in range(2):
                target = near_ref if core == 0 else far_ref
                g = 2 * (z ^ step) + (b ^ core)
                for h in range(heads_here):
                    place = pl.ds(aligned((g * heads_here + h) * HEAD, 8), HEAD)
                    target[step, h] = turned[place, :].astype(bfloat)

    return call(
        body,
        [
            shape((z_size, heads_here, HEAD, tok)),
            shape((z_size, heads_here, HEAD, tok)),
            shape((3, tok, D)),
            shape((tok, D), single),
            shape((3, D), single),
            shape((z_size, kv_wide, TEXT), single),
            shape((z_size, kv_wide, TEXT)),
        ],
        [ids, own, second, branch, cotangent, modulation, p, cq, pairs] + list(got) + list(pieces),
        [SMEM] + [VMEM] * (8 + n_got) + piece_specs(kinds),
        [
            pltpu.VMEM((3, D, D), bfloat),
            pltpu.VMEM((D, tok), single),
            pltpu.VMEM((2 * D, TEXT), single),
            pltpu.VMEM((D, tok), single),
            pltpu.SemaphoreType.DMA((n_pieces,)),
        ],
        megabytes=28,
        micros=0.1,
    )


def square_grads(ids, left, left_far, right, right_far, f_size):
    count, half, tok = left.shape
    part = half // f_size

    def body(*refs):
        ids_ref, left_ref, lf_ref, right_ref, rf_ref, keep_ref, send_ref = refs[:7]
        left_s, right_s, flat = refs[7:]
        f, b = ids_ref[0], ids_ref[2]
        for i in range(count):
            left_s[:, 0:tok] = left_ref[i]
            left_s[:, tok : 2 * tok] = lf_ref[i]
            right_s[0:tok, :] = right_ref[i]
            right_s[tok : 2 * tok, :] = rf_ref[i]
            value = dot(left_s[...], right_s[...])
            for k in range(f_size):
                flat[k] = value[k * part : (k + 1) * part]
            for q in range(f_size):
                value = flat[f ^ step_of(q, b, f_size)]
                if q < f_size // 2:
                    keep_ref[q, i] = value
                else:
                    send_ref[q - f_size // 2, i] = value.astype(bfloat)

    return call(
        body,
        [
            shape((f_size // 2, count, part, D), single),
            shape((f_size // 2, count, part, D)),
        ],
        [ids, left, left_far, right, right_far],
        [SMEM] + [VMEM] * 4,
        [
            pltpu.VMEM((half, 2 * tok), bfloat),
            pltpu.VMEM((2 * tok, D), bfloat),
            pltpu.VMEM((f_size, part, D), single),
        ],
        megabytes=20,
        micros=0.1,
    )


def sum_split(ids, index, own, got, count, add):
    lead, rows, cols = own.shape
    part = rows // count
    n_got = len(got)
    groups = lead if add else lead * (1 + n_got)

    def body(*refs):
        ids_ref, own_ref = refs[:2]
        got_refs = refs[2 : 2 + n_got]
        keep_ref, send_ref, flat, chunks = refs[2 + n_got :]
        i, b = ids_ref[index], ids_ref[2]

        for k in range(lead):
            if add:
                value = own_ref[k]
                for ref in got_refs:
                    value = value + ref[k].astype(single)
                flat[k] = value
            else:
                flat[k] = own_ref[k]
                for j, ref in enumerate(got_refs):
                    flat[(j + 1) * lead + k] = ref[k].astype(single)
        for k in range(groups):
            for c in range(count):
                chunks[c, pl.ds(k * part, part), :] = flat[k, pl.ds(c * part, part), :]
        for q in range(count):
            value = chunks[i ^ step_of(q, b, count)]
            if q < count // 2:
                keep_ref[q] = value
            else:
                send_ref[q - count // 2] = value.astype(bfloat)

    return call(
        body,
        [
            shape((count // 2, groups * part, cols), single),
            shape((count // 2, groups * part, cols)),
        ],
        [ids, own] + list(got),
        [SMEM] + [VMEM] * (1 + n_got),
        [
            pltpu.VMEM((groups, rows, cols), single),
            pltpu.VMEM((count, groups * part, cols), single),
        ],
        megabytes=24,
        micros=0.1,
    )


def attend_backward(ids, h, qkv, norm, near, far, got, z_size):
    heads_here, _, tok = near.shape[1:]
    count = 2 * z_size
    total = count * tok
    width = 256 if total % 256 == 0 else tok
    n_got = len(got)

    def body(*refs):
        ids_ref, qkv_ref, norm_ref, near_ref, far_ref = refs[:5]
        got_refs = refs[5 : 5 + n_got]
        out_ref, by_step, grad, flat_k, flat_v = refs[5 + n_got :]
        b = ids_ref[2]
        by_step[0, 0] = near_ref[0, h]
        by_step[1, 0] = far_ref[0, h]
        for step in range(1, z_size):
            for core in range(2):
                by_step[core, step] = got_refs[step - 1][core, h]
        for core in range(2):
            for q in range(z_size):
                at = (core * z_size + q) * tok
                grad[:, at : at + tok] = by_step[core, step_of(q, b ^ core, z_size)]
        flat_k[...] = jnp.zeros_like(flat_k)
        flat_v[...] = jnp.zeros_like(flat_v)
        keys = qkv_ref[heads_here + h]
        values = qkv_ref[2 * heads_here + h]

        def block(j, carry):
            place = pl.ds(aligned(j * width, width), width)
            query = qkv_ref[h, :, place]
            grad_h = grad[:, place]
            scores = dot(keys, query, (0, 0)) * scaling
            weights = jnp.exp(scores - norm_ref[h, :, place])
            grad_weights = dot(values, grad_h, (0, 0))
            inner = jnp.sum(weights * grad_weights, axis=0, keepdims=True)
            grad_scores = (weights * (grad_weights - inner)).astype(bfloat)
            flat_v[...] += dot(grad_h, weights.astype(bfloat), (1, 1))
            out_ref[0, :, place] = (scaling * dot(keys, grad_scores)).astype(bfloat)
            flat_k[...] += scaling * dot(query, grad_scores, (1, 1))
            return carry

        lax.fori_loop(0, total // width, block, 0)
        out_ref[1] = flat_k[...].astype(bfloat)
        out_ref[2] = flat_v[...].astype(bfloat)

    return call(
        body,
        [shape((3, HEAD, total))],
        [ids, qkv, norm, near, far] + list(got),
        [SMEM] + [VMEM] * (4 + n_got),
        [
            pltpu.VMEM((2, z_size, HEAD, tok), bfloat),
            pltpu.VMEM((HEAD, total), bfloat),
            pltpu.VMEM((HEAD, total), single),
            pltpu.VMEM((HEAD, total), single),
        ],
        megabytes=20,
        micros=0.1,
    )


def attend_project(ids, grads, w_t, x_all, z_size):
    heads_here = len(grads)
    total = x_all.shape[0]
    count = 2 * z_size
    tok = total // count
    wide3 = 3 * heads_here * HEAD

    def body(*refs):
        w_ref, x_ref = refs[1:3]
        grad_refs = refs[3 : 3 + heads_here]
        close_ref, away_ref, turned_ref, flat, low = refs[3 + heads_here :]
        for h in range(heads_here):
            for i in range(3):
                place = pl.ds((i * heads_here + h) * HEAD, HEAD)
                flat[place, :] = grad_refs[h][i].astype(single)
        low[...] = flat[...].astype(bfloat)

        def tokens(j, carry):
            place = pl.ds(aligned(j * tok, tok), tok)
            part = dot(low[:, place], w_ref[...], (0, 0))

            @pl.when(j < z_size)
            def _():
                close_ref[j] = part

            @pl.when(j >= z_size)
            def _():
                away_ref[j - z_size] = part.astype(bfloat)

            return carry

        lax.fori_loop(0, count, tokens, 0)
        turned_ref[...] = dot(low[...], x_ref[...]).T

    return call(
        body,
        [
            shape((z_size, tok, D), single),
            shape((z_size, tok, D)),
            shape((D, wide3), single),
        ],
        [ids, w_t, x_all] + list(grads),
        [SMEM] + [VMEM] * (2 + heads_here),
        [pltpu.VMEM((wide3, total), single), pltpu.VMEM((wide3, total), bfloat)],
        megabytes=20,
        micros=0.1,
    )


def text_grads(ids, own, got, kv_t):
    def body(ids_ref, own_ref, got_ref, kv_ref, pairs_ref, keep_ref, send_ref, flat):
        b = ids_ref[2]
        pairs = (own_ref[...] + got_ref[...].astype(single)).astype(bfloat)
        pairs_ref[...] = pairs
        part = dot(kv_ref[...], pairs, (0, 0))
        flat[0] = part[: D // 2]
        flat[1] = part[D // 2 :]
        keep_ref[...] = flat[b]
        send_ref[...] = flat[1 - b]

    return call(
        body,
        [
            shape(own.shape),
            shape((D // 2, TEXT), single),
            shape((D // 2, TEXT), single),
        ],
        [ids, own, got, kv_t],
        [SMEM] + [VMEM] * 3,
        [pltpu.VMEM((2, D // 2, TEXT), single)],
        megabytes=16,
        micros=0.1,
    )


def split_columns(ids, own, got, z_size):
    rows, cols = own.shape
    part = rows // z_size

    def body(ids_ref, own_ref, got_ref, out_ref, chunks):
        z = ids_ref[1]
        value = own_ref[...] + got_ref[...].astype(single)
        for k in range(z_size):
            chunks[k] = value[k * part : (k + 1) * part]
        for step in range(z_size):
            out_ref[step] = chunks[z ^ step].astype(bfloat)

    return call(
        body,
        [shape((z_size, part, cols))],
        [ids, own, got],
        [SMEM] + [VMEM] * 2,
        [pltpu.VMEM((z_size, part, cols), single)],
        megabytes=16,
        micros=0.1,
    )


def place_columns(ids, near, far, wide, z_size):
    part, cols = near[0].shape[0] // 2, near[0].shape[1]
    kv_wide = cols - 3 * wide

    def body(*refs):
        ids_ref = refs[0]
        in_ref, kv_ref, blocks, pair = refs[1 + 2 * z_size :]
        z, b = ids_ref[1], ids_ref[2]
        for core in range(2):
            for step in range(z_size):
                both = refs[1 + core * z_size + step][...].astype(single)
                pair[0] = both[:part]
                pair[1] = both[part:]
                blocks[z ^ step, b ^ core] = pair[b]
        for k in range(z_size):
            for core in range(2):
                g = 2 * k + core
                block = blocks[k, core]
                for i in range(3):
                    at = i * D + g * wide
                    in_ref[:, at : at + wide] = block[:, i * wide : (i + 1) * wide]
                kv_ref[:, g * kv_wide : (g + 1) * kv_wide] = block[:, 3 * wide :]

    return call(
        body,
        [shape((part, 3 * D), single), shape((part, 2 * D), single)],
        [ids] + list(near) + list(far),
        [SMEM] + [VMEM] * (2 * z_size),
        [pltpu.VMEM((z_size, 2, part, cols), single), pltpu.VMEM((2, part, cols), single)],
        megabytes=16,
        micros=0.1,
    )


def column_grads(ids, turned, text, grad_pairs, f_size):
    wide3 = turned.shape[1]
    kv_wide = grad_pairs.shape[0]
    rows = D // f_size
    cols = wide3 + kv_wide

    def body(*refs):
        ids_ref, turned_ref, text_ref, pairs_ref, keep_ref, send_ref, kv_s = refs
        f, b = ids_ref[0], ids_ref[2]
        pairs = pairs_ref[...]
        kv_s[...] = dot(text_ref[...], pairs, (0, 1))
        held = f_size // 2
        for q in range(f_size):
            place = pl.ds(aligned((f ^ step_of(q, b, f_size)) * rows, 8), rows)
            if q < held:
                keep_ref[q, :, 0:wide3] = turned_ref[place, :]
                keep_ref[q, :, wide3:cols] = kv_s[place, :]
            else:
                send_ref[q - held, :, 0:wide3] = turned_ref[place, :].astype(bfloat)
                send_ref[q - held, :, wide3:cols] = kv_s[place, :].astype(bfloat)

    return call(
        body,
        [
            shape((f_size // 2, rows, cols), single),
            shape((f_size // 2, rows, cols)),
        ],
        [ids, turned, text, grad_pairs],
        [SMEM] + [VMEM] * 3,
        [pltpu.VMEM((D, kv_wide), single)],
        megabytes=20,
        micros=0.1,
    )


def finish(ids, own, got, x, modulation, grad_first):
    tok = x.shape[0]
    n_got = len(got)

    def body(*refs):
        _, own_ref, x_ref, mod_ref, first_ref = refs[:5]
        got_refs = refs[5 : 5 + n_got]
        out_ref, stat_ref = refs[5 + n_got :]
        grad_mod = own_ref[...]
        for ref in got_refs:
            grad_mod = grad_mod + ref[...].astype(single)
        normed, inverse = layer_norm(x_ref[...].astype(single))
        stat_ref[0:1] = jnp.sum(grad_mod, axis=0, keepdims=True)
        stat_ref[1:2] = jnp.sum(grad_mod * normed, axis=0, keepdims=True)
        out_ref[...] = first_ref[...] + norm_back(grad_mod * (1.0 + mod_ref[1:2]), normed, inverse)

    return call(
        body,
        [shape((tok, D), single), shape((2, D), single)],
        [ids, own, x, modulation, grad_first] + list(got),
        [SMEM] + [VMEM] * (4 + n_got),
        micros=0.1,
    )


def shards(
    latents,
    text_embed,
    timestep,
    ada_table,
    w_attn_in,
    w_attn_out,
    w_cross_q,
    w_cross_kv,
    w_cross_out,
    w_mlp_up,
    w_mlp_down,
    grad_out,
):
    f_size = lax.axis_size("fsdp")
    z_size = lax.axis_size("ctx")
    group = 2 * z_size
    f = lax.axis_index("fsdp")
    z = lax.axis_index("ctx")
    b = lax.axis_index("blk")
    g = 2 * z + b
    ids = jnp.stack([f, z, b]).astype(jnp.int32)
    tok = latents.shape[1]
    heads_here = HEADS // group
    wide = heads_here * HEAD
    kv_wide = 2 * D // group
    rows_f = D // f_size
    half_f = rows_f // 2
    own = D // (f_size * group)
    ff = w_mlp_up.shape[1] // f_size
    own_down = w_mlp_down.shape[0] // group

    x = latents[0]
    cotangent = grad_out[0]
    text = text_embed[0]

    clock = Clock(ids)

    x_z = Doubling(clock, x, "ctx")
    x_z.start()

    own_in = jnp.concatenate(
        [lax.dynamic_slice(w_attn_in, (0, i * D + g * wide), (rows_f, wide)) for i in range(3)]
        + [lax.dynamic_slice(w_cross_kv, (0, g * kv_wide), (rows_f, kv_wide)), ada_table.T],
        axis=1,
    )
    in_f = Doubling(clock, own_in, "fsdp")
    in_f.start()

    squares = [w_attn_out, w_cross_q, w_cross_out]
    half = jnp.stack([lax.dynamic_slice(w, (b * half_f, 0), (half_f, D)) for w in squares], 0)
    w_f = Doubling(clock, half, "fsdp")
    w_f.start()

    up_half = lax.dynamic_slice(w_mlp_up, (b * half_f, 0), (half_f, f_size * ff))
    up_own = lax.dynamic_slice(w_mlp_up, (0, f * ff), (rows_f, ff))
    up_parts = [None] + [
        lax.dynamic_slice(up_half, (0, (f ^ step_of(q, b, f_size)) * ff), (half_f, ff))
        for q in range(1, f_size)
    ]
    up_f = Transposing(clock, up_parts, "fsdp")

    x_z.wait()
    x_z.start()
    x_far = [clock.swap(part, "blk", 1) for part in (x, x_z.arrays[0])]
    in_f.wait()
    in_f.start()
    w_f.wait()
    w_f.start()
    up_f.start()
    w_far = [clock.swap(part, "blk", 1) for part in w_f.arrays]
    x_z.finish()
    x_far += [clock.swap(part, "blk", 1) for part in x_z.arrays[1:]]
    in_f.finish()
    w_t, kv_t, pairs_here, table = clock.run(
        project_text, own_in, in_f.arrays, text, 3 * wide, kv_wide, f_size
    )
    modulation = table + timestep.reshape(6, D)
    pair_z = Doubling(clock, pairs_here, "ctx")
    pair_z.start()
    pair_far = [clock.swap(pairs_here, "blk", 1)]

    branch_two_grad = (modulation[5:6] * cotangent.astype(single)).astype(bfloat)
    grad_f = Doubling(clock, branch_two_grad, "fsdp")
    grad_f.start()
    x_far = list(clock.wait(*x_far))
    pair_z.wait()
    pair_z.start()
    pair_far.append(clock.swap(pair_z.arrays[0], "blk", 1))
    pair_far = list(clock.wait(*pair_far))

    x_parts = [x] + x_z.arrays + x_far
    x_kinds, at = [], 0
    for part in x_parts:
        n = 1 if part.ndim == 2 else part.shape[0]
        x_kinds.append(list(range(at, at + n)))
        at += n
    near, far, qkv, norm, x_all = clock.run(
        attend_forward, w_t, modulation, x_parts, x_kinds, heads_here, z_size
    )
    to_owner = Exchange(clock, near, far)
    pair_z.finish()
    pair_far += [clock.swap(part, "blk", 1) for part in pair_z.arrays[1:]]
    grad_f.wait()
    to_owner.cross()
    while w_f.stage < w_f.bits:
        w_f.wait()
        w_far.append(clock.swap(w_f.arrays[-1], "blk", 1))
        w_f.start()
    w_f.wait()
    w_far.append(clock.swap(w_f.arrays[-1], "blk", 1))
    up_f.wait()
    up_f.start()
    to_owner.finish()
    grad_f.start()
    pair_far = list(clock.wait(*pair_far))
    w_far = list(clock.wait(*w_far, near)[:-1])

    def assemble(pieces, kinds):
        if half_f % 16 == 0:
            return pieces, kinds
        count = sum(kind[0] == "own" for kind in kinds)
        whole = jnp.zeros((count, f_size, rows_f, pieces[0].shape[-1]), bfloat)
        for part, kind in zip(pieces, kinds):
            if kind[0] == "own":
                whole = lax.dynamic_update_slice(whole, part[None, None], (kind[1], f, 0, 0))
            else:
                core = b if kind[0] == "near" else 1 - b
                part = part if kind[1] is None else part[kind[1]]
                whole = lax.dynamic_update_slice(
                    whole, part[:, None], (0, f ^ kind[2](core), core * half_f, 0)
                )
        return [whole.reshape(count, D, -1)], [("whole",)]

    pieces, kinds = list(squares), [("own", i) for i in range(3)]
    for name, arrays in (("near", w_f.arrays), ("far", w_far)):
        place = 1
        for part in arrays:
            for i in range(part.shape[0]):
                pieces.append(part)
                kinds.append((name, i, functools.partial(step_of, place, size=f_size)))
                place += 1
    pieces, kinds = assemble(pieces, kinds)

    x_two, second, branch_one, p, cq, left, left_far, pairs = clock.run(
        token_forward,
        to_owner.near,
        to_owner.far,
        to_owner.got,
        x,
        modulation,
        [pairs_here] + pair_z.arrays + pair_far,
        pieces,
        kinds,
        f_size,
        z_size,
    )
    x_two_f = Doubling(clock, x_two, "fsdp")
    x_two_f.start()
    left_far = clock.swap(left_far, "blk", 1)
    grad_f.finish()
    branch_two_all = jnp.concatenate(grad_f.pieces, 0)
    branch_two_far = clock.swap(branch_two_all, "blk", 1)
    x_two_f.wait()
    x_two_f.start()
    up_f.finish()
    up_far = {
        q: clock.swap(up_f.pieces[q][None], "blk", 1) for q in range(1, f_size)
    }
    grad_hidden = dot(branch_two_all, w_mlp_down, (1, 1))
    got = clock.wait(*[up_far[q] for q in range(1, f_size)], left_far, grad_hidden)
    left_far, grad_hidden = got[-2:]
    x_two_f.finish()
    up_pieces, up_kinds = [up_own], [("own", 0)]
    for q in range(1, f_size):
        place = functools.partial(step_of, q, size=f_size)
        up_pieces += [up_f.found[q][0][up_f.found[q][1]][None], got[q - 1]]
        up_kinds += [("near", None, place), ("far", None, place)]
    up_pieces, up_kinds = assemble(up_pieces, up_kinds)
    x_two_parts = [x_two] + x_two_f.arrays

    hidden, pre, gm_keep, gm_send = clock.run(
        feed_forward, x_two_parts, grad_hidden, up_pieces, up_kinds, ff, f_size
    )
    gm = Halving(clock, gm_keep, gm_send, "fsdp")
    gm.start()
    pre_far = clock.swap(pre, "blk", 1)
    hk, hs, xk, xs = clock.run(feed_forward_turn, x_two_parts, hidden, f_size, z_size)
    hs = clock.swap(hs, "blk", 1)
    xs = clock.swap(xs, "blk", 1)
    hs, branch_two_far = clock.wait(hs, branch_two_far)
    d = Halving(
        clock,
        *clock.run(chip_grads, 1, hk, hs, branch_two_all, branch_two_far, z_size, False),
        "ctx",
    )
    d.start()
    gm.wait()
    while gm.stage >= 0:
        gm.start()
        if gm.stage >= 0:
            gm.wait()
    xs, pre_far = clock.wait(xs, pre_far)
    u_own, u_send = clock.run(chip_grads, 0, xk, xs, pre, pre_far, f_size, True)
    u_f = Transposing(clock, [None] + [u_send[q - 1] for q in range(1, f_size)], "fsdp")
    u_f.start()
    branch = Halving(clock, *clock.run(feed_forward_out, hidden, w_mlp_down, f_size), "fsdp")
    gm.wait()
    near, far, right, grad_first, stat_mid, pair_keep, pair_send = clock.run(
        token_backward,
        gm.own,
        [gm.last],
        second,
        branch_one,
        cotangent,
        modulation,
        p,
        cq,
        pairs,
        pieces,
        kinds,
        f_size,
        z_size,
    )
    u_f.wait()
    u_f.start()
    branch.start()
    d.wait()
    to_heads = Exchange(clock, near, far)
    right_far = clock.swap(right, "blk", 1)
    to_heads.cross()
    right_far = clock.wait(right_far)
    s = Halving(
        clock, *clock.run(square_grads, left, left_far, right, right_far, f_size), "fsdp"
    )
    pair_far = clock.swap(pair_send, "blk", 1)
    u_f.finish()
    u_got = [u_f.pieces[q][None] for q in range(1, f_size)]
    u = Halving(clock, *clock.run(sum_split, 1, u_own, u_got, z_size, False), "ctx")
    branch.wait()
    branch.start()
    to_heads.finish()
    s.start()
    d.start()
    pair_far = clock.wait(pair_far)
    pair_sum = pair_keep + pair_far.astype(single)
    m_half = z_size // 2
    pair = Halving(clock, pair_sum[:m_half], pair_sum[m_half:].astype(bfloat), "ctx")
    pair.start()
    u.start()
    grads = []
    for h in range(heads_here):
        grads += clock.run(
            attend_backward, h, qkv, norm, to_heads.near, to_heads.far, to_heads.got, z_size
        )
        if h == 0:
            pair.wait()
            pair.start()
            d.finish()
    pair.finish()
    grad_pairs, text_keep, text_send = clock.run(text_grads, pair.own, pair.last, kv_t)
    text_far = clock.swap(text_send, "blk", 1)
    branch.finish()
    mlp_branch = branch.sum()
    block_out = (second + modulation[5:6] * mlp_branch).astype(bfloat)
    stat_gate = jnp.sum(cotangent.astype(single) * mlp_branch, axis=0, keepdims=True)
    grad_mlp_down = d.sum()
    close, away, turned = clock.run(attend_project, grads, w_t, x_all, z_size)
    away = clock.swap(away, "blk", 1)
    u.wait()
    u.start()
    grad_text = (text_keep + clock.wait(text_far)).astype(bfloat)
    away = clock.wait(away)
    m_sum = close + away.astype(single)
    m = Halving(clock, m_sum[:m_half], m_sum[m_half:].astype(bfloat), "ctx")
    m.start()
    text_far = cross(clock.gate(grad_text), "ctx", 0)
    s.wait()
    s.start()
    c = Halving(clock, *clock.run(column_grads, turned, text_embed[0], grad_pairs, f_size), "fsdp")
    c.start()
    u.finish()
    u_sum = u.sum()
    grad_text = grad_text.astype(single) + clock.wait(text_far).astype(single)
    m.wait()
    m.start()
    c.wait()
    c.start()
    s.finish()
    s = Halving(clock, *clock.run(sum_split, 1, s.own, [s.last], z_size, True), "ctx")
    s.start()
    for stage in range(1, bits_of(z_size)):
        grad_text = grad_text.astype(bfloat)
        text_far = cross(clock.gate(grad_text), "ctx", stage)
        if stage == 1:
            c.finish()
            (c_rows,) = clock.run(split_columns, c.own, c.last, z_size)
            m.finish()
        grad_text = grad_text.astype(single) + clock.wait(text_far).astype(single)
    grad_latents, stat_last = clock.run(finish, m.own, [m.last], x, modulation, grad_first)
    stamp = jnp.concatenate([stat_last, stat_mid, stat_gate], axis=0)
    stamp_far = clock.swap(stamp, "blk", 1)
    text_far = clock.swap(grad_text, "blk", 1)
    stamp = stamp + clock.wait(stamp_far)
    for stage in range(bits_of(z_size)):
        got = clock.swap(stamp, "ctx", 1 << stage)
        if stage == 0:
            c_near = [c_rows[0]]
            c_near += [clock.swap(c_rows[step], "ctx", step) for step in range(1, z_size)]
            text_far = clock.wait(text_far)
        if stage == 1:
            s.wait()
            s.start()
        stamp = stamp + clock.wait(got)
    grad_text = jnp.concatenate(reorder([grad_text, text_far], b), axis=0).T
    grad_timestep = stamp.reshape(1, 6 * D)
    c_near = list(clock.wait(*c_near))
    c_far = [clock.swap(part, "blk", 1) for part in c_near]
    table_sum = stamp
    for stage in range(bits_of(f_size)):
        got = clock.swap(table_sum, "fsdp", 1 << stage)
        if stage == 0:
            c_far = list(clock.wait(*c_far))
            grad_attn_in, grad_cross_kv = clock.run(place_columns, c_near, c_far, wide, z_size)
        table_sum = table_sum + clock.wait(got)
    grad_mlp_up = u_sum.reshape(f_size, own, ff)
    steps = [grad_mlp_up[q] for q in range(f_size)]
    back = [steps[back_of(q, f_size)] for q in range(f_size)]
    steps = [jnp.where(b == 0, steps[q], back[q]) for q in range(f_size)]
    grad_mlp_up = jnp.concatenate(reorder(steps, f), axis=1)
    s.finish()
    square_sum = s.sum().reshape(3, own, D)
    grad_table = lax.dynamic_slice(table_sum, (0, (f * group + g) * own), (6, own))

    return (
        block_out[None],
        grad_latents[None],
        grad_text[None],
        grad_timestep,
        grad_table,
        grad_attn_in,
        square_sum[0],
        square_sum[1],
        grad_cross_kv,
        square_sum[2],
        grad_mlp_up,
        grad_mlp_down,
        grad_table[3],
    )


def solution(mesh):
    placed = (
        P("fsdp", ("ctx", "blk"), None),
        P("fsdp", None, None),
        P("fsdp", None),
        P(None, "fsdp"),
        P("fsdp", None),
        P("fsdp", None),
        P("fsdp", None),
        P("fsdp", None),
        P("fsdp", None),
        P("fsdp", None),
        P("fsdp", None),
        P("fsdp", ("ctx", "blk"), None),
    )
    owned = P(("fsdp", "ctx", "blk"), None)
    return jax.shard_map(
        shards,
        mesh=mesh,
        in_specs=placed,
        out_specs=(
            P("fsdp", ("ctx", "blk"), None),
            P("fsdp", ("ctx", "blk"), None),
            P("fsdp", None, None),
            P("fsdp", None),
            P(None, ("fsdp", "ctx", "blk")),
            owned,
            owned,
            owned,
            owned,
            owned,
            owned,
            owned,
            P(("fsdp", "ctx", "blk")),
        ),
        check_vma=False,
    )
```

```python
import functools

import jax
import jax.numpy as jnp
from jax import lax
from jax.experimental import pallas as pl
from jax.experimental.pallas import tpu as pltpu
from jax.sharding import PartitionSpec as P

D = 1152
HEADS = 16
HEAD = 72
TEXT = 120

epsilon = 1e-06
bfloat = jnp.bfloat16
single = jnp.float32
scaling = HEAD ** (-0.5)

VMEM = pl.BlockSpec(memory_space=pltpu.VMEM)
SMEM = pl.BlockSpec(memory_space=pltpu.SMEM)
ANY = pl.BlockSpec(memory_space=pl.ANY)
HBM = pl.BlockSpec(memory_space=pltpu.HBM)


def layer_norm(values):
    centred = values - jnp.mean(values, axis=-1, keepdims=True)
    variance = jnp.mean(centred * centred, axis=-1, keepdims=True)
    inverse = lax.rsqrt(variance + epsilon)
    return (centred * inverse, inverse)


def norm_back(grad_normed, normed, inverse):
    first_mean = jnp.mean(grad_normed, axis=-1, keepdims=True)
    second_mean = jnp.mean(grad_normed * normed, axis=-1, keepdims=True)
    return inverse * (grad_normed - first_mean - normed * second_mean)


def dot(left, right, axes=(1, 0)):
    return lax.dot_general(
        left, right, (((axes[0],), (axes[1],)), ((), ())), preferred_element_type=single
    )


def shape(dims, dtype=bfloat):
    return jax.ShapeDtypeStruct(tuple(dims), dtype)


def call(body, outs, args, specs, scratch=(), megabytes=40, micros=2):
    return pl.pallas_call(
        body,
        out_shape=tuple(outs),
        in_specs=list(specs),
        out_specs=tuple(VMEM for _ in outs),
        scratch_shapes=list(scratch),
        compiler_params=pltpu.CompilerParams(vmem_limit_bytes=megabytes * 2**20),
        cost_estimate=pl.CostEstimate(
            flops=int(micros * 1.15e9), bytes_accessed=1, transcendentals=0
        ),
    )(*args)


def swap(values, axis, step):
    size = lax.axis_size(axis)
    return lax.ppermute(values, axis, [(i, i ^ step) for i in range(size)])


def bits_of(size):
    return size.bit_length() - 1


def back_of(place, size):
    bits = bits_of(size)
    return sum(((place >> j) & 1) << (bits - 1 - j) for j in range(bits))


def step_of(place, core, size):
    return jnp.where(core == 0, place, back_of(place, size))


def cross(values, axis, stage):
    size = lax.axis_size(axis)
    pairs = []
    for i in range(size):
        for core in range(2):
            step = 1 << stage if core == 0 else 1 << (bits_of(size) - 1 - stage)
            pairs.append((2 * i + core, 2 * (i ^ step) + core))
    return lax.ppermute(values, (axis, "blk"), pairs)


class Clock:
    def __init__(self, ids):
        self.ids = ids
        self.token = ids

    def gate(self, values):
        return after(values, self.token)

    def wait(self, *values):
        out = lax.optimization_barrier(values + (self.token,))
        self.token = out[-1]
        return out[0] if len(values) == 1 else out[:-1]

    def run(self, kernel, *args, **named):
        outs = kernel(self.gate(self.ids), *args, **named)
        self.token = after(self.token, outs[0])
        return outs

    def swap(self, values, axis, step):
        return swap(self.gate(values), axis, step)


class Doubling:
    def __init__(self, clock, values, axis):
        self.clock, self.axis = clock, axis
        self.pieces = [values]
        self.arrays = []
        self.bits = bits_of(lax.axis_size(axis))
        self.stage = 0
        self.got = None

    def start(self):
        message = self.pieces[0][None] if self.stage == 0 else jnp.stack(self.pieces, 0)
        self.got = cross(self.clock.gate(message), self.axis, self.stage)
        self.stage += 1

    def wait(self):
        got = self.clock.wait(self.got)
        self.arrays.append(got)
        self.pieces += [got[i] for i in range(len(self.pieces))]

    def finish(self):
        self.wait()
        while self.stage < self.bits:
            self.start()
            self.wait()


class Transposing:
    def __init__(self, clock, chunks, axis):
        self.clock, self.axis = clock, axis
        self.pieces = list(chunks)
        self.bits = bits_of(lax.axis_size(axis))
        self.stage = 0
        self.found = {}

    def moved(self):
        return [q for q in range(len(self.pieces)) if (q >> (self.stage - 1)) & 1]

    def start(self):
        self.stage += 1
        message = jnp.stack([self.pieces[q] for q in self.moved()], 0)
        self.got = cross(self.clock.gate(message), self.axis, self.stage - 1)

    def wait(self):
        self.got = self.clock.wait(self.got)
        for i, q in enumerate(self.moved()):
            self.pieces[q] = self.got[i]
            self.found[q] = (self.got, i)

    def finish(self):
        self.wait()
        while self.stage < self.bits:
            self.start()
            self.wait()


class Direct:
    def __init__(self, clock, chunks, axis):
        self.clock, self.axis = clock, axis
        self.pieces = list(chunks)

    def start(self):
        size = lax.axis_size(self.axis)
        for q in range(1, size):
            pairs = []
            for i in range(size):
                pairs += [(2 * i, 2 * (i ^ q)), (2 * i + 1, 2 * (i ^ back_of(q, size)) + 1)]
            chunk = self.clock.gate(self.pieces[q])
            self.pieces[q] = lax.ppermute(chunk, (self.axis, "blk"), pairs)

    def finish(self):
        self.pieces[1:] = list(self.clock.wait(*self.pieces[1:]))


class Halving:
    def __init__(self, clock, keep, send, axis):
        self.clock, self.axis = clock, axis
        self.keep, self.send = keep, send
        self.stage = bits_of(lax.axis_size(axis)) - 1
        self.got = None

    def start(self):
        self.got = cross(self.clock.gate(self.send), self.axis, self.stage)
        self.stage -= 1

    def wait(self):
        got = self.clock.wait(self.got)
        if self.stage < 0:
            self.own, self.last = self.keep[0], got[0]
            return
        half = self.keep.shape[0] // 2
        self.send = (self.keep[half:] + got[half:].astype(single)).astype(bfloat)
        self.keep = self.keep[:half] + got[:half].astype(single)

    def finish(self):
        self.wait()
        while self.stage >= 0:
            self.start()
            self.wait()

    def sum(self):
        return self.own + self.last.astype(single)


class Exchange:
    def __init__(self, clock, near, far):
        self.clock, self.near = clock, near
        self.far = clock.swap(far, "blk", 1)

    def cross(self):
        self.far = self.clock.wait(self.far)
        both = [jnp.stack([self.near[q], self.far[q]], 0) for q in range(self.near.shape[0])]
        self.by_z = Transposing(self.clock, both, "ctx")
        self.by_z.start()

    def wait(self):
        self.by_z.wait()
        self.by_z.start()

    def finish(self):
        self.by_z.finish()
        self.pieces = self.by_z.pieces


def tree_sum(parts):
    while len(parts) > 1:
        parts = [parts[i] + parts[i + 1] for i in range(0, len(parts), 2)]
    return parts[0]


def reorder(parts, index):
    count = len(parts)
    bit = 1
    parts = list(parts)
    while bit < count:
        flag = (index & bit) != 0
        parts = [jnp.where(flag, parts[i ^ bit], parts[i]) for i in range(count)]
        bit *= 2
    return parts


def after(values, *earlier):
    return lax.optimization_barrier((values,) + earlier)[0]


def aligned(index, unit):
    return pl.multiple_of(index, unit)


def project_text(ids, own_part, parts, text, own_wide, kv_wide, f_size):
    rows, cols = own_part.shape
    count = f_size
    n_parts = len(parts)

    def body(*refs):
        ids_ref, text_ref = refs[0], refs[1]
        own_ref = refs[2]
        part_refs = refs[3 : 3 + n_parts]
        w_ref, kv_ref, pairs_ref, table_ref = refs[3 + n_parts : 7 + n_parts]
        full, sems = refs[7 + n_parts :]
        f, b = ids_ref[0], ids_ref[2]
        sources = [own_ref] + [ref.at[i] for ref in part_refs for i in range(ref.shape[0])]
        copies = []
        for q, source in enumerate(sources):
            place = pl.ds(aligned((f ^ step_of(q, b, count)) * rows, 16), rows)
            copies.append(pltpu.make_async_copy(source, full.at[place, :], sems.at[q]))
        for copy in copies:
            copy.start()
        for copy in copies:
            copy.wait()
        turned = full[...].T
        w_ref[...] = turned[:own_wide]
        kv = turned[own_wide : own_wide + kv_wide]
        kv_ref[...] = kv
        pairs_ref[...] = dot(kv, text_ref[...], (1, 1)).astype(bfloat)
        table_ref[...] = turned[own_wide + kv_wide :].astype(single)

    return call(
        body,
        [
            shape((own_wide, D)),
            shape((kv_wide, D)),
            shape((kv_wide, TEXT)),
            shape((cols - own_wide - kv_wide, D), single),
        ],
        [ids, text, own_part] + list(parts),
        [SMEM, VMEM] + [ANY] * (1 + n_parts),
        [pltpu.VMEM((count * rows, cols), bfloat), pltpu.SemaphoreType.DMA((count,))],
        megabytes=16,
        micros=MICROS["project_text"],
    )


def attend_forward(ids, w_t, modulation, x_parts, x_kinds, heads_here, z_size):
    tok = x_parts[0].shape[-2]
    count = 2 * z_size
    total = count * tok
    width = 256 if total % 256 == 0 else tok
    per = width // tok
    n_parts = len(x_parts)

    def body(*refs):
        ids_ref, w_ref, mod_ref = refs[:3]
        x_refs = refs[3 : 3 + n_parts]
        near_ref, far_ref, qkv_ref, norm_ref, x_all = refs[3 + n_parts : 8 + n_parts]
        raw, sems = refs[8 + n_parts :]
        b = ids_ref[2]
        copies = []
        for ref, chunks in zip(x_refs, x_kinds):
            for i, chunk in enumerate(chunks):
                source = ref if len(ref.shape) == 2 else ref.at[i]
                target = raw.at[pl.ds(chunk * tok, tok), :]
                copies.append(pltpu.make_async_copy(source, target, sems.at[chunk]))
        for copy in copies:
            copy.start()
        for copy in copies:
            copy.wait()

        def project(j, carry):
            place = pl.ds(aligned(j * width, width), width)
            normed, _ = layer_norm(raw[place, :].astype(single))
            modulated = (normed * (1.0 + mod_ref[1:2]) + mod_ref[0:1]).astype(bfloat)
            x_all[place, :] = modulated
            got = dot(w_ref[...], modulated, (1, 1))
            for i in range(3 * heads_here):
                qkv_ref[i, :, place] = got[i * HEAD : (i + 1) * HEAD].astype(bfloat)
            return carry

        lax.fori_loop(0, total // width, project, 0)

        def attend(h, carry):
            keys = qkv_ref[heads_here + h]
            values = qkv_ref[2 * heads_here + h]
            for core, target in ((0, near_ref), (1, far_ref)):

                def block(j, carry, core=core, target=target):
                    at = core * z_size * tok + j * width
                    place = pl.ds(aligned(at, width), width)
                    scores = dot(keys, qkv_ref[h, :, place], (0, 0)) * scaling
                    top = jnp.max(scores, axis=0, keepdims=True)
                    exponent = jnp.exp(scores - top)
                    summed = jnp.sum(exponent, axis=0, keepdims=True)
                    weights = (exponent * (1.0 / summed)).astype(bfloat)
                    mixed = dot(values, weights).astype(bfloat)
                    norm_ref[h, :, place] = top + jnp.log(summed)
                    for i in range(per):
                        piece = mixed[:, i * tok : (i + 1) * tok]
                        target[j * per + i, h] = piece
                    return carry

                lax.fori_loop(0, z_size * tok // width, block, 0)
            return carry

        lax.fori_loop(0, heads_here, attend, 0)

    wide = heads_here * HEAD
    return call(
        body,
        [
            shape((z_size, heads_here, HEAD, tok)),
            shape((z_size, heads_here, HEAD, tok)),
            shape((3 * heads_here, HEAD, total)),
            shape((heads_here, 1, total), single),
            shape((total, D)),
        ],
        [ids, w_t, modulation] + list(x_parts),
        [SMEM, VMEM, VMEM] + [ANY] * n_parts,
        [pltpu.VMEM((total, D), bfloat), pltpu.SemaphoreType.DMA((count,))],
        megabytes=24,
        micros=MICROS["attend_forward"],
    )


def weight_copies(piece_refs, kinds, full, sems, f, b, rows):
    copies = []
    half = rows // 2
    for i, (ref, kind) in enumerate(zip(piece_refs, kinds)):
        sem = sems.at[i]
        if kind[0] == "whole":
            copies.append(pltpu.make_async_copy(ref, full, sem))
        elif kind[0] == "own":
            place = pl.ds(aligned(f * rows, 16), rows)
            copies.append(pltpu.make_async_copy(ref, full.at[kind[1], place, :], sem))
        else:
            core = b if kind[0] == "near" else 1 - b
            source = f ^ kind[2](core)
            place = pl.ds(aligned(source * rows + core * half, 16), half)
            target = full.at[:, place, :]
            ref = ref if kind[1] is None else ref.at[kind[1]]
            copies.append(pltpu.make_async_copy(ref, target, sem))
    return copies


def piece_specs(kinds):
    return [HBM if kind[0] == "own" else ANY for kind in kinds]


def permute_rows(source, target, count, piece):
    for k in range(count):
        for core in range(2):
            target[core, pl.ds(k * piece, piece), :] = source[
                pl.ds((2 * k + core) * piece, piece), :
            ]


def token_forward(ids, got, x, modulation, pair_parts, pieces, kinds, f_size, z_size):
    tok = x.shape[0]
    heads_here = got[0].shape[1]
    rows = D // f_size
    own = D // (2 * f_size * z_size)
    kv_wide = D // z_size
    n_got, n_pieces, n_pairs = len(got), len(pieces), len(pair_parts)

    def body(*refs):
        ids_ref, x_ref, mod_ref = refs[:3]
        got_refs = refs[3 : 3 + n_got]
        pair_refs = refs[3 + n_got : 3 + n_got + n_pairs]
        at = 3 + n_got + n_pairs
        piece_refs = refs[at : at + n_pieces]
        rest = refs[at + n_pieces :]
        x_two_ref, second_ref, branch_ref, p_ref, cq_ref, keep_ref, send_ref, pairs_ref = rest[:8]
        full, mixed, pair_s, turned, left, sems = rest[8:]
        f, z, b = ids_ref[0], ids_ref[1], ids_ref[2]
        copies = weight_copies(piece_refs, kinds, full, sems, f, b, rows)
        for copy in copies:
            copy.start()

        for q in range(z_size):
            for core in range(2):
                g = 2 * (z ^ step_of(q, b, z_size)) + (b ^ core)
                for h in range(heads_here):
                    place = pl.ds(aligned((g * heads_here + h) * HEAD, 8), HEAD)
                    mixed[place, :] = got_refs[q][core, h].astype(single)
        for core in range(2):
            q = 0
            for ref in pair_refs[core * (n_pairs // 2) : (core + 1) * (n_pairs // 2)]:
                for source in [ref] if len(ref.shape) == 2 else [ref.at[i] for i in range(ref.shape[0])]:
                    g = 2 * (z ^ step_of(q, b ^ core, z_size)) + (b ^ core)
                    place = pl.ds(aligned(g * kv_wide, 8), kv_wide)
                    pair_s[place, :] = source[...].astype(single)
                    q += 1
        pairs_ref[...] = pair_s[...]

        def keep_left(i, source):
            permute_rows(source, left, f_size * z_size, own)
            keep_ref[i] = left[b].astype(bfloat)
            send_ref[i] = left[1 - b].astype(bfloat)

        keep_left(0, mixed)
        shift_two, scale_two, gate_one = mod_ref[3:4], mod_ref[4:5], mod_ref[2:3]
        for copy in copies:
            copy.wait()
        branch = dot(mixed[...].T.astype(bfloat), full[0])
        branch_ref[...] = branch
        first = x_ref[...].astype(single) + gate_one * branch
        first_low = first.astype(bfloat)
        turned[...] = first_low.astype(single).T
        keep_left(1, turned)
        turned[...] = dot(first_low, full[1]).T
        cq_ref[...] = turned[...].astype(bfloat)
        def attend(h, carry):
            rows_h = pl.ds(aligned(h * HEAD, 8), HEAD)
            keys = pair_s[rows_h, :].astype(bfloat)
            values = pair_s[pl.ds(aligned(D + h * HEAD, 8), HEAD), :].astype(bfloat)
            scores = dot(keys, turned[rows_h, :].astype(bfloat), (0, 0)) * scaling
            top = jnp.max(scores, axis=0, keepdims=True)
            exponent = jnp.exp(scores - top)
            weights = exponent * (1.0 / jnp.sum(exponent, axis=0, keepdims=True))
            p_ref[h] = weights
            mixed[rows_h, :] = dot(values, weights.astype(bfloat)).astype(bfloat).astype(single)
            return carry

        lax.fori_loop(0, HEADS, attend, 0, unroll=4)
        second = first + dot(mixed[...].T.astype(bfloat), full[2])
        second_ref[...] = second
        normed, _ = layer_norm(second)
        x_two_ref[...] = (normed * (1.0 + scale_two) + shift_two).astype(bfloat)
        keep_left(2, mixed)

    return call(
        body,
        [
            shape((tok, D)),
            shape((tok, D), single),
            shape((tok, D), single),
            shape((HEADS, TEXT, tok), single),
            shape((D, tok)),
            shape((3, D // 2, tok)),
            shape((3, D // 2, tok)),
            shape((2 * D, TEXT), single),
        ],
        [ids, x, modulation] + list(got) + list(pair_parts) + list(pieces),
        [SMEM] + [VMEM] * (2 + n_got + n_pairs) + piece_specs(kinds),
        [
            pltpu.VMEM((3, D, D), bfloat),
            pltpu.VMEM((D, tok), single),
            pltpu.VMEM((2 * D, TEXT), single),
            pltpu.VMEM((D, tok), single),
            pltpu.VMEM((2, D // 2, tok), single),
            pltpu.SemaphoreType.DMA((n_pieces,)),
        ],
        megabytes=28,
        micros=MICROS["token_forward"],
    )


def feed_forward(ids, x_parts, grad_hidden, pieces, kinds, ff, f_size):
    count = f_size
    n_parts = len(x_parts)
    tok = x_parts[0].shape[0]
    tile = 384 if ff % 384 == 0 else ff
    rows = D // f_size
    n_pieces = len(pieces)

    def body(*refs):
        ids_ref = refs[0]
        x_refs = refs[1 : 1 + n_parts]
        gh_ref = refs[1 + n_parts]
        piece_refs = refs[2 + n_parts : 2 + n_parts + n_pieces]
        rest = refs[2 + n_parts + n_pieces :]
        hidden_ref, pre_ref, keep_ref, send_ref = rest[:4]
        x_all, full, sems = rest[4:]
        up_ref = full.at[0]
        copies = weight_copies(piece_refs, kinds, full, sems, ids_ref[0], ids_ref[2], rows)
        for copy in copies:
            copy.start()
        x_all[0:tok, :] = x_refs[0][...]
        at = tok
        for ref in x_refs[1:]:
            for i in range(ref.shape[0]):
                x_all[at : at + tok, :] = ref[i]
                at += tok
        for copy in copies:
            copy.wait()

        def step(j, carry):
            place = pl.ds(aligned(j * tile, 128), tile) if ff > tile else pl.ds(0, tile)
            u = dot(x_all[...], up_ref[:, place])
            square = u * u
            t = jnp.tanh(0.7978845608028654 * u * (1.0 + 0.044715 * square))
            half = 0.5 * (1.0 + t)
            hidden_ref[:, place] = (u * half).astype(bfloat)
            slope = half + 0.5 * u * (1.0 - t * t) * (
                0.7978845608028654 * (1.0 + 0.134145 * square)
            )
            pre_ref[:, place] = (gh_ref[:, place] * slope).astype(bfloat)
            return carry

        if ff > tile:
            lax.fori_loop(0, ff // tile, step, 0)
        else:
            step(0, 0)
        part = dot(pre_ref[...], up_ref[...], (1, 1))
        for i in range(count):
            piece = part[i * tok : (i + 1) * tok]
            if i < count // 2:
                keep_ref[i] = piece
            else:
                send_ref[i - count // 2] = piece.astype(bfloat)

    total = count * tok
    return call(
        body,
        [
            shape((total, ff)),
            shape((total, ff)),
            shape((count // 2, tok, D), single),
            shape((count // 2, tok, D)),
        ],
        [ids] + list(x_parts) + [grad_hidden] + list(pieces),
        [SMEM] + [VMEM] * (n_parts + 1) + piece_specs(kinds),
        [
            pltpu.VMEM((total, D), bfloat),
            pltpu.VMEM((1, D, ff), bfloat),
            pltpu.SemaphoreType.DMA((n_pieces,)),
        ],
        megabytes=24,
        micros=MICROS["feed_forward"],
    )


def feed_forward_turn(ids, x_parts, hidden, f_size, z_size):
    n_parts = len(x_parts)
    tok = x_parts[0].shape[0]
    total, ff = hidden.shape
    own = D // (2 * f_size * z_size)
    own_down = ff // (2 * z_size)

    def body(*refs):
        ids_ref, hidden_ref = refs[:2]
        x_refs = refs[2 : 2 + n_parts]
        hk_ref, hs_ref, xk_ref, xs_ref, flat, halves, flat_down, halves_down = refs[2 + n_parts :]
        b = ids_ref[2]
        flat_down[...] = hidden_ref[...].T.astype(single)
        permute_rows(flat_down, halves_down, z_size, own_down)
        hk_ref[...] = halves_down[b].astype(bfloat)
        hs_ref[...] = halves_down[1 - b].astype(bfloat)
        flat[:, 0:tok] = x_refs[0][...].T.astype(single)
        at = tok
        for ref in x_refs[1:]:
            for i in range(ref.shape[0]):
                flat[:, at : at + tok] = ref[i].T.astype(single)
                at += tok
        permute_rows(flat, halves, f_size * z_size, own)
        xk_ref[...] = halves[b].astype(bfloat)
        xs_ref[...] = halves[1 - b].astype(bfloat)

    return call(
        body,
        [shape((ff // 2, total))] * 2 + [shape((D // 2, total))] * 2,
        [ids, hidden] + list(x_parts),
        [SMEM] + [VMEM] * (1 + n_parts),
        [
            pltpu.VMEM((D, total), single),
            pltpu.VMEM((2, D // 2, total), single),
            pltpu.VMEM((ff, total), single),
            pltpu.VMEM((2, ff // 2, total), single),
        ],
        megabytes=20,
        micros=MICROS["feed_forward_turn"],
    )


def feed_forward_out(ids, hidden, down, count):
    total = hidden.shape[0]
    tok = total // count

    def body(_, hidden_ref, down_ref, keep_ref, send_ref):
        part = dot(hidden_ref[...], down_ref[...])
        for i in range(count):
            piece = part[i * tok : (i + 1) * tok]
            if i < count // 2:
                keep_ref[i] = piece
            else:
                send_ref[i - count // 2] = piece.astype(bfloat)

    return call(
        body,
        [shape((count // 2, tok, D), single), shape((count // 2, tok, D))],
        [ids, hidden, down],
        [SMEM, VMEM, VMEM],
        megabytes=12,
        micros=MICROS["feed_forward_out"],
    )


def chip_grads(ids, index, left, left_far, right, right_far, count, direct):
    rows, tok = left.shape
    cols = right.shape[1]
    part = rows // count
    held = 1 if direct else count // 2

    def body(*refs):
        ids_ref, left_ref, lf_ref, right_ref, rf_ref, keep_ref, send_ref = refs[:7]
        left_s, right_s, flat = refs[7:]
        i, b = ids_ref[index], ids_ref[2]
        left_s[:, 0:tok] = left_ref[...]
        left_s[:, tok : 2 * tok] = lf_ref[...]
        right_s[0:tok, :] = right_ref[...]
        right_s[tok : 2 * tok, :] = rf_ref[...]
        value = dot(left_s[...], right_s[...])
        for k in range(count):
            flat[k] = value[k * part : (k + 1) * part]
        for q in range(count):
            piece = flat[i ^ step_of(q, b, count)]
            if q < held:
                keep_ref[q] = piece
            else:
                send_ref[q - held] = piece.astype(bfloat)

    return call(
        body,
        [shape((held, part, cols), single), shape((count - held, part, cols))],
        [ids, left, left_far, right, right_far],
        [SMEM] + [VMEM] * 4,
        [
            pltpu.VMEM((rows, 2 * tok), bfloat),
            pltpu.VMEM((2 * tok, cols), bfloat),
            pltpu.VMEM((count, part, cols), single),
        ],
        megabytes=24,
        micros=MICROS["chip_grads"],
    )


def token_backward(
    ids, own, got, second, branch, cotangent, modulation, p, cq, pairs, pieces, kinds, f_size, z_size
):
    tok = second.shape[0]
    heads_here = HEADS // (2 * z_size)
    rows = D // f_size
    kv_wide = D // z_size
    n_got, n_pieces = len(got), len(pieces)

    def body(*refs):
        ids_ref, own_ref, second_ref, branch_ref, cot_ref, mod_ref, p_ref, cq_ref, pairs_ref = refs[:9]
        got_refs = refs[9 : 9 + n_got]
        piece_refs = refs[9 + n_got : 9 + n_got + n_pieces]
        rest = refs[9 + n_got + n_pieces :]
        near_ref, far_ref, right_ref, first_ref, stat_ref, pair_keep, pair_send = rest[:7]
        full, turned, grads, low, sems = rest[7:]
        pair_s = pairs_ref
        f, z, b = ids_ref[0], ids_ref[1], ids_ref[2]
        copies = weight_copies(piece_refs, kinds, full, sems, f, b, rows)
        for copy in copies:
            copy.start()
        gate_one, scale_two = mod_ref[2:3], mod_ref[4:5]
        grad_mod = own_ref[...]
        for ref in got_refs:
            grad_mod = grad_mod + ref[...].astype(single)
        normed, inverse = layer_norm(second_ref[...])
        stat_ref[1:2] = jnp.sum(grad_mod, axis=0, keepdims=True)
        stat_ref[2:3] = jnp.sum(grad_mod * normed, axis=0, keepdims=True)
        grad_second = cot_ref[...].astype(single) + norm_back(
            grad_mod * (1.0 + scale_two), normed, inverse
        )
        grad_low = grad_second.astype(bfloat)
        right_ref[2] = grad_low
        for copy in copies:
            copy.wait()
        turned[...] = dot(full[2], grad_low, (1, 1))
        low[...] = cq_ref[...].astype(single)
        def attend(h, carry):
            rows_h = pl.ds(aligned(h * HEAD, 8), HEAD)
            rows_v = pl.ds(aligned(D + h * HEAD, 8), HEAD)
            keys = pair_s[rows_h, :].astype(bfloat)
            values = pair_s[rows_v, :].astype(bfloat)
            grad_h = turned[rows_h, :].astype(bfloat)
            weights = p_ref[h]
            grad_weights = dot(values, grad_h, (0, 0))
            grads[rows_v, :] = dot(grad_h, weights.astype(bfloat), (1, 1))
            inner = jnp.sum(weights * grad_weights, axis=0, keepdims=True)
            grad_scores = (weights * (grad_weights - inner)).astype(bfloat)
            turned[rows_h, :] = scaling * dot(keys, grad_scores)
            grads[rows_h, :] = scaling * dot(low[rows_h, :].astype(bfloat), grad_scores, (1, 1))
            return carry

        lax.fori_loop(0, HEADS, attend, 0, unroll=4)
        for q in range(z_size):
            here = 2 * (z ^ step_of(q, b, z_size)) + b
            there = 2 * (z ^ step_of(q, 1 - b, z_size)) + 1 - b
            pair_keep[q] = grads[pl.ds(aligned(here * kv_wide, 8), kv_wide), :]
            place = pl.ds(aligned(there * kv_wide, 8), kv_wide)
            pair_send[q] = grads[place, :].astype(bfloat)
        grad_query = turned[...].T.astype(bfloat)
        right_ref[1] = grad_query
        grad_first = grad_second + dot(grad_query, full[1], (1, 1))
        first_ref[...] = grad_first
        stat_ref[0:1] = jnp.sum(grad_first * branch_ref[...], axis=0, keepdims=True)
        grad_branch = (gate_one * grad_first).astype(bfloat)
        right_ref[0] = grad_branch
        turned[...] = dot(full[0], grad_branch, (1, 1))
        for q in range(z_size):
            for core in range(2):
                target = near_ref if core == 0 else far_ref
                g = 2 * (z ^ step_of(q, b ^ core, z_size)) + (b ^ core)
                for h in range(heads_here):
                    place = pl.ds(aligned((g * heads_here + h) * HEAD, 8), HEAD)
                    target[q, h] = turned[place, :].astype(bfloat)

    return call(
        body,
        [
            shape((z_size, heads_here, HEAD, tok)),
            shape((z_size, heads_here, HEAD, tok)),
            shape((3, tok, D)),
            shape((tok, D), single),
            shape((3, D), single),
            shape((z_size, kv_wide, TEXT), single),
            shape((z_size, kv_wide, TEXT)),
        ],
        [ids, own, second, branch, cotangent, modulation, p, cq, pairs] + list(got) + list(pieces),
        [SMEM] + [VMEM] * (8 + n_got) + piece_specs(kinds),
        [
            pltpu.VMEM((3, D, D), bfloat),
            pltpu.VMEM((D, tok), single),
            pltpu.VMEM((2 * D, TEXT), single),
            pltpu.VMEM((D, tok), single),
            pltpu.SemaphoreType.DMA((n_pieces,)),
        ],
        megabytes=28,
        micros=MICROS["token_backward"],
    )


def square_grads(ids, left, left_far, right, right_far, f_size):
    count, half, tok = left.shape
    part = half // f_size

    def body(*refs):
        ids_ref, left_ref, lf_ref, right_ref, rf_ref, keep_ref, send_ref = refs[:7]
        left_s, right_s, flat = refs[7:]
        f, b = ids_ref[0], ids_ref[2]
        for i in range(count):
            left_s[:, 0:tok] = left_ref[i]
            left_s[:, tok : 2 * tok] = lf_ref[i]
            right_s[0:tok, :] = right_ref[i]
            right_s[tok : 2 * tok, :] = rf_ref[i]
            value = dot(left_s[...], right_s[...])
            for k in range(f_size):
                flat[k] = value[k * part : (k + 1) * part]
            for q in range(f_size):
                value = flat[f ^ step_of(q, b, f_size)]
                if q < f_size // 2:
                    keep_ref[q, i] = value
                else:
                    send_ref[q - f_size // 2, i] = value.astype(bfloat)

    return call(
        body,
        [
            shape((f_size // 2, count, part, D), single),
            shape((f_size // 2, count, part, D)),
        ],
        [ids, left, left_far, right, right_far],
        [SMEM] + [VMEM] * 4,
        [
            pltpu.VMEM((half, 2 * tok), bfloat),
            pltpu.VMEM((2 * tok, D), bfloat),
            pltpu.VMEM((f_size, part, D), single),
        ],
        megabytes=20,
        micros=MICROS["square_grads"],
    )


def sum_split(ids, index, own, got, count, add):
    lead, rows, cols = own.shape
    part = rows // count
    n_got = len(got)
    groups = lead if add else lead * (1 + n_got)

    def body(*refs):
        ids_ref, own_ref = refs[:2]
        got_refs = refs[2 : 2 + n_got]
        keep_ref, send_ref, flat, chunks = refs[2 + n_got :]
        i, b = ids_ref[index], ids_ref[2]

        for k in range(lead):
            if add:
                value = own_ref[k]
                for ref in got_refs:
                    value = value + ref[k].astype(single)
                flat[k] = value
            else:
                flat[k] = own_ref[k]
                for j, ref in enumerate(got_refs):
                    flat[(j + 1) * lead + k] = ref[k].astype(single)
        for k in range(groups):
            for c in range(count):
                chunks[c, pl.ds(k * part, part), :] = flat[k, pl.ds(c * part, part), :]
        for q in range(count):
            value = chunks[i ^ step_of(q, b, count)]
            if q < count // 2:
                keep_ref[q] = value
            else:
                send_ref[q - count // 2] = value.astype(bfloat)

    return call(
        body,
        [
            shape((count // 2, groups * part, cols), single),
            shape((count // 2, groups * part, cols)),
        ],
        [ids, own] + list(got),
        [SMEM] + [VMEM] * (1 + n_got),
        [
            pltpu.VMEM((groups, rows, cols), single),
            pltpu.VMEM((count, groups * part, cols), single),
        ],
        megabytes=24,
        micros=MICROS["sum_split"],
    )


def attend_backward(ids, h, qkv, norm, got, z_size):
    heads_here, _, tok = got[0].shape[1:]
    count = 2 * z_size
    total = count * tok
    width = 256 if total % 256 == 0 else tok
    n_got = len(got)

    def body(*refs):
        _, qkv_ref, norm_ref = refs[:3]
        got_refs = refs[3 : 3 + n_got]
        out_ref, grad, flat_k, flat_v = refs[3 + n_got :]
        for core in range(2):
            for q in range(z_size):
                at = (core * z_size + q) * tok
                place = q if core == 0 else back_of(q, z_size)
                grad[:, at : at + tok] = got_refs[place][core, h]
        flat_k[...] = jnp.zeros_like(flat_k)
        flat_v[...] = jnp.zeros_like(flat_v)
        keys = qkv_ref[heads_here + h]
        values = qkv_ref[2 * heads_here + h]

        def block(j, carry):
            place = pl.ds(aligned(j * width, width), width)
            query = qkv_ref[h, :, place]
            grad_h = grad[:, place]
            scores = dot(keys, query, (0, 0)) * scaling
            weights = jnp.exp(scores - norm_ref[h, :, place])
            grad_weights = dot(values, grad_h, (0, 0))
            inner = jnp.sum(weights * grad_weights, axis=0, keepdims=True)
            grad_scores = (weights * (grad_weights - inner)).astype(bfloat)
            flat_v[...] += dot(grad_h, weights.astype(bfloat), (1, 1))
            out_ref[0, :, place] = (scaling * dot(keys, grad_scores)).astype(bfloat)
            flat_k[...] += scaling * dot(query, grad_scores, (1, 1))
            return carry

        lax.fori_loop(0, total // width, block, 0)
        out_ref[1] = flat_k[...].astype(bfloat)
        out_ref[2] = flat_v[...].astype(bfloat)

    return call(
        body,
        [shape((3, HEAD, total))],
        [ids, qkv, norm] + list(got),
        [SMEM] + [VMEM] * (2 + n_got),
        [
            pltpu.VMEM((HEAD, total), bfloat),
            pltpu.VMEM((HEAD, total), single),
            pltpu.VMEM((HEAD, total), single),
        ],
        megabytes=20,
        micros=MICROS["attend_backward"],
    )


def attend_project(ids, grads, w_t, z_size):
    heads_here = len(grads)
    total = grads[0].shape[-1]
    tok = total // (2 * z_size)
    wide3 = 3 * heads_here * HEAD
    width = z_size * tok

    def body(*refs):
        w_ref = refs[1]
        grad_refs = refs[2 : 2 + heads_here]
        close_ref, away_ref, low, flat = refs[2 + heads_here :]
        for h in range(heads_here):
            for i in range(3):
                place = pl.ds((i * heads_here + h) * HEAD, HEAD)
                flat[place, :] = grad_refs[h][i].astype(single)
        low[...] = flat[...].astype(bfloat)
        for core in (1, 0):
            part = dot(low[:, core * width : (core + 1) * width], w_ref[...], (0, 0))
            for q in range(z_size):
                piece = part[q * tok : (q + 1) * tok]
                if core == 0:
                    close_ref[q] = piece
                else:
                    away_ref[q] = piece.astype(bfloat)

    return call(
        body,
        [
            shape((z_size, tok, D), single),
            shape((z_size, tok, D)),
            shape((wide3, total)),
        ],
        [ids, w_t] + list(grads),
        [SMEM] + [VMEM] * (1 + heads_here),
        [pltpu.VMEM((wide3, total), single)],
        megabytes=24,
        micros=MICROS["attend_project"],
    )


def text_grads(ids, own, got, kv_t):
    def body(ids_ref, own_ref, got_ref, kv_ref, pairs_ref, keep_ref, send_ref, flat):
        b = ids_ref[2]
        pairs = (own_ref[...] + got_ref[...].astype(single)).astype(bfloat)
        pairs_ref[...] = pairs
        part = dot(kv_ref[...], pairs, (0, 0))
        flat[0] = part[: D // 2]
        flat[1] = part[D // 2 :]
        keep_ref[...] = flat[b]
        send_ref[...] = flat[1 - b]

    return call(
        body,
        [
            shape(own.shape),
            shape((D // 2, TEXT), single),
            shape((D // 2, TEXT), single),
        ],
        [ids, own, got, kv_t],
        [SMEM] + [VMEM] * 3,
        [pltpu.VMEM((2, D // 2, TEXT), single)],
        megabytes=16,
        micros=MICROS["text_grads"],
    )


def split_columns(ids, own, got, z_size):
    rows, cols = own.shape
    part = rows // z_size

    def body(ids_ref, own_ref, got_ref, out_ref, chunks):
        z, b = ids_ref[1], ids_ref[2]
        value = own_ref[...] + got_ref[...].astype(single)
        for k in range(z_size):
            chunks[k] = value[k * part : (k + 1) * part]
        for q in range(z_size):
            out_ref[q] = chunks[z ^ step_of(q, b, z_size)].astype(bfloat)

    return call(
        body,
        [shape((z_size, part, cols))],
        [ids, own, got],
        [SMEM] + [VMEM] * 2,
        [pltpu.VMEM((z_size, part, cols), single)],
        megabytes=16,
        micros=MICROS["split_columns"],
    )


def place_columns(ids, near, far, wide, z_size):
    part, cols = near[0].shape[0] // 2, near[0].shape[1]
    kv_wide = cols - 3 * wide

    def body(*refs):
        ids_ref = refs[0]
        in_ref, kv_ref, blocks, pair = refs[1 + 2 * z_size :]
        z, b = ids_ref[1], ids_ref[2]
        for core in range(2):
            for q in range(z_size):
                both = refs[1 + core * z_size + q][...].astype(single)
                pair[0] = both[:part]
                pair[1] = both[part:]
                blocks[z ^ step_of(q, b ^ core, z_size), b ^ core] = pair[b]
        for k in range(z_size):
            for core in range(2):
                g = 2 * k + core
                block = blocks[k, core]
                for i in range(3):
                    at = i * D + g * wide
                    in_ref[:, at : at + wide] = block[:, i * wide : (i + 1) * wide]
                kv_ref[:, g * kv_wide : (g + 1) * kv_wide] = block[:, 3 * wide :]

    return call(
        body,
        [shape((part, 3 * D), single), shape((part, 2 * D), single)],
        [ids] + list(near) + list(far),
        [SMEM] + [VMEM] * (2 * z_size),
        [pltpu.VMEM((z_size, 2, part, cols), single), pltpu.VMEM((2, part, cols), single)],
        megabytes=16,
        micros=MICROS["place_columns"],
    )


def column_grads(ids, joined, x_all, text, grad_pairs, f_size):
    wide3 = joined.shape[0]
    kv_wide = grad_pairs.shape[0]
    rows = D // f_size
    cols = wide3 + kv_wide

    def body(ids_ref, joined_ref, x_ref, text_ref, pairs_ref, keep_ref, send_ref, turned, kv_s):
        f, b = ids_ref[0], ids_ref[2]
        turned[...] = dot(joined_ref[...], x_ref[...]).T
        kv_s[...] = dot(text_ref[...], pairs_ref[...], (0, 1))
        held = f_size // 2
        for q in range(f_size):
            place = pl.ds(aligned((f ^ step_of(q, b, f_size)) * rows, 8), rows)
            if q < held:
                keep_ref[q, :, 0:wide3] = turned[place, :]
                keep_ref[q, :, wide3:cols] = kv_s[place, :]
            else:
                send_ref[q - held, :, 0:wide3] = turned[place, :].astype(bfloat)
                send_ref[q - held, :, wide3:cols] = kv_s[place, :].astype(bfloat)

    return call(
        body,
        [
            shape((f_size // 2, rows, cols), single),
            shape((f_size // 2, rows, cols)),
        ],
        [ids, joined, x_all, text, grad_pairs],
        [SMEM] + [VMEM] * 4,
        [pltpu.VMEM((D, wide3), single), pltpu.VMEM((D, kv_wide), single)],
        megabytes=24,
        micros=MICROS["column_grads"],
    )


def finish(ids, own, got, x, modulation, grad_first):
    tok = x.shape[0]
    n_got = len(got)

    def body(*refs):
        _, own_ref, x_ref, mod_ref, first_ref = refs[:5]
        got_refs = refs[5 : 5 + n_got]
        out_ref, stat_ref = refs[5 + n_got :]
        grad_mod = own_ref[...]
        for ref in got_refs:
            grad_mod = grad_mod + ref[...].astype(single)
        normed, inverse = layer_norm(x_ref[...].astype(single))
        stat_ref[0:1] = jnp.sum(grad_mod, axis=0, keepdims=True)
        stat_ref[1:2] = jnp.sum(grad_mod * normed, axis=0, keepdims=True)
        out_ref[...] = first_ref[...] + norm_back(grad_mod * (1.0 + mod_ref[1:2]), normed, inverse)

    return call(
        body,
        [shape((tok, D), single), shape((2, D), single)],
        [ids, own, x, modulation, grad_first] + list(got),
        [SMEM] + [VMEM] * (4 + n_got),
        micros=MICROS["finish"],
    )


class Summing:
    def __init__(self, clock, value, axes):
        self.clock, self.value = clock, value
        self.axes = list(axes)

    def start(self):
        axis = self.axes.pop(0)
        size = lax.axis_size(axis)
        self.got = [self.clock.swap(self.value, axis, step) for step in range(1, size)]

    def wait(self):
        parts = self.clock.wait(self.value, *self.got)
        self.value = tree_sum(list(parts))

    def finish(self):
        self.wait()
        while self.axes:
            self.start()
            self.wait()


MICROS = {
    "project_text": 2.6,
    "attend_forward": 1.5,
    "token_forward": 7.0,
    "feed_forward": 7.0,
    "feed_forward_turn": 0.1,
    "feed_forward_out": 0.1,
    "chip_grads": 0.1,
    "token_backward": 0.1,
    "square_grads": 0.1,
    "sum_split": 0.1,
    "attend_backward": 0.1,
    "attend_project": 0.1,
    "text_grads": 0.1,
    "split_columns": 0.1,
    "place_columns": 0.1,
    "column_grads": 1.5,
    "finish": 0.1,
}

ORDER = (
    "w0", "x0", "in0", "up0", "x1", "xc", "in1", "w1", "x2", "xd0", "in2", "proj",
    "pz0", "gb0", "xd", "attn", "ex0", "pz1", "pc", "gb1", "ex1", "ex2", "up1", "pz2",
    "pd", "w2", "wd", "ex3", "tok", "xt0", "lc", "gb2", "gbc", "xt1", "up2", "upc",
    "gh", "upd", "xt2", "ff", "gm0", "prc", "turn", "hsc", "xsc", "hsd", "down", "d0",
    "gm1", "xsd", "upg", "out", "gm2", "u0", "tb", "d1", "br0", "hx0", "rc", "hx1",
    "rd", "sq", "s0", "hx2", "u2", "us", "pg0", "br1", "hx3", "pgd", "pp0", "uz0",
    "h0", "h1", "pp1", "pj", "s1", "ac", "d2", "uz1", "pp2", "tg", "tc0", "br2",
    "ad", "m0", "col", "c0", "td0", "tz0", "s2", "ss", "c1", "uz2", "tz1", "m1",
    "sz0", "c2", "sp", "m2", "fin", "st0", "st1", "cx0", "sz1", "cx1", "tz2", "st3",
    "cx2", "cc", "cd", "pl", "td1", "st4", "sz2",
)


def shards(
    latents,
    text_embed,
    timestep,
    ada_table,
    w_attn_in,
    w_attn_out,
    w_cross_q,
    w_cross_kv,
    w_cross_out,
    w_mlp_up,
    w_mlp_down,
    grad_out,
):
    f_size = lax.axis_size("fsdp")
    z_size = lax.axis_size("ctx")
    group = 2 * z_size
    f = lax.axis_index("fsdp")
    z = lax.axis_index("ctx")
    b = lax.axis_index("blk")
    g = 2 * z + b
    ids = jnp.stack([f, z, b]).astype(jnp.int32)
    heads_here = HEADS // group
    wide = heads_here * HEAD
    kv_wide = 2 * D // group
    rows_f = D // f_size
    half_f = rows_f // 2
    own = D // (f_size * group)
    ff = w_mlp_up.shape[1] // f_size
    m_half = z_size // 2

    x = latents[0]
    cotangent = grad_out[0]
    text = text_embed[0]
    squares = [w_attn_out, w_cross_q, w_cross_out]
    clock = Clock(ids)
    run, swap_at, wait = clock.run, clock.swap, clock.wait

    def assemble(pieces, kinds):
        if half_f % 16 == 0:
            return pieces, kinds
        count = sum(kind[0] == "own" for kind in kinds)
        whole = jnp.zeros((count, f_size, rows_f, pieces[0].shape[-1]), bfloat)
        for part, kind in zip(pieces, kinds):
            if kind[0] == "own":
                whole = lax.dynamic_update_slice(whole, part[None, None], (kind[1], f, 0, 0))
            else:
                core = b if kind[0] == "near" else 1 - b
                part = part if kind[1] is None else part[kind[1]]
                whole = lax.dynamic_update_slice(
                    whole, part[:, None], (0, f ^ kind[2](core), core * half_f, 0)
                )
        return [whole.reshape(count, D, -1)], [("whole",)]

    class Events:
        def x0(self):
            self.x_z = Doubling(clock, x, "ctx")
            self.x_z.start()

        def x1(self):
            self.x_z.wait()
            self.x_z.start()

        def xc(self):
            self.x_far = [swap_at(part, "blk", 1) for part in (x, self.x_z.arrays[0])]

        def x2(self):
            self.x_z.finish()

        def xd0(self):
            self.x_far += [swap_at(part, "blk", 1) for part in self.x_z.arrays[1:]]

        def xd(self):
            self.x_far = list(wait(*self.x_far))

        def in0(self):
            self.own_in = jnp.concatenate(
                [
                    lax.dynamic_slice(w_attn_in, (0, i * D + g * wide), (rows_f, wide))
                    for i in range(3)
                ]
                + [lax.dynamic_slice(w_cross_kv, (0, g * kv_wide), (rows_f, kv_wide)), ada_table.T],
                axis=1,
            )
            self.in_f = Doubling(clock, self.own_in, "fsdp")
            self.in_f.start()

        def in1(self):
            self.in_f.wait()
            self.in_f.start()

        def in2(self):
            self.in_f.finish()

        def proj(self):
            self.w_t, self.kv_t, self.pairs_here, table = run(
                project_text, self.own_in, self.in_f.arrays, text, 3 * wide, kv_wide, f_size
            )
            self.modulation = table + timestep.reshape(6, D)

        def pz0(self):
            self.pair_z = Doubling(clock, self.pairs_here, "ctx")
            self.pair_z.start()

        def pz1(self):
            self.pair_z.wait()
            self.pair_z.start()

        def pc(self):
            self.pair_far = [
                swap_at(part, "blk", 1) for part in [self.pairs_here] + self.pair_z.arrays[:1]
            ]

        def pz2(self):
            self.pair_z.finish()
            self.pair_far += [swap_at(part, "blk", 1) for part in self.pair_z.arrays[1:]]

        def pd(self):
            self.pair_far = list(wait(*self.pair_far))

        def w0(self):
            half = jnp.stack(
                [lax.dynamic_slice(w, (b * half_f, 0), (half_f, D)) for w in squares], 0
            )
            self.w_f = Doubling(clock, half, "fsdp")
            self.w_f.start()

        def w1(self):
            self.w_f.wait()
            self.w_f.start()
            self.w_far = [swap_at(part, "blk", 1) for part in self.w_f.arrays]

        def w2(self):
            self.w_f.finish()
            self.w_far += [swap_at(part, "blk", 1) for part in self.w_f.arrays[1:]]

        def wd(self):
            self.w_far = list(wait(*self.w_far))
            pieces, kinds = list(squares), [("own", i) for i in range(3)]
            for name, arrays in (("near", self.w_f.arrays), ("far", self.w_far)):
                place = 1
                for part in arrays:
                    for i in range(part.shape[0]):
                        pieces.append(part)
                        kinds.append((name, i, functools.partial(step_of, place, size=f_size)))
                        place += 1
            self.pieces, self.kinds = assemble(pieces, kinds)

        def up0(self):
            up_half = lax.dynamic_slice(w_mlp_up, (b * half_f, 0), (half_f, f_size * ff))
            parts = [None] + [
                lax.dynamic_slice(up_half, (0, (f ^ step_of(q, b, f_size)) * ff), (half_f, ff))
                for q in range(1, f_size)
            ]
            self.up_f = Transposing(clock, parts, "fsdp")
            self.up_f.start()

        def up1(self):
            self.up_f.wait()
            self.up_f.start()

        def up2(self):
            self.up_f.finish()

        def upc(self):
            self.up_far = [
                swap_at(self.up_f.pieces[q][None], "blk", 1) for q in range(1, f_size)
            ]

        def upd(self):
            far = wait(*self.up_far)
            pieces = [lax.dynamic_slice(w_mlp_up, (0, f * ff), (rows_f, ff))]
            kinds = [("own", 0)]
            for q in range(1, f_size):
                place = functools.partial(step_of, q, size=f_size)
                got, i = self.up_f.found[q]
                pieces += [got[i][None], far[q - 1]]
                kinds += [("near", None, place), ("far", None, place)]
            self.up_pieces, self.up_kinds = assemble(pieces, kinds)

        def gb0(self):
            grad = (self.modulation[5:6] * cotangent.astype(single)).astype(bfloat)
            self.grad_f = Doubling(clock, grad, "fsdp")
            self.grad_f.start()

        def gb1(self):
            self.grad_f.wait()
            self.grad_f.start()

        def gb2(self):
            self.grad_f.finish()
            self.branch_all = jnp.concatenate(self.grad_f.pieces, 0)

        def gbc(self):
            self.branch_far = swap_at(self.branch_all, "blk", 1)

        def gh(self):
            self.grad_hidden = wait(dot(self.branch_all, w_mlp_down, (1, 1)))

        def attn(self):
            parts = [x] + self.x_z.arrays + self.x_far
            kinds, at = [], 0
            for part in parts:
                n = 1 if part.ndim == 2 else part.shape[0]
                kinds.append(list(range(at, at + n)))
                at += n
            near, far, self.qkv, self.norm, self.x_all = run(
                attend_forward, self.w_t, self.modulation, parts, kinds, heads_here, z_size
            )
            self.mixed = (near, far)

        def ex0(self):
            self.to_owner = Exchange(clock, *self.mixed)

        def ex1(self):
            self.to_owner.cross()

        def ex2(self):
            self.to_owner.wait()

        def ex3(self):
            self.to_owner.finish()

        def tok(self):
            (
                self.x_two,
                self.second,
                self.branch_one,
                self.p,
                self.cq,
                self.left,
                self.left_send,
                self.pairs,
            ) = run(
                token_forward,
                self.to_owner.pieces,
                x,
                self.modulation,
                [self.pairs_here] + self.pair_z.arrays + self.pair_far,
                self.pieces,
                self.kinds,
                f_size,
                z_size,
            )

        def lc(self):
            self.left_far = swap_at(self.left_send, "blk", 1)

        def xt0(self):
            self.x_two_f = Doubling(clock, self.x_two, "fsdp")
            self.x_two_f.start()

        def xt1(self):
            self.x_two_f.wait()
            self.x_two_f.start()

        def xt2(self):
            self.x_two_f.finish()
            self.x_two_parts = [self.x_two] + self.x_two_f.arrays

        def ff(self):
            self.hidden, self.pre, keep, send = run(
                feed_forward,
                self.x_two_parts,
                self.grad_hidden,
                self.up_pieces,
                self.up_kinds,
                ff,
                f_size,
            )
            self.gm = Halving(clock, keep, send, "fsdp")

        def gm0(self):
            self.gm.start()

        def gm1(self):
            self.gm.wait()
            self.gm.start()

        def gm2(self):
            self.gm.finish()

        def prc(self):
            self.pre_far = swap_at(self.pre, "blk", 1)

        def turn(self):
            self.hk, self.hs, self.xk, self.xs = run(
                feed_forward_turn, self.x_two_parts, self.hidden, f_size, z_size
            )

        def hsc(self):
            self.hs = swap_at(self.hs, "blk", 1)

        def xsc(self):
            self.xs = swap_at(self.xs, "blk", 1)

        def hsd(self):
            self.hs, self.branch_far = wait(self.hs, self.branch_far)

        def down(self):
            terms = run(
                chip_grads, 1, self.hk, self.hs, self.branch_all, self.branch_far, z_size, False
            )
            self.d = Halving(clock, *terms, "ctx")

        def d0(self):
            self.d.start()

        def d1(self):
            self.d.wait()
            self.d.start()

        def d2(self):
            self.d.finish()

        def xsd(self):
            self.xs, self.pre_far = wait(self.xs, self.pre_far)

        def upg(self):
            self.u_own, send = run(
                chip_grads, 0, self.xk, self.xs, self.pre, self.pre_far, f_size, True
            )
            self.u_f = Direct(clock, [None] + [send[q - 1] for q in range(1, f_size)], "fsdp")

        def u0(self):
            self.u_f.start()

        def u2(self):
            self.u_f.finish()

        def us(self):
            got = [self.u_f.pieces[q][None] for q in range(1, f_size)]
            terms = run(sum_split, 1, self.u_own, got, z_size, False)
            self.u = Halving(clock, *terms, "ctx")

        def uz0(self):
            self.u.start()

        def uz1(self):
            self.u.wait()
            self.u.start()

        def uz2(self):
            self.u.finish()

        def out(self):
            terms = run(feed_forward_out, self.hidden, w_mlp_down, f_size)
            self.branch = Halving(clock, *terms, "fsdp")

        def br0(self):
            self.branch.start()

        def br1(self):
            self.branch.wait()
            self.branch.start()

        def br2(self):
            self.branch.finish()
            mlp_branch = self.branch.sum()
            self.block_out = (self.second + self.modulation[5:6] * mlp_branch).astype(bfloat)
            self.stat_gate = jnp.sum(cotangent.astype(single) * mlp_branch, axis=0, keepdims=True)

        def tb(self):
            (
                near,
                far,
                self.right,
                self.grad_first,
                self.stat_mid,
                self.pair_keep,
                self.pair_send,
            ) = run(
                token_backward,
                self.gm.own,
                [self.gm.last],
                self.second,
                self.branch_one,
                cotangent,
                self.modulation,
                self.p,
                self.cq,
                self.pairs,
                self.pieces,
                self.kinds,
                f_size,
                z_size,
            )
            self.grad_mixed = (near, far)

        def hx0(self):
            self.to_heads = Exchange(clock, *self.grad_mixed)

        def hx1(self):
            self.to_heads.cross()

        def hx2(self):
            self.to_heads.wait()

        def hx3(self):
            self.to_heads.finish()

        def rc(self):
            self.right_far = swap_at(self.right, "blk", 1)

        def rd(self):
            self.right_far, self.left_far = wait(self.right_far, self.left_far)

        def sq(self):
            terms = run(
                square_grads, self.left, self.left_far, self.right, self.right_far, f_size
            )
            self.s = Halving(clock, *terms, "fsdp")

        def s0(self):
            self.s.start()

        def s1(self):
            self.s.wait()
            self.s.start()

        def s2(self):
            self.s.finish()

        def ss(self):
            terms = run(sum_split, 1, self.s.own, [self.s.last], z_size, True)
            self.s = Halving(clock, *terms, "ctx")

        def sz0(self):
            self.s.start()

        def sz1(self):
            self.s.wait()
            self.s.start()

        def sz2(self):
            self.s.finish()

        def pg0(self):
            self.pair_back = swap_at(self.pair_send, "blk", 1)

        def pgd(self):
            value = self.pair_keep + wait(self.pair_back).astype(single)
            self.pair = Halving(clock, value[:m_half], value[m_half:].astype(bfloat), "ctx")

        def pp0(self):
            self.pair.start()

        def pp1(self):
            self.pair.wait()
            self.pair.start()

        def pp2(self):
            self.pair.finish()

        def tg(self):
            self.grad_pairs, self.text_keep, self.text_send = run(
                text_grads, self.pair.own, self.pair.last, self.kv_t
            )

        def tc0(self):
            self.text_got = swap_at(self.text_send, "blk", 1)

        def td0(self):
            self.grad_text = (self.text_keep + wait(self.text_got)).astype(bfloat)

        def tz0(self):
            self.text_got = cross(clock.gate(self.grad_text), "ctx", 0)
            self.text_stage = 1

        def tz1(self):
            value = self.grad_text.astype(single) + wait(self.text_got).astype(single)
            self.grad_text = value.astype(bfloat)
            self.text_got = cross(clock.gate(self.grad_text), "ctx", self.text_stage)
            self.text_stage += 1

        def tz2(self):
            while self.text_stage < bits_of(z_size):
                self.tz1()
            self.grad_text = self.grad_text.astype(single) + wait(self.text_got).astype(single)
            self.text_got = swap_at(self.grad_text, "blk", 1)

        def td1(self):
            self.text_got = wait(self.text_got)

        def h0(self):
            self.grads = list(
                run(attend_backward, 0, self.qkv, self.norm, self.to_heads.pieces, z_size)
            )

        def h1(self):
            for h in range(1, heads_here):
                self.grads += run(
                    attend_backward, h, self.qkv, self.norm, self.to_heads.pieces, z_size
                )

        def pj(self):
            self.close, self.away, self.joined = run(
                attend_project, self.grads, self.w_t, z_size
            )

        def ac(self):
            self.away = swap_at(self.away, "blk", 1)

        def ad(self):
            value = self.close + wait(self.away).astype(single)
            self.m = Halving(clock, value[:m_half], value[m_half:].astype(bfloat), "ctx")

        def m0(self):
            self.m.start()

        def m1(self):
            self.m.wait()
            self.m.start()

        def m2(self):
            self.m.finish()

        def col(self):
            terms = run(
                column_grads, self.joined, self.x_all, text, self.grad_pairs, f_size
            )
            self.c = Halving(clock, *terms, "fsdp")

        def c0(self):
            self.c.start()

        def c1(self):
            self.c.wait()
            self.c.start()

        def c2(self):
            self.c.finish()

        def sp(self):
            (rows,) = run(split_columns, self.c.own, self.c.last, z_size)
            self.to_rows = Transposing(clock, [rows[q] for q in range(z_size)], "ctx")

        def cx0(self):
            self.to_rows.start()

        def cx1(self):
            self.to_rows.wait()
            self.to_rows.start()

        def cx2(self):
            self.to_rows.finish()

        def cc(self):
            self.c_far = [swap_at(part, "blk", 1) for part in self.to_rows.pieces]

        def cd(self):
            self.c_far = list(wait(*self.c_far))

        def pl(self):
            self.grad_attn_in, self.grad_cross_kv = run(
                place_columns, self.to_rows.pieces, self.c_far, wide, z_size
            )

        def fin(self):
            self.grad_latents, self.stat_last = run(
                finish, self.m.own, [self.m.last], x, self.modulation, self.grad_first
            )

        def st0(self):
            rows = [self.stat_last, self.stat_mid, self.stat_gate]
            self.stamp = Summing(clock, jnp.concatenate(rows, axis=0), ("blk", "ctx"))
            self.stamp.start()

        def st1(self):
            self.stamp.wait()
            self.stamp.start()

        def st3(self):
            self.stamp.finish()
            self.table = Summing(clock, self.stamp.value, ("fsdp",))
            self.table.start()

        def st4(self):
            self.table.finish()

    run_event = Events()
    for name in ORDER:
        getattr(run_event, name)()
    e = run_event

    grad_table = lax.dynamic_slice(e.table.value, (0, (f * group + g) * own), (6, own))
    square_sum = e.s.sum().reshape(3, own, D)
    up = e.u.sum().reshape(f_size, own, ff)
    back = [up[back_of(q, f_size)] for q in range(f_size)]
    steps = [jnp.where(b == 0, up[q], back[q]) for q in range(f_size)]
    grad_text = jnp.concatenate(reorder([e.grad_text, e.text_got], b), axis=0).T

    return (
        e.block_out[None],
        e.grad_latents[None],
        grad_text[None],
        e.stamp.value.reshape(1, 6 * D),
        grad_table,
        e.grad_attn_in,
        square_sum[0],
        square_sum[1],
        e.grad_cross_kv,
        square_sum[2],
        jnp.concatenate(reorder(steps, f), axis=1),
        e.d.sum(),
        grad_table[3],
    )


def solution(mesh):
    placed = (
        P("fsdp", ("ctx", "blk"), None),
        P("fsdp", None, None),
        P("fsdp", None),
        P(None, "fsdp"),
        P("fsdp", None),
        P("fsdp", None),
        P("fsdp", None),
        P("fsdp", None),
        P("fsdp", None),
        P("fsdp", None),
        P("fsdp", None),
        P("fsdp", ("ctx", "blk"), None),
    )
    owned = P(("fsdp", "ctx", "blk"), None)
    return jax.shard_map(
        shards,
        mesh=mesh,
        in_specs=placed,
        out_specs=(
            P("fsdp", ("ctx", "blk"), None),
            P("fsdp", ("ctx", "blk"), None),
            P("fsdp", None, None),
            P("fsdp", None),
            P(None, ("fsdp", "ctx", "blk")),
            owned,
            owned,
            owned,
            owned,
            owned,
            owned,
            owned,
            P(("fsdp", "ctx", "blk")),
        ),
        check_vma=False,
    )
```

```python
import functools

import jax
import jax.numpy as jnp
from jax import lax
from jax.experimental import pallas as pl
from jax.experimental.pallas import tpu as pltpu
from jax.sharding import PartitionSpec as P

D = 1152
HEADS = 16
HEAD = 72
TEXT = 120

epsilon = 1e-06
bfloat = jnp.bfloat16
single = jnp.float32
scaling = HEAD ** (-0.5)

VMEM = pl.BlockSpec(memory_space=pltpu.VMEM)
SMEM = pl.BlockSpec(memory_space=pltpu.SMEM)
ANY = pl.BlockSpec(memory_space=pl.ANY)
HBM = pl.BlockSpec(memory_space=pltpu.HBM)


def layer_norm(values):
    centred = values - jnp.mean(values, axis=-1, keepdims=True)
    variance = jnp.mean(centred * centred, axis=-1, keepdims=True)
    inverse = lax.rsqrt(variance + epsilon)
    return (centred * inverse, inverse)


def norm_back(grad_normed, normed, inverse):
    first_mean = jnp.mean(grad_normed, axis=-1, keepdims=True)
    second_mean = jnp.mean(grad_normed * normed, axis=-1, keepdims=True)
    return inverse * (grad_normed - first_mean - normed * second_mean)


def dot(left, right, axes=(1, 0)):
    return lax.dot_general(
        left, right, (((axes[0],), (axes[1],)), ((), ())), preferred_element_type=single
    )


def shape(dims, dtype=bfloat):
    return jax.ShapeDtypeStruct(tuple(dims), dtype)


def call(body, outs, args, specs, scratch=(), megabytes=40, micros=2):
    return pl.pallas_call(
        body,
        out_shape=tuple(outs),
        in_specs=list(specs),
        out_specs=tuple(VMEM for _ in outs),
        scratch_shapes=list(scratch),
        compiler_params=pltpu.CompilerParams(vmem_limit_bytes=megabytes * 2**20),
        cost_estimate=pl.CostEstimate(
            flops=int(micros * 1.15e9), bytes_accessed=1, transcendentals=0
        ),
    )(*args)


def swap(values, axis, step):
    size = lax.axis_size(axis)
    return lax.ppermute(values, axis, [(i, i ^ step) for i in range(size)])


def bits_of(size):
    return size.bit_length() - 1


def back_of(place, size):
    bits = bits_of(size)
    return sum(((place >> j) & 1) << (bits - 1 - j) for j in range(bits))


def step_of(place, core, size):
    return jnp.where(core == 0, place, back_of(place, size))


def cross(values, axis, stage):
    size = lax.axis_size(axis)
    pairs = []
    for i in range(size):
        for core in range(2):
            step = 1 << stage if core == 0 else 1 << (bits_of(size) - 1 - stage)
            pairs.append((2 * i + core, 2 * (i ^ step) + core))
    return lax.ppermute(values, (axis, "blk"), pairs)


class Clock:
    def __init__(self, ids):
        self.ids = ids
        self.token = ids

    def gate(self, values):
        return after(values, self.token)

    def wait(self, *values):
        out = lax.optimization_barrier(values + (self.token,))
        self.token = out[-1]
        return out[0] if len(values) == 1 else out[:-1]

    def run(self, kernel, *args, **named):
        outs = kernel(self.gate(self.ids), *args, **named)
        self.token = after(self.token, outs[0])
        return outs

    def swap(self, values, axis, step):
        return swap(self.gate(values), axis, step)


class Doubling:
    def __init__(self, clock, values, axis):
        self.clock, self.axis = clock, axis
        self.pieces = [values]
        self.arrays = []
        self.bits = bits_of(lax.axis_size(axis))
        self.stage = 0
        self.got = None

    def start(self):
        message = self.pieces[0][None] if self.stage == 0 else jnp.stack(self.pieces, 0)
        self.got = cross(self.clock.gate(message), self.axis, self.stage)
        self.stage += 1

    def wait(self):
        got = self.clock.wait(self.got)
        self.arrays.append(got)
        self.pieces += [got[i] for i in range(len(self.pieces))]

    def finish(self):
        self.wait()
        while self.stage < self.bits:
            self.start()
            self.wait()


class Transposing:
    def __init__(self, clock, chunks, axis):
        self.clock, self.axis = clock, axis
        self.pieces = list(chunks)
        self.bits = bits_of(lax.axis_size(axis))
        self.stage = 0
        self.found = {}

    def moved(self):
        return [q for q in range(len(self.pieces)) if (q >> (self.stage - 1)) & 1]

    def start(self):
        self.stage += 1
        message = jnp.stack([self.pieces[q] for q in self.moved()], 0)
        self.got = cross(self.clock.gate(message), self.axis, self.stage - 1)

    def wait(self):
        self.got = self.clock.wait(self.got)
        for i, q in enumerate(self.moved()):
            self.pieces[q] = self.got[i]
            self.found[q] = (self.got, i)

    def finish(self):
        self.wait()
        while self.stage < self.bits:
            self.start()
            self.wait()


class Direct:
    def __init__(self, clock, chunks, axis):
        self.clock, self.axis = clock, axis
        self.pieces = list(chunks)

    def start(self):
        size = lax.axis_size(self.axis)
        for q in range(1, size):
            pairs = []
            for i in range(size):
                pairs += [(2 * i, 2 * (i ^ q)), (2 * i + 1, 2 * (i ^ back_of(q, size)) + 1)]
            chunk = self.clock.gate(self.pieces[q])
            self.pieces[q] = lax.ppermute(chunk, (self.axis, "blk"), pairs)

    def finish(self):
        self.pieces[1:] = list(self.clock.wait(*self.pieces[1:]))


class Halving:
    def __init__(self, clock, keep, send, axis):
        self.clock, self.axis = clock, axis
        self.keep, self.send = keep, send
        self.stage = bits_of(lax.axis_size(axis)) - 1
        self.got = None

    def start(self):
        self.got = cross(self.clock.gate(self.send), self.axis, self.stage)
        self.stage -= 1

    def wait(self):
        got = self.clock.wait(self.got)
        if self.stage < 0:
            self.own, self.last = self.keep[0], got[0]
            return
        half = self.keep.shape[0] // 2
        self.send = (self.keep[half:] + got[half:].astype(single)).astype(bfloat)
        self.keep = self.keep[:half] + got[:half].astype(single)

    def finish(self):
        self.wait()
        while self.stage >= 0:
            self.start()
            self.wait()

    def sum(self):
        return self.own + self.last.astype(single)


class Exchange:
    def __init__(self, clock, near, far):
        self.clock, self.near = clock, near
        self.far = clock.swap(far, "blk", 1)

    def cross(self):
        self.far = self.clock.wait(self.far)
        both = [jnp.stack([self.near[q], self.far[q]], 0) for q in range(self.near.shape[0])]
        self.by_z = Transposing(self.clock, both, "ctx")
        self.by_z.start()

    def wait(self):
        self.by_z.wait()
        self.by_z.start()

    def finish(self):
        self.by_z.finish()
        self.pieces = self.by_z.pieces


def tree_sum(parts):
    while len(parts) > 1:
        parts = [parts[i] + parts[i + 1] for i in range(0, len(parts), 2)]
    return parts[0]


def reorder(parts, index):
    count = len(parts)
    bit = 1
    parts = list(parts)
    while bit < count:
        flag = (index & bit) != 0
        parts = [jnp.where(flag, parts[i ^ bit], parts[i]) for i in range(count)]
        bit *= 2
    return parts


def after(values, *earlier):
    return lax.optimization_barrier((values,) + earlier)[0]


def aligned(index, unit):
    return pl.multiple_of(index, unit)


def project_text(ids, own_part, parts, text, own_wide, kv_wide, f_size):
    rows, cols = own_part.shape
    count = f_size
    n_parts = len(parts)

    def body(*refs):
        ids_ref, text_ref = refs[0], refs[1]
        own_ref = refs[2]
        part_refs = refs[3 : 3 + n_parts]
        w_ref, kv_ref, pairs_ref, table_ref = refs[3 + n_parts : 7 + n_parts]
        full, sems = refs[7 + n_parts :]
        f, b = ids_ref[0], ids_ref[2]
        sources = [own_ref] + [ref.at[i] for ref in part_refs for i in range(ref.shape[0])]
        copies = []
        for q, source in enumerate(sources):
            place = pl.ds(aligned((f ^ step_of(q, b, count)) * rows, 16), rows)
            copies.append(pltpu.make_async_copy(source, full.at[place, :], sems.at[q]))
        for copy in copies:
            copy.start()
        for copy in copies:
            copy.wait()
        turned = full[...].T
        w_ref[...] = turned[:own_wide]
        kv = turned[own_wide : own_wide + kv_wide]
        kv_ref[...] = kv
        pairs_ref[...] = dot(kv, text_ref[...], (1, 1)).astype(bfloat)
        table_ref[...] = turned[own_wide + kv_wide :].astype(single)

    return call(
        body,
        [
            shape((own_wide, D)),
            shape((kv_wide, D)),
            shape((kv_wide, TEXT)),
            shape((cols - own_wide - kv_wide, D), single),
        ],
        [ids, text, own_part] + list(parts),
        [SMEM, VMEM] + [ANY] * (1 + n_parts),
        [pltpu.VMEM((count * rows, cols), bfloat), pltpu.SemaphoreType.DMA((count,))],
        megabytes=16,
        micros=2.6,
    )


def attend_forward(ids, w_t, modulation, x_parts, x_kinds, heads_here, z_size):
    tok = x_parts[0].shape[-2]
    count = 2 * z_size
    total = count * tok
    width = 256 if total % 256 == 0 else tok
    per = width // tok
    n_parts = len(x_parts)

    def body(*refs):
        ids_ref, w_ref, mod_ref = refs[:3]
        x_refs = refs[3 : 3 + n_parts]
        near_ref, far_ref, qkv_ref, norm_ref, x_all = refs[3 + n_parts : 8 + n_parts]
        raw, sems = refs[8 + n_parts :]
        b = ids_ref[2]
        copies = []
        for ref, chunks in zip(x_refs, x_kinds):
            for i, chunk in enumerate(chunks):
                source = ref if len(ref.shape) == 2 else ref.at[i]
                target = raw.at[pl.ds(chunk * tok, tok), :]
                copies.append(pltpu.make_async_copy(source, target, sems.at[chunk]))
        for copy in copies:
            copy.start()
        for copy in copies:
            copy.wait()

        def project(j, carry):
            place = pl.ds(aligned(j * width, width), width)
            normed, _ = layer_norm(raw[place, :].astype(single))
            modulated = (normed * (1.0 + mod_ref[1:2]) + mod_ref[0:1]).astype(bfloat)
            x_all[place, :] = modulated
            got = dot(w_ref[...], modulated, (1, 1))
            for i in range(3 * heads_here):
                qkv_ref[i, :, place] = got[i * HEAD : (i + 1) * HEAD].astype(bfloat)
            return carry

        lax.fori_loop(0, total // width, project, 0)

        def attend(h, carry):
            keys = qkv_ref[heads_here + h]
            values = qkv_ref[2 * heads_here + h]
            for core, target in ((0, near_ref), (1, far_ref)):

                def block(j, carry, core=core, target=target):
                    at = core * z_size * tok + j * width
                    place = pl.ds(aligned(at, width), width)
                    scores = dot(keys, qkv_ref[h, :, place], (0, 0)) * scaling
                    top = jnp.max(scores, axis=0, keepdims=True)
                    exponent = jnp.exp(scores - top)
                    summed = jnp.sum(exponent, axis=0, keepdims=True)
                    weights = (exponent * (1.0 / summed)).astype(bfloat)
                    mixed = dot(values, weights).astype(bfloat)
                    norm_ref[h, :, place] = top + jnp.log(summed)
                    for i in range(per):
                        piece = mixed[:, i * tok : (i + 1) * tok]
                        target[j * per + i, h] = piece
                    return carry

                lax.fori_loop(0, z_size * tok // width, block, 0)
            return carry

        lax.fori_loop(0, heads_here, attend, 0)

    wide = heads_here * HEAD
    return call(
        body,
        [
            shape((z_size, heads_here, HEAD, tok)),
            shape((z_size, heads_here, HEAD, tok)),
            shape((3 * heads_here, HEAD, total)),
            shape((heads_here, 1, total), single),
            shape((total, D)),
        ],
        [ids, w_t, modulation] + list(x_parts),
        [SMEM, VMEM, VMEM] + [ANY] * n_parts,
        [pltpu.VMEM((total, D), bfloat), pltpu.SemaphoreType.DMA((count,))],
        megabytes=24,
        micros=1.5,
    )


def weight_copies(piece_refs, kinds, full, sems, f, b, rows):
    copies = []
    half = rows // 2
    for i, (ref, kind) in enumerate(zip(piece_refs, kinds)):
        sem = sems.at[i]
        if kind[0] == "whole":
            copies.append(pltpu.make_async_copy(ref, full, sem))
        elif kind[0] == "own":
            place = pl.ds(aligned(f * rows, 16), rows)
            copies.append(pltpu.make_async_copy(ref, full.at[kind[1], place, :], sem))
        else:
            core = b if kind[0] == "near" else 1 - b
            source = f ^ kind[2](core)
            place = pl.ds(aligned(source * rows + core * half, 16), half)
            target = full.at[:, place, :]
            ref = ref if kind[1] is None else ref.at[kind[1]]
            copies.append(pltpu.make_async_copy(ref, target, sem))
    return copies


def piece_specs(kinds):
    return [HBM if kind[0] == "own" else ANY for kind in kinds]


def permute_rows(source, target, count, piece):
    for k in range(count):
        for core in range(2):
            target[core, pl.ds(k * piece, piece), :] = source[
                pl.ds((2 * k + core) * piece, piece), :
            ]


def token_forward(ids, got, x, modulation, pair_parts, pieces, kinds, f_size, z_size):
    tok = x.shape[0]
    heads_here = got[0].shape[1]
    rows = D // f_size
    own = D // (2 * f_size * z_size)
    kv_wide = D // z_size
    n_got, n_pieces, n_pairs = len(got), len(pieces), len(pair_parts)

    def body(*refs):
        ids_ref, x_ref, mod_ref = refs[:3]
        got_refs = refs[3 : 3 + n_got]
        pair_refs = refs[3 + n_got : 3 + n_got + n_pairs]
        at = 3 + n_got + n_pairs
        piece_refs = refs[at : at + n_pieces]
        rest = refs[at + n_pieces :]
        x_two_ref, second_ref, branch_ref, p_ref, cq_ref, keep_ref, send_ref, pairs_ref = rest[:8]
        full, mixed, pair_s, turned, left, sems = rest[8:]
        f, z, b = ids_ref[0], ids_ref[1], ids_ref[2]
        copies = weight_copies(piece_refs, kinds, full, sems, f, b, rows)
        for copy in copies:
            copy.start()

        for q in range(z_size):
            for core in range(2):
                g = 2 * (z ^ step_of(q, b, z_size)) + (b ^ core)
                for h in range(heads_here):
                    place = pl.ds(aligned((g * heads_here + h) * HEAD, 8), HEAD)
                    mixed[place, :] = got_refs[q][core, h].astype(single)
        for core in range(2):
            q = 0
            for ref in pair_refs[core * (n_pairs // 2) : (core + 1) * (n_pairs // 2)]:
                for source in [ref] if len(ref.shape) == 2 else [ref.at[i] for i in range(ref.shape[0])]:
                    g = 2 * (z ^ step_of(q, b ^ core, z_size)) + (b ^ core)
                    place = pl.ds(aligned(g * kv_wide, 8), kv_wide)
                    pair_s[place, :] = source[...].astype(single)
                    q += 1
        pairs_ref[...] = pair_s[...]

        def keep_left(i, source):
            permute_rows(source, left, f_size * z_size, own)
            keep_ref[i] = left[b].astype(bfloat)
            send_ref[i] = left[1 - b].astype(bfloat)

        keep_left(0, mixed)
        shift_two, scale_two, gate_one = mod_ref[3:4], mod_ref[4:5], mod_ref[2:3]
        for copy in copies:
            copy.wait()
        branch = dot(mixed[...].T.astype(bfloat), full[0])
        branch_ref[...] = branch
        first = x_ref[...].astype(single) + gate_one * branch
        first_low = first.astype(bfloat)
        turned[...] = first_low.astype(single).T
        keep_left(1, turned)
        turned[...] = dot(first_low, full[1]).T
        cq_ref[...] = turned[...].astype(bfloat)
        def attend(h, carry):
            rows_h = pl.ds(aligned(h * HEAD, 8), HEAD)
            keys = pair_s[rows_h, :].astype(bfloat)
            values = pair_s[pl.ds(aligned(D + h * HEAD, 8), HEAD), :].astype(bfloat)
            scores = dot(keys, turned[rows_h, :].astype(bfloat), (0, 0)) * scaling
            top = jnp.max(scores, axis=0, keepdims=True)
            exponent = jnp.exp(scores - top)
            weights = exponent * (1.0 / jnp.sum(exponent, axis=0, keepdims=True))
            p_ref[h] = weights
            mixed[rows_h, :] = dot(values, weights.astype(bfloat)).astype(bfloat).astype(single)
            return carry

        lax.fori_loop(0, HEADS, attend, 0, unroll=4)
        second = first + dot(mixed[...].T.astype(bfloat), full[2])
        second_ref[...] = second
        normed, _ = layer_norm(second)
        x_two_ref[...] = (normed * (1.0 + scale_two) + shift_two).astype(bfloat)
        keep_left(2, mixed)

    return call(
        body,
        [
            shape((tok, D)),
            shape((tok, D), single),
            shape((tok, D), single),
            shape((HEADS, TEXT, tok), single),
            shape((D, tok)),
            shape((3, D // 2, tok)),
            shape((3, D // 2, tok)),
            shape((2 * D, TEXT), single),
        ],
        [ids, x, modulation] + list(got) + list(pair_parts) + list(pieces),
        [SMEM] + [VMEM] * (2 + n_got + n_pairs) + piece_specs(kinds),
        [
            pltpu.VMEM((3, D, D), bfloat),
            pltpu.VMEM((D, tok), single),
            pltpu.VMEM((2 * D, TEXT), single),
            pltpu.VMEM((D, tok), single),
            pltpu.VMEM((2, D // 2, tok), single),
            pltpu.SemaphoreType.DMA((n_pieces,)),
        ],
        megabytes=28,
        micros=7.0,
    )


def feed_forward(ids, x_parts, grad_hidden, pieces, kinds, ff, f_size):
    count = f_size
    n_parts = len(x_parts)
    tok = x_parts[0].shape[0]
    tile = 384 if ff % 384 == 0 else ff
    rows = D // f_size
    n_pieces = len(pieces)

    def body(*refs):
        ids_ref = refs[0]
        x_refs = refs[1 : 1 + n_parts]
        gh_ref = refs[1 + n_parts]
        piece_refs = refs[2 + n_parts : 2 + n_parts + n_pieces]
        rest = refs[2 + n_parts + n_pieces :]
        hidden_ref, pre_ref, keep_ref, send_ref = rest[:4]
        x_all, full, sems = rest[4:]
        up_ref = full.at[0]
        copies = weight_copies(piece_refs, kinds, full, sems, ids_ref[0], ids_ref[2], rows)
        for copy in copies:
            copy.start()
        x_all[0:tok, :] = x_refs[0][...]
        at = tok
        for ref in x_refs[1:]:
            for i in range(ref.shape[0]):
                x_all[at : at + tok, :] = ref[i]
                at += tok
        for copy in copies:
            copy.wait()

        def step(j, carry):
            place = pl.ds(aligned(j * tile, 128), tile) if ff > tile else pl.ds(0, tile)
            u = dot(x_all[...], up_ref[:, place])
            square = u * u
            t = jnp.tanh(0.7978845608028654 * u * (1.0 + 0.044715 * square))
            half = 0.5 * (1.0 + t)
            hidden_ref[:, place] = (u * half).astype(bfloat)
            slope = half + 0.5 * u * (1.0 - t * t) * (
                0.7978845608028654 * (1.0 + 0.134145 * square)
            )
            pre_ref[:, place] = (gh_ref[:, place] * slope).astype(bfloat)
            return carry

        if ff > tile:
            lax.fori_loop(0, ff // tile, step, 0)
        else:
            step(0, 0)
        part = dot(pre_ref[...], up_ref[...], (1, 1))
        for i in range(count):
            piece = part[i * tok : (i + 1) * tok]
            if i < count // 2:
                keep_ref[i] = piece
            else:
                send_ref[i - count // 2] = piece.astype(bfloat)

    total = count * tok
    return call(
        body,
        [
            shape((total, ff)),
            shape((total, ff)),
            shape((count // 2, tok, D), single),
            shape((count // 2, tok, D)),
        ],
        [ids] + list(x_parts) + [grad_hidden] + list(pieces),
        [SMEM] + [VMEM] * (n_parts + 1) + piece_specs(kinds),
        [
            pltpu.VMEM((total, D), bfloat),
            pltpu.VMEM((1, D, ff), bfloat),
            pltpu.SemaphoreType.DMA((n_pieces,)),
        ],
        megabytes=24,
        micros=7.0,
    )


def feed_forward_turn(ids, x_parts, hidden, f_size, z_size):
    n_parts = len(x_parts)
    tok = x_parts[0].shape[0]
    total, ff = hidden.shape
    own = D // (2 * f_size * z_size)
    own_down = ff // (2 * z_size)

    def body(*refs):
        ids_ref, hidden_ref = refs[:2]
        x_refs = refs[2 : 2 + n_parts]
        hk_ref, hs_ref, xk_ref, xs_ref, flat, halves, flat_down, halves_down = refs[2 + n_parts :]
        b = ids_ref[2]
        flat_down[...] = hidden_ref[...].T.astype(single)
        permute_rows(flat_down, halves_down, z_size, own_down)
        hk_ref[...] = halves_down[b].astype(bfloat)
        hs_ref[...] = halves_down[1 - b].astype(bfloat)
        flat[:, 0:tok] = x_refs[0][...].T.astype(single)
        at = tok
        for ref in x_refs[1:]:
            for i in range(ref.shape[0]):
                flat[:, at : at + tok] = ref[i].T.astype(single)
                at += tok
        permute_rows(flat, halves, f_size * z_size, own)
        xk_ref[...] = halves[b].astype(bfloat)
        xs_ref[...] = halves[1 - b].astype(bfloat)

    return call(
        body,
        [shape((ff // 2, total))] * 2 + [shape((D // 2, total))] * 2,
        [ids, hidden] + list(x_parts),
        [SMEM] + [VMEM] * (1 + n_parts),
        [
            pltpu.VMEM((D, total), single),
            pltpu.VMEM((2, D // 2, total), single),
            pltpu.VMEM((ff, total), single),
            pltpu.VMEM((2, ff // 2, total), single),
        ],
        megabytes=20,
        micros=0.1,
    )


def feed_forward_out(ids, hidden, down, count):
    total = hidden.shape[0]
    tok = total // count

    def body(_, hidden_ref, down_ref, keep_ref, send_ref):
        part = dot(hidden_ref[...], down_ref[...])
        for i in range(count):
            piece = part[i * tok : (i + 1) * tok]
            if i < count // 2:
                keep_ref[i] = piece
            else:
                send_ref[i - count // 2] = piece.astype(bfloat)

    return call(
        body,
        [shape((count // 2, tok, D), single), shape((count // 2, tok, D))],
        [ids, hidden, down],
        [SMEM, VMEM, VMEM],
        megabytes=12,
        micros=0.1,
    )


def chip_grads(ids, index, left, left_far, right, right_far, count, direct):
    rows, tok = left.shape
    cols = right.shape[1]
    part = rows // count
    held = 1 if direct else count // 2

    def body(*refs):
        ids_ref, left_ref, lf_ref, right_ref, rf_ref, keep_ref, send_ref = refs[:7]
        left_s, right_s, flat = refs[7:]
        i, b = ids_ref[index], ids_ref[2]
        left_s[:, 0:tok] = left_ref[...]
        left_s[:, tok : 2 * tok] = lf_ref[...]
        right_s[0:tok, :] = right_ref[...]
        right_s[tok : 2 * tok, :] = rf_ref[...]
        value = dot(left_s[...], right_s[...])
        for k in range(count):
            flat[k] = value[k * part : (k + 1) * part]
        for q in range(count):
            piece = flat[i ^ step_of(q, b, count)]
            if q < held:
                keep_ref[q] = piece
            else:
                send_ref[q - held] = piece.astype(bfloat)

    return call(
        body,
        [shape((held, part, cols), single), shape((count - held, part, cols))],
        [ids, left, left_far, right, right_far],
        [SMEM] + [VMEM] * 4,
        [
            pltpu.VMEM((rows, 2 * tok), bfloat),
            pltpu.VMEM((2 * tok, cols), bfloat),
            pltpu.VMEM((count, part, cols), single),
        ],
        megabytes=24,
        micros=0.1,
    )


def token_backward(
    ids, own, got, second, branch, cotangent, modulation, p, cq, pairs, pieces, kinds, f_size, z_size
):
    tok = second.shape[0]
    heads_here = HEADS // (2 * z_size)
    rows = D // f_size
    kv_wide = D // z_size
    n_got, n_pieces = len(got), len(pieces)

    def body(*refs):
        ids_ref, own_ref, second_ref, branch_ref, cot_ref, mod_ref, p_ref, cq_ref, pairs_ref = refs[:9]
        got_refs = refs[9 : 9 + n_got]
        piece_refs = refs[9 + n_got : 9 + n_got + n_pieces]
        rest = refs[9 + n_got + n_pieces :]
        near_ref, far_ref, right_ref, first_ref, stat_ref, pair_keep, pair_send = rest[:7]
        full, turned, grads, low, sems = rest[7:]
        pair_s = pairs_ref
        f, z, b = ids_ref[0], ids_ref[1], ids_ref[2]
        copies = weight_copies(piece_refs, kinds, full, sems, f, b, rows)
        for copy in copies:
            copy.start()
        gate_one, scale_two = mod_ref[2:3], mod_ref[4:5]
        grad_mod = own_ref[...]
        for ref in got_refs:
            grad_mod = grad_mod + ref[...].astype(single)
        normed, inverse = layer_norm(second_ref[...])
        stat_ref[1:2] = jnp.sum(grad_mod, axis=0, keepdims=True)
        stat_ref[2:3] = jnp.sum(grad_mod * normed, axis=0, keepdims=True)
        grad_second = cot_ref[...].astype(single) + norm_back(
            grad_mod * (1.0 + scale_two), normed, inverse
        )
        grad_low = grad_second.astype(bfloat)
        right_ref[2] = grad_low
        for copy in copies:
            copy.wait()
        turned[...] = dot(full[2], grad_low, (1, 1))
        low[...] = cq_ref[...].astype(single)
        def attend(h, carry):
            rows_h = pl.ds(aligned(h * HEAD, 8), HEAD)
            rows_v = pl.ds(aligned(D + h * HEAD, 8), HEAD)
            keys = pair_s[rows_h, :].astype(bfloat)
            values = pair_s[rows_v, :].astype(bfloat)
            grad_h = turned[rows_h, :].astype(bfloat)
            weights = p_ref[h]
            grad_weights = dot(values, grad_h, (0, 0))
            grads[rows_v, :] = dot(grad_h, weights.astype(bfloat), (1, 1))
            inner = jnp.sum(weights * grad_weights, axis=0, keepdims=True)
            grad_scores = (weights * (grad_weights - inner)).astype(bfloat)
            turned[rows_h, :] = scaling * dot(keys, grad_scores)
            grads[rows_h, :] = scaling * dot(low[rows_h, :].astype(bfloat), grad_scores, (1, 1))
            return carry

        lax.fori_loop(0, HEADS, attend, 0, unroll=4)
        for q in range(z_size):
            here = 2 * (z ^ step_of(q, b, z_size)) + b
            there = 2 * (z ^ step_of(q, 1 - b, z_size)) + 1 - b
            pair_keep[q] = grads[pl.ds(aligned(here * kv_wide, 8), kv_wide), :]
            place = pl.ds(aligned(there * kv_wide, 8), kv_wide)
            pair_send[q] = grads[place, :].astype(bfloat)
        grad_query = turned[...].T.astype(bfloat)
        right_ref[1] = grad_query
        grad_first = grad_second + dot(grad_query, full[1], (1, 1))
        first_ref[...] = grad_first
        stat_ref[0:1] = jnp.sum(grad_first * branch_ref[...], axis=0, keepdims=True)
        grad_branch = (gate_one * grad_first).astype(bfloat)
        right_ref[0] = grad_branch
        turned[...] = dot(full[0], grad_branch, (1, 1))
        for q in range(z_size):
            for core in range(2):
                target = near_ref if core == 0 else far_ref
                g = 2 * (z ^ step_of(q, b ^ core, z_size)) + (b ^ core)
                for h in range(heads_here):
                    place = pl.ds(aligned((g * heads_here + h) * HEAD, 8), HEAD)
                    target[q, h] = turned[place, :].astype(bfloat)

    return call(
        body,
        [
            shape((z_size, heads_here, HEAD, tok)),
            shape((z_size, heads_here, HEAD, tok)),
            shape((3, tok, D)),
            shape((tok, D), single),
            shape((3, D), single),
            shape((z_size, kv_wide, TEXT), single),
            shape((z_size, kv_wide, TEXT)),
        ],
        [ids, own, second, branch, cotangent, modulation, p, cq, pairs] + list(got) + list(pieces),
        [SMEM] + [VMEM] * (8 + n_got) + piece_specs(kinds),
        [
            pltpu.VMEM((3, D, D), bfloat),
            pltpu.VMEM((D, tok), single),
            pltpu.VMEM((2 * D, TEXT), single),
            pltpu.VMEM((D, tok), single),
            pltpu.SemaphoreType.DMA((n_pieces,)),
        ],
        megabytes=28,
        micros=0.1,
    )


def square_grads(ids, left, left_far, right, right_far, f_size):
    count, half, tok = left.shape
    part = half // f_size

    def body(*refs):
        ids_ref, left_ref, lf_ref, right_ref, rf_ref, keep_ref, send_ref = refs[:7]
        left_s, right_s, flat = refs[7:]
        f, b = ids_ref[0], ids_ref[2]
        for i in range(count):
            left_s[:, 0:tok] = left_ref[i]
            left_s[:, tok : 2 * tok] = lf_ref[i]
            right_s[0:tok, :] = right_ref[i]
            right_s[tok : 2 * tok, :] = rf_ref[i]
            value = dot(left_s[...], right_s[...])
            for k in range(f_size):
                flat[k] = value[k * part : (k + 1) * part]
            for q in range(f_size):
                value = flat[f ^ step_of(q, b, f_size)]
                if q < f_size // 2:
                    keep_ref[q, i] = value
                else:
                    send_ref[q - f_size // 2, i] = value.astype(bfloat)

    return call(
        body,
        [
            shape((f_size // 2, count, part, D), single),
            shape((f_size // 2, count, part, D)),
        ],
        [ids, left, left_far, right, right_far],
        [SMEM] + [VMEM] * 4,
        [
            pltpu.VMEM((half, 2 * tok), bfloat),
            pltpu.VMEM((2 * tok, D), bfloat),
            pltpu.VMEM((f_size, part, D), single),
        ],
        megabytes=20,
        micros=0.1,
    )


def sum_split(ids, index, own, got, count, add):
    lead, rows, cols = own.shape
    part = rows // count
    n_got = len(got)
    groups = lead if add else lead * (1 + n_got)

    def body(*refs):
        ids_ref, own_ref = refs[:2]
        got_refs = refs[2 : 2 + n_got]
        keep_ref, send_ref, flat, chunks = refs[2 + n_got :]
        i, b = ids_ref[index], ids_ref[2]

        for k in range(lead):
            if add:
                value = own_ref[k]
                for ref in got_refs:
                    value = value + ref[k].astype(single)
                flat[k] = value
            else:
                flat[k] = own_ref[k]
                for j, ref in enumerate(got_refs):
                    flat[(j + 1) * lead + k] = ref[k].astype(single)
        for k in range(groups):
            for c in range(count):
                chunks[c, pl.ds(k * part, part), :] = flat[k, pl.ds(c * part, part), :]
        for q in range(count):
            value = chunks[i ^ step_of(q, b, count)]
            if q < count // 2:
                keep_ref[q] = value
            else:
                send_ref[q - count // 2] = value.astype(bfloat)

    return call(
        body,
        [
            shape((count // 2, groups * part, cols), single),
            shape((count // 2, groups * part, cols)),
        ],
        [ids, own] + list(got),
        [SMEM] + [VMEM] * (1 + n_got),
        [
            pltpu.VMEM((groups, rows, cols), single),
            pltpu.VMEM((count, groups * part, cols), single),
        ],
        megabytes=24,
        micros=0.1,
    )


def attend_backward(ids, h, qkv, norm, got, z_size):
    heads_here, _, tok = got[0].shape[1:]
    count = 2 * z_size
    total = count * tok
    width = 256 if total % 256 == 0 else tok
    n_got = len(got)

    def body(*refs):
        _, qkv_ref, norm_ref = refs[:3]
        got_refs = refs[3 : 3 + n_got]
        out_ref, grad, flat_k, flat_v = refs[3 + n_got :]
        for core in range(2):
            for q in range(z_size):
                at = (core * z_size + q) * tok
                place = q if core == 0 else back_of(q, z_size)
                grad[:, at : at + tok] = got_refs[place][core, h]
        flat_k[...] = jnp.zeros_like(flat_k)
        flat_v[...] = jnp.zeros_like(flat_v)
        keys = qkv_ref[heads_here + h]
        values = qkv_ref[2 * heads_here + h]

        def block(j, carry):
            place = pl.ds(aligned(j * width, width), width)
            query = qkv_ref[h, :, place]
            grad_h = grad[:, place]
            scores = dot(keys, query, (0, 0)) * scaling
            weights = jnp.exp(scores - norm_ref[h, :, place])
            grad_weights = dot(values, grad_h, (0, 0))
            inner = jnp.sum(weights * grad_weights, axis=0, keepdims=True)
            grad_scores = (weights * (grad_weights - inner)).astype(bfloat)
            flat_v[...] += dot(grad_h, weights.astype(bfloat), (1, 1))
            out_ref[0, :, place] = (scaling * dot(keys, grad_scores)).astype(bfloat)
            flat_k[...] += scaling * dot(query, grad_scores, (1, 1))
            return carry

        lax.fori_loop(0, total // width, block, 0)
        out_ref[1] = flat_k[...].astype(bfloat)
        out_ref[2] = flat_v[...].astype(bfloat)

    return call(
        body,
        [shape((3, HEAD, total))],
        [ids, qkv, norm] + list(got),
        [SMEM] + [VMEM] * (2 + n_got),
        [
            pltpu.VMEM((HEAD, total), bfloat),
            pltpu.VMEM((HEAD, total), single),
            pltpu.VMEM((HEAD, total), single),
        ],
        megabytes=20,
        micros=0.1,
    )


def attend_project(ids, grads, w_t, z_size):
    heads_here = len(grads)
    total = grads[0].shape[-1]
    tok = total // (2 * z_size)
    wide3 = 3 * heads_here * HEAD
    width = z_size * tok

    def body(*refs):
        w_ref = refs[1]
        grad_refs = refs[2 : 2 + heads_here]
        close_ref, away_ref, low, flat = refs[2 + heads_here :]
        for h in range(heads_here):
            for i in range(3):
                place = pl.ds((i * heads_here + h) * HEAD, HEAD)
                flat[place, :] = grad_refs[h][i].astype(single)
        low[...] = flat[...].astype(bfloat)
        for core in (1, 0):
            part = dot(low[:, core * width : (core + 1) * width], w_ref[...], (0, 0))
            for q in range(z_size):
                piece = part[q * tok : (q + 1) * tok]
                if core == 0:
                    close_ref[q] = piece
                else:
                    away_ref[q] = piece.astype(bfloat)

    return call(
        body,
        [
            shape((z_size, tok, D), single),
            shape((z_size, tok, D)),
            shape((wide3, total)),
        ],
        [ids, w_t] + list(grads),
        [SMEM] + [VMEM] * (1 + heads_here),
        [pltpu.VMEM((wide3, total), single)],
        megabytes=24,
        micros=0.1,
    )


def text_grads(ids, own, got, kv_t):
    def body(ids_ref, own_ref, got_ref, kv_ref, pairs_ref, keep_ref, send_ref, flat):
        b = ids_ref[2]
        pairs = (own_ref[...] + got_ref[...].astype(single)).astype(bfloat)
        pairs_ref[...] = pairs
        part = dot(kv_ref[...], pairs, (0, 0))
        flat[0] = part[: D // 2]
        flat[1] = part[D // 2 :]
        keep_ref[...] = flat[b]
        send_ref[...] = flat[1 - b]

    return call(
        body,
        [
            shape(own.shape),
            shape((D // 2, TEXT), single),
            shape((D // 2, TEXT), single),
        ],
        [ids, own, got, kv_t],
        [SMEM] + [VMEM] * 3,
        [pltpu.VMEM((2, D // 2, TEXT), single)],
        megabytes=16,
        micros=0.1,
    )


def split_columns(ids, own, got, z_size):
    rows, cols = own.shape
    part = rows // z_size

    def body(ids_ref, own_ref, got_ref, out_ref, chunks):
        z, b = ids_ref[1], ids_ref[2]
        value = own_ref[...] + got_ref[...].astype(single)
        for k in range(z_size):
            chunks[k] = value[k * part : (k + 1) * part]
        for q in range(z_size):
            out_ref[q] = chunks[z ^ step_of(q, b, z_size)].astype(bfloat)

    return call(
        body,
        [shape((z_size, part, cols))],
        [ids, own, got],
        [SMEM] + [VMEM] * 2,
        [pltpu.VMEM((z_size, part, cols), single)],
        megabytes=16,
        micros=0.1,
    )


def place_columns(ids, near, far, wide, z_size):
    part, cols = near[0].shape[0] // 2, near[0].shape[1]
    kv_wide = cols - 3 * wide

    def body(*refs):
        ids_ref = refs[0]
        in_ref, kv_ref, blocks, pair = refs[1 + 2 * z_size :]
        z, b = ids_ref[1], ids_ref[2]
        for core in range(2):
            for q in range(z_size):
                both = refs[1 + core * z_size + q][...].astype(single)
                pair[0] = both[:part]
                pair[1] = both[part:]
                blocks[z ^ step_of(q, b ^ core, z_size), b ^ core] = pair[b]
        for k in range(z_size):
            for core in range(2):
                g = 2 * k + core
                block = blocks[k, core]
                for i in range(3):
                    at = i * D + g * wide
                    in_ref[:, at : at + wide] = block[:, i * wide : (i + 1) * wide]
                kv_ref[:, g * kv_wide : (g + 1) * kv_wide] = block[:, 3 * wide :]

    return call(
        body,
        [shape((part, 3 * D), single), shape((part, 2 * D), single)],
        [ids] + list(near) + list(far),
        [SMEM] + [VMEM] * (2 * z_size),
        [pltpu.VMEM((z_size, 2, part, cols), single), pltpu.VMEM((2, part, cols), single)],
        megabytes=16,
        micros=0.1,
    )


def column_grads(ids, joined, x_all, text, grad_pairs, f_size):
    wide3 = joined.shape[0]
    kv_wide = grad_pairs.shape[0]
    rows = D // f_size
    cols = wide3 + kv_wide

    def body(ids_ref, joined_ref, x_ref, text_ref, pairs_ref, keep_ref, send_ref, turned, kv_s):
        f, b = ids_ref[0], ids_ref[2]
        turned[...] = dot(joined_ref[...], x_ref[...]).T
        kv_s[...] = dot(text_ref[...], pairs_ref[...], (0, 1))
        held = f_size // 2
        for q in range(f_size):
            place = pl.ds(aligned((f ^ step_of(q, b, f_size)) * rows, 8), rows)
            if q < held:
                keep_ref[q, :, 0:wide3] = turned[place, :]
                keep_ref[q, :, wide3:cols] = kv_s[place, :]
            else:
                send_ref[q - held, :, 0:wide3] = turned[place, :].astype(bfloat)
                send_ref[q - held, :, wide3:cols] = kv_s[place, :].astype(bfloat)

    return call(
        body,
        [
            shape((f_size // 2, rows, cols), single),
            shape((f_size // 2, rows, cols)),
        ],
        [ids, joined, x_all, text, grad_pairs],
        [SMEM] + [VMEM] * 4,
        [pltpu.VMEM((D, wide3), single), pltpu.VMEM((D, kv_wide), single)],
        megabytes=24,
        micros=1.5,
    )


def finish(ids, own, got, x, modulation, grad_first):
    tok = x.shape[0]
    n_got = len(got)

    def body(*refs):
        _, own_ref, x_ref, mod_ref, first_ref = refs[:5]
        got_refs = refs[5 : 5 + n_got]
        out_ref, stat_ref = refs[5 + n_got :]
        grad_mod = own_ref[...]
        for ref in got_refs:
            grad_mod = grad_mod + ref[...].astype(single)
        normed, inverse = layer_norm(x_ref[...].astype(single))
        stat_ref[0:1] = jnp.sum(grad_mod, axis=0, keepdims=True)
        stat_ref[1:2] = jnp.sum(grad_mod * normed, axis=0, keepdims=True)
        out_ref[...] = first_ref[...] + norm_back(grad_mod * (1.0 + mod_ref[1:2]), normed, inverse)

    return call(
        body,
        [shape((tok, D), single), shape((2, D), single)],
        [ids, own, x, modulation, grad_first] + list(got),
        [SMEM] + [VMEM] * (4 + n_got),
        micros=0.1,
    )


class Summing:
    def __init__(self, clock, value, axes):
        self.clock, self.value = clock, value
        self.axes = list(axes)

    def start(self):
        axis = self.axes.pop(0)
        size = lax.axis_size(axis)
        self.got = [self.clock.swap(self.value, axis, step) for step in range(1, size)]

    def wait(self):
        parts = self.clock.wait(self.value, *self.got)
        self.value = tree_sum(list(parts))

    def finish(self):
        self.wait()
        while self.axes:
            self.start()
            self.wait()


def shards(
    latents,
    text_embed,
    timestep,
    ada_table,
    w_attn_in,
    w_attn_out,
    w_cross_q,
    w_cross_kv,
    w_cross_out,
    w_mlp_up,
    w_mlp_down,
    grad_out,
):
    f_size = lax.axis_size("fsdp")
    z_size = lax.axis_size("ctx")
    group = 2 * z_size
    f = lax.axis_index("fsdp")
    z = lax.axis_index("ctx")
    b = lax.axis_index("blk")
    g = 2 * z + b
    ids = jnp.stack([f, z, b]).astype(jnp.int32)
    heads_here = HEADS // group
    wide = heads_here * HEAD
    kv_wide = 2 * D // group
    rows_f = D // f_size
    half_f = rows_f // 2
    own = D // (f_size * group)
    ff = w_mlp_up.shape[1] // f_size
    m_half = z_size // 2

    x = latents[0]
    cotangent = grad_out[0]
    text = text_embed[0]
    squares = [w_attn_out, w_cross_q, w_cross_out]
    clock = Clock(ids)
    run, swap_at, wait = clock.run, clock.swap, clock.wait

    def assemble(pieces, kinds):
        if half_f % 16 == 0:
            return pieces, kinds
        count = sum(kind[0] == "own" for kind in kinds)
        whole = jnp.zeros((count, f_size, rows_f, pieces[0].shape[-1]), bfloat)
        for part, kind in zip(pieces, kinds):
            if kind[0] == "own":
                whole = lax.dynamic_update_slice(whole, part[None, None], (kind[1], f, 0, 0))
            else:
                core = b if kind[0] == "near" else 1 - b
                part = part if kind[1] is None else part[kind[1]]
                whole = lax.dynamic_update_slice(
                    whole, part[:, None], (0, f ^ kind[2](core), core * half_f, 0)
                )
        return [whole.reshape(count, D, -1)], [("whole",)]

    class Events:
        def x0(self):
            self.x_z = Doubling(clock, x, "ctx")
            self.x_z.start()

        def x1(self):
            self.x_z.wait()
            self.x_z.start()

        def xc(self):
            self.x_far = [swap_at(part, "blk", 1) for part in (x, self.x_z.arrays[0])]

        def x2(self):
            self.x_z.finish()

        def xd0(self):
            self.x_far += [swap_at(part, "blk", 1) for part in self.x_z.arrays[1:]]

        def xd(self):
            *self.x_far, self.w_far[0] = wait(*self.x_far, self.w_far[0])

        def in0(self):
            self.own_in = jnp.concatenate(
                [
                    lax.dynamic_slice(w_attn_in, (0, i * D + g * wide), (rows_f, wide))
                    for i in range(3)
                ]
                + [lax.dynamic_slice(w_cross_kv, (0, g * kv_wide), (rows_f, kv_wide)), ada_table.T],
                axis=1,
            )
            self.in_f = Doubling(clock, self.own_in, "fsdp")
            self.in_f.start()

        def in1(self):
            self.in_f.wait()
            self.in_f.start()

        def in2(self):
            self.in_f.finish()

        def proj(self):
            self.w_t, self.kv_t, self.pairs_here, table = run(
                project_text, self.own_in, self.in_f.arrays, text, 3 * wide, kv_wide, f_size
            )
            self.modulation = table + timestep.reshape(6, D)

        def pz0(self):
            self.pair_z = Doubling(clock, self.pairs_here, "ctx")
            self.pair_z.start()

        def pz1(self):
            self.pair_z.wait()
            self.pair_z.start()

        def pc(self):
            self.pair_far = [
                swap_at(part, "blk", 1) for part in [self.pairs_here] + self.pair_z.arrays[:1]
            ]

        def pz2(self):
            self.pair_z.finish()
            self.pair_far += [swap_at(part, "blk", 1) for part in self.pair_z.arrays[1:]]

        def pd(self):
            self.pair_far = list(wait(*self.pair_far))

        def w0(self):
            half = jnp.stack(
                [lax.dynamic_slice(w, (b * half_f, 0), (half_f, D)) for w in squares], 0
            )
            self.w_f = Doubling(clock, half, "fsdp")
            self.w_f.start()

        def w1(self):
            self.w_f.wait()
            self.w_f.start()
            self.w_far = [swap_at(part, "blk", 1) for part in self.w_f.arrays]

        def w2(self):
            self.w_f.finish()
            self.w_far += [swap_at(part, "blk", 1) for part in self.w_f.arrays[1:]]

        def wd(self):
            self.w_far = self.w_far[:1] + list(wait(*self.w_far[1:], self.mixed[0])[:-1])
            pieces, kinds = list(squares), [("own", i) for i in range(3)]
            for name, arrays in (("near", self.w_f.arrays), ("far", self.w_far)):
                place = 1
                for part in arrays:
                    for i in range(part.shape[0]):
                        pieces.append(part)
                        kinds.append((name, i, functools.partial(step_of, place, size=f_size)))
                        place += 1
            self.pieces, self.kinds = assemble(pieces, kinds)

        def up0(self):
            up_half = lax.dynamic_slice(w_mlp_up, (b * half_f, 0), (half_f, f_size * ff))
            parts = [None] + [
                lax.dynamic_slice(up_half, (0, (f ^ step_of(q, b, f_size)) * ff), (half_f, ff))
                for q in range(1, f_size)
            ]
            self.up_f = Transposing(clock, parts, "fsdp")
            self.up_f.start()

        def upw(self):
            self.up_f.wait()

        def up1(self):
            self.up_f.start()

        def up2(self):
            self.up_f.finish()

        def upc(self):
            self.up_far = [
                swap_at(self.up_f.pieces[q][None], "blk", 1) for q in range(1, f_size)
            ]

        def upd(self):
            far = wait(*self.up_far)
            pieces = [lax.dynamic_slice(w_mlp_up, (0, f * ff), (rows_f, ff))]
            kinds = [("own", 0)]
            for q in range(1, f_size):
                place = functools.partial(step_of, q, size=f_size)
                got, i = self.up_f.found[q]
                pieces += [got[i][None], far[q - 1]]
                kinds += [("near", None, place), ("far", None, place)]
            self.up_pieces, self.up_kinds = assemble(pieces, kinds)

        def gb0(self):
            grad = (self.modulation[5:6] * cotangent.astype(single)).astype(bfloat)
            self.grad_f = Doubling(clock, grad, "fsdp")
            self.grad_f.start()

        def gbw(self):
            self.grad_f.wait()

        def gb1(self):
            self.grad_f.start()

        def gb2(self):
            self.grad_f.finish()
            self.branch_all = jnp.concatenate(self.grad_f.pieces, 0)

        def gbc(self):
            self.branch_far = swap_at(self.branch_all, "blk", 1)

        def gh(self):
            self.grad_hidden = wait(dot(self.branch_all, w_mlp_down, (1, 1)))

        def attn(self):
            parts = [x] + self.x_z.arrays + self.x_far
            kinds, at = [], 0
            for part in parts:
                n = 1 if part.ndim == 2 else part.shape[0]
                kinds.append(list(range(at, at + n)))
                at += n
            near, far, self.qkv, self.norm, self.x_all = run(
                attend_forward, self.w_t, self.modulation, parts, kinds, heads_here, z_size
            )
            self.mixed = (near, far)

        def ex0(self):
            self.to_owner = Exchange(clock, *self.mixed)

        def ex1(self):
            self.to_owner.cross()

        def ex2(self):
            self.to_owner.wait()

        def ex3(self):
            self.to_owner.finish()

        def tok(self):
            (
                self.x_two,
                self.second,
                self.branch_one,
                self.p,
                self.cq,
                self.left,
                self.left_send,
                self.pairs,
            ) = run(
                token_forward,
                self.to_owner.pieces,
                x,
                self.modulation,
                [self.pairs_here] + self.pair_z.arrays + self.pair_far,
                self.pieces,
                self.kinds,
                f_size,
                z_size,
            )

        def lc(self):
            self.left_far = swap_at(self.left_send, "blk", 1)

        def xt0(self):
            self.x_two_f = Doubling(clock, self.x_two, "fsdp")
            self.x_two_f.start()

        def xt1(self):
            self.x_two_f.wait()
            self.x_two_f.start()

        def xt2(self):
            self.x_two_f.finish()
            self.x_two_parts = [self.x_two] + self.x_two_f.arrays

        def ff(self):
            self.hidden, self.pre, keep, send = run(
                feed_forward,
                self.x_two_parts,
                self.grad_hidden,
                self.up_pieces,
                self.up_kinds,
                ff,
                f_size,
            )
            self.gm = Halving(clock, keep, send, "fsdp")

        def gm0(self):
            self.gm.start()

        def gm1(self):
            self.gm.wait()
            self.gm.start()

        def gm2(self):
            self.gm.finish()

        def prc(self):
            self.pre_far = swap_at(self.pre, "blk", 1)

        def turn(self):
            self.hk, self.hs, self.xk, self.xs = run(
                feed_forward_turn, self.x_two_parts, self.hidden, f_size, z_size
            )

        def hsc(self):
            self.hs = swap_at(self.hs, "blk", 1)

        def xsc(self):
            self.xs = swap_at(self.xs, "blk", 1)

        def hsd(self):
            self.hs, self.branch_far = wait(self.hs, self.branch_far)

        def down(self):
            terms = run(
                chip_grads, 1, self.hk, self.hs, self.branch_all, self.branch_far, z_size, False
            )
            self.d = Halving(clock, *terms, "ctx")

        def d0(self):
            self.d.start()

        def d1(self):
            self.d.wait()
            self.d.start()

        def d2(self):
            self.d.finish()

        def xsd(self):
            self.xs, self.pre_far = wait(self.xs, self.pre_far)

        def upg(self):
            self.u_own, send = run(
                chip_grads, 0, self.xk, self.xs, self.pre, self.pre_far, f_size, True
            )
            self.u_f = Direct(clock, [None] + [send[q - 1] for q in range(1, f_size)], "fsdp")

        def u0(self):
            self.u_f.start()

        def u2(self):
            self.u_f.finish()

        def us(self):
            got = [self.u_f.pieces[q][None] for q in range(1, f_size)]
            terms = run(sum_split, 1, self.u_own, got, z_size, False)
            self.u = Halving(clock, *terms, "ctx")

        def uz0(self):
            self.u.start()

        def uz1(self):
            self.u.wait()
            self.u.start()

        def uz2(self):
            self.u.finish()

        def out(self):
            terms = run(feed_forward_out, self.hidden, w_mlp_down, f_size)
            self.branch = Halving(clock, *terms, "fsdp")

        def br0(self):
            self.branch.start()

        def br1(self):
            self.branch.wait()
            self.branch.start()

        def br2(self):
            self.branch.finish()
            mlp_branch = self.branch.sum()
            self.block_out = (self.second + self.modulation[5:6] * mlp_branch).astype(bfloat)
            self.stat_gate = jnp.sum(cotangent.astype(single) * mlp_branch, axis=0, keepdims=True)

        def tb(self):
            (
                near,
                far,
                self.right,
                self.grad_first,
                self.stat_mid,
                self.pair_keep,
                self.pair_send,
            ) = run(
                token_backward,
                self.gm.own,
                [self.gm.last],
                self.second,
                self.branch_one,
                cotangent,
                self.modulation,
                self.p,
                self.cq,
                self.pairs,
                self.pieces,
                self.kinds,
                f_size,
                z_size,
            )
            self.grad_mixed = (near, far)

        def hx0(self):
            self.to_heads = Exchange(clock, *self.grad_mixed)

        def hx1(self):
            self.to_heads.cross()

        def hx2(self):
            self.to_heads.wait()

        def hx3(self):
            self.to_heads.finish()

        def rc(self):
            self.right_far = swap_at(self.right, "blk", 1)

        def rd(self):
            self.right_far, self.left_far = wait(self.right_far, self.left_far)

        def sq(self):
            terms = run(
                square_grads, self.left, self.left_far, self.right, self.right_far, f_size
            )
            self.s = Halving(clock, *terms, "fsdp")

        def s0(self):
            self.s.start()

        def s1(self):
            self.s.wait()
            self.s.start()

        def s2(self):
            self.s.finish()

        def ss(self):
            terms = run(sum_split, 1, self.s.own, [self.s.last], z_size, True)
            self.s = Halving(clock, *terms, "ctx")

        def sz0(self):
            self.s.start()

        def sz1(self):
            self.s.wait()
            self.s.start()

        def sz2(self):
            self.s.finish()

        def pg0(self):
            self.pair_back = swap_at(self.pair_send, "blk", 1)

        def pgd(self):
            value = self.pair_keep + wait(self.pair_back).astype(single)
            self.pair = Halving(clock, value[:m_half], value[m_half:].astype(bfloat), "ctx")

        def pp0(self):
            self.pair.start()

        def pp1(self):
            self.pair.wait()
            self.pair.start()

        def pp2(self):
            self.pair.finish()

        def tg(self):
            self.grad_pairs, self.text_keep, self.text_send = run(
                text_grads, self.pair.own, self.pair.last, self.kv_t
            )

        def tc0(self):
            self.text_got = swap_at(self.text_send, "blk", 1)

        def td0(self):
            self.grad_text = (self.text_keep + wait(self.text_got)).astype(bfloat)

        def tz0(self):
            self.text_got = cross(clock.gate(self.grad_text), "ctx", 0)
            self.text_stage = 1

        def tz1(self):
            value = self.grad_text.astype(single) + wait(self.text_got).astype(single)
            self.grad_text = value.astype(bfloat)
            self.text_got = cross(clock.gate(self.grad_text), "ctx", self.text_stage)
            self.text_stage += 1

        def tz2(self):
            while self.text_stage < bits_of(z_size):
                self.tz1()
            self.grad_text = self.grad_text.astype(single) + wait(self.text_got).astype(single)
            self.text_got = swap_at(self.grad_text, "blk", 1)

        def td1(self):
            self.text_got = wait(self.text_got)

        def h0(self):
            self.grads = list(
                run(attend_backward, 0, self.qkv, self.norm, self.to_heads.pieces, z_size)
            )

        def h1(self):
            for h in range(1, heads_here):
                self.grads += run(
                    attend_backward, h, self.qkv, self.norm, self.to_heads.pieces, z_size
                )

        def pj(self):
            self.close, self.away, self.joined = run(
                attend_project, self.grads, self.w_t, z_size
            )

        def ac(self):
            self.away = swap_at(self.away, "blk", 1)

        def ad(self):
            value = self.close + wait(self.away).astype(single)
            self.m = Halving(clock, value[:m_half], value[m_half:].astype(bfloat), "ctx")

        def m0(self):
            self.m.start()

        def m1(self):
            self.m.wait()
            self.m.start()

        def m2(self):
            self.m.finish()

        def col(self):
            terms = run(
                column_grads, self.joined, self.x_all, text, self.grad_pairs, f_size
            )
            self.c = Halving(clock, *terms, "fsdp")

        def c0(self):
            self.c.start()

        def c1(self):
            self.c.wait()
            self.c.start()

        def c2(self):
            self.c.finish()

        def sp(self):
            (rows,) = run(split_columns, self.c.own, self.c.last, z_size)
            self.to_rows = Transposing(clock, [rows[q] for q in range(z_size)], "ctx")

        def cx0(self):
            self.to_rows.start()

        def cx1(self):
            self.to_rows.wait()
            self.to_rows.start()

        def cx2(self):
            self.to_rows.finish()

        def cc(self):
            self.c_far = [swap_at(part, "blk", 1) for part in self.to_rows.pieces]

        def cd(self):
            self.c_far = list(wait(*self.c_far))

        def pl(self):
            self.grad_attn_in, self.grad_cross_kv = run(
                place_columns, self.to_rows.pieces, self.c_far, wide, z_size
            )

        def fin(self):
            self.grad_latents, self.stat_last = run(
                finish, self.m.own, [self.m.last], x, self.modulation, self.grad_first
            )

        def st0(self):
            rows = [self.stat_last, self.stat_mid, self.stat_gate]
            self.stamp = Summing(clock, jnp.concatenate(rows, axis=0), ("blk", "ctx"))
            self.stamp.start()

        def st1(self):
            self.stamp.wait()
            self.stamp.start()

        def st3(self):
            self.stamp.finish()
            self.table = Summing(clock, self.stamp.value, ("fsdp",))
            self.table.start()

        def st4(self):
            self.table.finish()

    e = Events()
    for event in (
        e.w0, e.x0, e.in0, e.up0, e.x1, e.xc, e.in1, e.w1, e.x2, e.xd0, e.in2, e.proj, e.pz0,
        e.gb0, e.xd, e.attn, e.ex0, e.gbw, e.pz1, e.ex1, e.upw, e.w2, e.ex2, e.pc, e.pz2, e.gb1,
        e.up1, e.pd, e.wd, e.ex3, e.tok, e.xt0, e.lc, e.gb2, e.gbc, e.xt1, e.up2, e.upc, e.gh,
        e.upd, e.xt2, e.ff, e.gm0, e.prc, e.turn, e.hsc, e.xsc, e.hsd, e.down, e.d0, e.gm1, e.xsd,
        e.upg, e.out, e.gm2, e.u0, e.tb, e.hx0, e.rc, e.hx1, e.d1, e.rd, e.sq, e.s0, e.hx2, e.u2,
        e.br0, e.us, e.pg0, e.hx3, e.pgd, e.pp0, e.uz0, e.h0, e.h1, e.br1, e.pp1, e.pj, e.s1, e.ac,
        e.d2, e.uz1, e.pp2, e.tg, e.tc0, e.br2, e.ad, e.m0, e.col, e.c0, e.td0, e.tz0, e.s2, e.ss,
        e.c1, e.uz2, e.tz1, e.m1, e.sz0, e.c2, e.sp, e.m2, e.fin, e.st0, e.st1, e.cx0, e.sz1,
        e.cx1, e.tz2, e.st3, e.cx2, e.cc, e.cd, e.pl, e.td1, e.st4, e.sz2,
    ):
        event()

    grad_table = lax.dynamic_slice(e.table.value, (0, (f * group + g) * own), (6, own))
    square_sum = e.s.sum().reshape(3, own, D)
    up = e.u.sum().reshape(f_size, own, ff)
    back = [up[back_of(q, f_size)] for q in range(f_size)]
    steps = [jnp.where(b == 0, up[q], back[q]) for q in range(f_size)]
    grad_text = jnp.concatenate(reorder([e.grad_text, e.text_got], b), axis=0).T

    return (
        e.block_out[None],
        e.grad_latents[None],
        grad_text[None],
        e.stamp.value.reshape(1, 6 * D),
        grad_table,
        e.grad_attn_in,
        square_sum[0],
        square_sum[1],
        e.grad_cross_kv,
        square_sum[2],
        jnp.concatenate(reorder(steps, f), axis=1),
        e.d.sum(),
        grad_table[3],
    )


def solution(mesh):
    placed = (
        P("fsdp", ("ctx", "blk"), None),
        P("fsdp", None, None),
        P("fsdp", None),
        P(None, "fsdp"),
        P("fsdp", None),
        P("fsdp", None),
        P("fsdp", None),
        P("fsdp", None),
        P("fsdp", None),
        P("fsdp", None),
        P("fsdp", None),
        P("fsdp", ("ctx", "blk"), None),
    )
    owned = P(("fsdp", "ctx", "blk"), None)
    return jax.shard_map(
        shards,
        mesh=mesh,
        in_specs=placed,
        out_specs=(
            P("fsdp", ("ctx", "blk"), None),
            P("fsdp", ("ctx", "blk"), None),
            P("fsdp", None, None),
            P("fsdp", None),
            P(None, ("fsdp", "ctx", "blk")),
            owned,
            owned,
            owned,
            owned,
            owned,
            owned,
            owned,
            P(("fsdp", "ctx", "blk")),
        ),
        check_vma=False,
    )
```

```python
import functools

import jax
import jax.numpy as jnp
from jax import lax
from jax.experimental import pallas as pl
from jax.experimental.pallas import tpu as pltpu
from jax.sharding import PartitionSpec as P

D = 1152
HEADS = 16
HEAD = 72
TEXT = 120

epsilon = 1e-06
bfloat = jnp.bfloat16
single = jnp.float32
scaling = HEAD ** (-0.5)

VMEM = pl.BlockSpec(memory_space=pltpu.VMEM)
SMEM = pl.BlockSpec(memory_space=pltpu.SMEM)
ANY = pl.BlockSpec(memory_space=pl.ANY)
HBM = pl.BlockSpec(memory_space=pltpu.HBM)


def layer_norm(values):
    centred = values - jnp.mean(values, axis=-1, keepdims=True)
    variance = jnp.mean(centred * centred, axis=-1, keepdims=True)
    inverse = lax.rsqrt(variance + epsilon)
    return (centred * inverse, inverse)


def norm_back(grad_normed, normed, inverse):
    first_mean = jnp.mean(grad_normed, axis=-1, keepdims=True)
    second_mean = jnp.mean(grad_normed * normed, axis=-1, keepdims=True)
    return inverse * (grad_normed - first_mean - normed * second_mean)


def dot(left, right, axes=(1, 0)):
    return lax.dot_general(
        left, right, (((axes[0],), (axes[1],)), ((), ())), preferred_element_type=single
    )


def shape(dims, dtype=bfloat):
    return jax.ShapeDtypeStruct(tuple(dims), dtype)


def call(body, outs, args, specs, scratch=(), megabytes=40, micros=2):
    return pl.pallas_call(
        body,
        out_shape=tuple(outs),
        in_specs=list(specs),
        out_specs=tuple(VMEM for _ in outs),
        scratch_shapes=list(scratch),
        compiler_params=pltpu.CompilerParams(vmem_limit_bytes=megabytes * 2**20),
        cost_estimate=pl.CostEstimate(
            flops=int(micros * 1.15e9), bytes_accessed=1, transcendentals=0
        ),
    )(*args)


def swap(values, axis, step):
    size = lax.axis_size(axis)
    return lax.ppermute(values, axis, [(i, i ^ step) for i in range(size)])


def bits_of(size):
    return size.bit_length() - 1


def back_of(place, size):
    bits = bits_of(size)
    return sum(((place >> j) & 1) << (bits - 1 - j) for j in range(bits))


def step_of(place, core, size):
    return jnp.where(core == 0, place, back_of(place, size))


def cross(values, axis, stage):
    size = lax.axis_size(axis)
    pairs = []
    for i in range(size):
        for core in range(2):
            step = 1 << stage if core == 0 else 1 << (bits_of(size) - 1 - stage)
            pairs.append((2 * i + core, 2 * (i ^ step) + core))
    return lax.ppermute(values, (axis, "blk"), pairs)


class Clock:
    def __init__(self, ids):
        self.ids = ids
        self.token = ids

    def gate(self, values):
        return after(values, self.token)

    def wait(self, *values):
        out = lax.optimization_barrier(values + (self.token,))
        self.token = out[-1]
        return out[0] if len(values) == 1 else out[:-1]

    def run(self, kernel, *args, **named):
        outs = kernel(self.gate(self.ids), *args, **named)
        self.token = after(self.token, outs[0])
        return outs

    def swap(self, values, axis, step):
        return swap(self.gate(values), axis, step)


class Doubling:
    def __init__(self, clock, values, axis):
        self.clock, self.axis = clock, axis
        self.pieces = [values]
        self.arrays = []
        self.bits = bits_of(lax.axis_size(axis))
        self.stage = 0
        self.got = None

    def start(self):
        message = self.pieces[0][None] if self.stage == 0 else jnp.stack(self.pieces, 0)
        self.got = cross(self.clock.gate(message), self.axis, self.stage)
        self.stage += 1

    def wait(self):
        got = self.clock.wait(self.got)
        self.arrays.append(got)
        self.pieces += [got[i] for i in range(len(self.pieces))]

    def finish(self):
        self.wait()
        while self.stage < self.bits:
            self.start()
            self.wait()


class Transposing:
    def __init__(self, clock, chunks, axis):
        self.clock, self.axis = clock, axis
        self.pieces = list(chunks)
        self.bits = bits_of(lax.axis_size(axis))
        self.stage = 0
        self.found = {}

    def moved(self):
        return [q for q in range(len(self.pieces)) if (q >> (self.stage - 1)) & 1]

    def start(self):
        self.stage += 1
        message = jnp.stack([self.pieces[q] for q in self.moved()], 0)
        self.got = cross(self.clock.gate(message), self.axis, self.stage - 1)

    def wait(self):
        self.got = self.clock.wait(self.got)
        for i, q in enumerate(self.moved()):
            self.pieces[q] = self.got[i]
            self.found[q] = (self.got, i)

    def finish(self):
        self.wait()
        while self.stage < self.bits:
            self.start()
            self.wait()


class Direct:
    def __init__(self, clock, chunks, axis):
        self.clock, self.axis = clock, axis
        self.pieces = list(chunks)

    def start(self):
        size = lax.axis_size(self.axis)
        for q in range(1, size):
            pairs = []
            for i in range(size):
                pairs += [(2 * i, 2 * (i ^ q)), (2 * i + 1, 2 * (i ^ back_of(q, size)) + 1)]
            chunk = self.clock.gate(self.pieces[q])
            self.pieces[q] = lax.ppermute(chunk, (self.axis, "blk"), pairs)

    def finish(self):
        self.pieces[1:] = list(self.clock.wait(*self.pieces[1:]))


class Halving:
    def __init__(self, clock, keep, send, axis):
        self.clock, self.axis = clock, axis
        self.keep, self.send = keep, send
        self.stage = bits_of(lax.axis_size(axis)) - 1
        self.got = None

    def start(self):
        self.got = cross(self.clock.gate(self.send), self.axis, self.stage)
        self.stage -= 1

    def wait(self):
        got = self.clock.wait(self.got)
        if self.stage < 0:
            self.own, self.last = self.keep[0], got[0]
            return
        half = self.keep.shape[0] // 2
        self.send = (self.keep[half:] + got[half:].astype(single)).astype(bfloat)
        self.keep = self.keep[:half] + got[:half].astype(single)

    def finish(self):
        self.wait()
        while self.stage >= 0:
            self.start()
            self.wait()

    def sum(self):
        return self.own + self.last.astype(single)


class Exchange:
    def __init__(self, clock, near, far):
        self.clock, self.near = clock, near
        self.far = clock.swap(far, "blk", 1)

    def cross(self):
        self.far = self.clock.wait(self.far)
        both = [jnp.stack([self.near[q], self.far[q]], 0) for q in range(self.near.shape[0])]
        self.by_z = Transposing(self.clock, both, "ctx")
        self.by_z.start()

    def wait(self):
        self.by_z.wait()
        self.by_z.start()

    def finish(self):
        self.by_z.finish()
        self.pieces = self.by_z.pieces


def tree_sum(parts):
    while len(parts) > 1:
        parts = [parts[i] + parts[i + 1] for i in range(0, len(parts), 2)]
    return parts[0]


def reorder(parts, index):
    count = len(parts)
    bit = 1
    parts = list(parts)
    while bit < count:
        flag = (index & bit) != 0
        parts = [jnp.where(flag, parts[i ^ bit], parts[i]) for i in range(count)]
        bit *= 2
    return parts


def after(values, *earlier):
    return lax.optimization_barrier((values,) + earlier)[0]


def aligned(index, unit):
    return pl.multiple_of(index, unit)


def project_text(ids, own_part, parts, text, own_wide, kv_wide, f_size):
    rows, cols = own_part.shape
    count = f_size
    n_parts = len(parts)

    def body(*refs):
        ids_ref, text_ref = refs[0], refs[1]
        own_ref = refs[2]
        part_refs = refs[3 : 3 + n_parts]
        w_ref, kv_ref, pairs_ref, table_ref = refs[3 + n_parts : 7 + n_parts]
        full, sems = refs[7 + n_parts :]
        f, b = ids_ref[0], ids_ref[2]
        sources = [own_ref] + [ref.at[i] for ref in part_refs for i in range(ref.shape[0])]
        copies = []
        for q, source in enumerate(sources):
            place = pl.ds(aligned((f ^ step_of(q, b, count)) * rows, 16), rows)
            copies.append(pltpu.make_async_copy(source, full.at[place, :], sems.at[q]))
        for copy in copies:
            copy.start()
        for copy in copies:
            copy.wait()
        turned = full[...].T
        w_ref[...] = turned[:own_wide]
        kv = turned[own_wide : own_wide + kv_wide]
        kv_ref[...] = kv
        pairs_ref[...] = dot(kv, text_ref[...], (1, 1)).astype(bfloat)
        table_ref[...] = turned[own_wide + kv_wide :].astype(single)

    return call(
        body,
        [
            shape((own_wide, D)),
            shape((kv_wide, D)),
            shape((kv_wide, TEXT)),
            shape((cols - own_wide - kv_wide, D), single),
        ],
        [ids, text, own_part] + list(parts),
        [SMEM, VMEM] + [ANY] * (1 + n_parts),
        [pltpu.VMEM((count * rows, cols), bfloat), pltpu.SemaphoreType.DMA((count,))],
        megabytes=16,
        micros=2.6,
    )


def attend_forward(ids, w_t, modulation, x_parts, x_kinds, heads_here, z_size):
    tok = x_parts[0].shape[-2]
    count = 2 * z_size
    total = count * tok
    width = 256 if total % 256 == 0 else tok
    per = width // tok
    n_parts = len(x_parts)

    def body(*refs):
        ids_ref, w_ref, mod_ref = refs[:3]
        x_refs = refs[3 : 3 + n_parts]
        near_ref, far_ref, qkv_ref, norm_ref, x_all = refs[3 + n_parts : 8 + n_parts]
        raw, sems = refs[8 + n_parts :]
        b = ids_ref[2]
        copies = []
        for ref, chunks in zip(x_refs, x_kinds):
            for i, chunk in enumerate(chunks):
                source = ref if len(ref.shape) == 2 else ref.at[i]
                target = raw.at[pl.ds(chunk * tok, tok), :]
                copies.append(pltpu.make_async_copy(source, target, sems.at[chunk]))
        for copy in copies:
            copy.start()
        for copy in copies:
            copy.wait()

        def project(j, carry):
            place = pl.ds(aligned(j * width, width), width)
            normed, _ = layer_norm(raw[place, :].astype(single))
            modulated = (normed * (1.0 + mod_ref[1:2]) + mod_ref[0:1]).astype(bfloat)
            x_all[place, :] = modulated
            got = dot(w_ref[...], modulated, (1, 1))
            for i in range(3 * heads_here):
                qkv_ref[i, :, place] = got[i * HEAD : (i + 1) * HEAD].astype(bfloat)
            return carry

        lax.fori_loop(0, total // width, project, 0)

        def attend(h, carry):
            keys = qkv_ref[heads_here + h]
            values = qkv_ref[2 * heads_here + h]
            for core, target in ((0, near_ref), (1, far_ref)):

                def block(j, carry, core=core, target=target):
                    at = core * z_size * tok + j * width
                    place = pl.ds(aligned(at, width), width)
                    scores = dot(keys, qkv_ref[h, :, place], (0, 0)) * scaling
                    top = jnp.max(scores, axis=0, keepdims=True)
                    exponent = jnp.exp(scores - top)
                    summed = jnp.sum(exponent, axis=0, keepdims=True)
                    weights = (exponent * (1.0 / summed)).astype(bfloat)
                    mixed = dot(values, weights).astype(bfloat)
                    norm_ref[h, :, place] = top + jnp.log(summed)
                    for i in range(per):
                        piece = mixed[:, i * tok : (i + 1) * tok]
                        target[j * per + i, h] = piece
                    return carry

                lax.fori_loop(0, z_size * tok // width, block, 0)
            return carry

        lax.fori_loop(0, heads_here, attend, 0)

    wide = heads_here * HEAD
    return call(
        body,
        [
            shape((z_size, heads_here, HEAD, tok)),
            shape((z_size, heads_here, HEAD, tok)),
            shape((3 * heads_here, HEAD, total)),
            shape((heads_here, 1, total), single),
            shape((total, D)),
        ],
        [ids, w_t, modulation] + list(x_parts),
        [SMEM, VMEM, VMEM] + [ANY] * n_parts,
        [pltpu.VMEM((total, D), bfloat), pltpu.SemaphoreType.DMA((count,))],
        megabytes=24,
        micros=1.5,
    )


def weight_copies(piece_refs, kinds, full, sems, f, b, rows):
    copies = []
    half = rows // 2
    for i, (ref, kind) in enumerate(zip(piece_refs, kinds)):
        sem = sems.at[i]
        if kind[0] == "whole":
            copies.append(pltpu.make_async_copy(ref, full, sem))
        elif kind[0] == "own":
            place = pl.ds(aligned(f * rows, 16), rows)
            copies.append(pltpu.make_async_copy(ref, full.at[kind[1], place, :], sem))
        else:
            core = b if kind[0] == "near" else 1 - b
            source = f ^ kind[2](core)
            place = pl.ds(aligned(source * rows + core * half, 16), half)
            target = full.at[:, place, :]
            ref = ref if kind[1] is None else ref.at[kind[1]]
            copies.append(pltpu.make_async_copy(ref, target, sem))
    return copies


def piece_specs(kinds):
    return [HBM if kind[0] == "own" else ANY for kind in kinds]


def permute_rows(source, target, count, piece):
    for k in range(count):
        for core in range(2):
            target[core, pl.ds(k * piece, piece), :] = source[
                pl.ds((2 * k + core) * piece, piece), :
            ]


def token_forward(ids, got, x, modulation, pair_parts, pieces, kinds, f_size, z_size):
    tok = x.shape[0]
    heads_here = got[0].shape[1]
    rows = D // f_size
    own = D // (2 * f_size * z_size)
    kv_wide = D // z_size
    n_got, n_pieces, n_pairs = len(got), len(pieces), len(pair_parts)

    def body(*refs):
        ids_ref, x_ref, mod_ref = refs[:3]
        got_refs = refs[3 : 3 + n_got]
        pair_refs = refs[3 + n_got : 3 + n_got + n_pairs]
        at = 3 + n_got + n_pairs
        piece_refs = refs[at : at + n_pieces]
        rest = refs[at + n_pieces :]
        x_two_ref, second_ref, branch_ref, p_ref, cq_ref, keep_ref, send_ref, pairs_ref = rest[:8]
        full, mixed, pair_s, turned, left, sems = rest[8:]
        f, z, b = ids_ref[0], ids_ref[1], ids_ref[2]
        copies = weight_copies(piece_refs, kinds, full, sems, f, b, rows)
        for copy in copies:
            copy.start()

        for q in range(z_size):
            for core in range(2):
                g = 2 * (z ^ step_of(q, b, z_size)) + (b ^ core)
                for h in range(heads_here):
                    place = pl.ds(aligned((g * heads_here + h) * HEAD, 8), HEAD)
                    mixed[place, :] = got_refs[q][core, h].astype(single)
        for core in range(2):
            q = 0
            for ref in pair_refs[core * (n_pairs // 2) : (core + 1) * (n_pairs // 2)]:
                for source in [ref] if len(ref.shape) == 2 else [ref.at[i] for i in range(ref.shape[0])]:
                    g = 2 * (z ^ step_of(q, b ^ core, z_size)) + (b ^ core)
                    place = pl.ds(aligned(g * kv_wide, 8), kv_wide)
                    pair_s[place, :] = source[...].astype(single)
                    q += 1
        pairs_ref[...] = pair_s[...]

        def keep_left(i, source):
            permute_rows(source, left, f_size * z_size, own)
            keep_ref[i] = left[b].astype(bfloat)
            send_ref[i] = left[1 - b].astype(bfloat)

        keep_left(0, mixed)
        shift_two, scale_two, gate_one = mod_ref[3:4], mod_ref[4:5], mod_ref[2:3]
        for copy in copies:
            copy.wait()
        branch = dot(mixed[...].T.astype(bfloat), full[0])
        branch_ref[...] = branch
        first = x_ref[...].astype(single) + gate_one * branch
        first_low = first.astype(bfloat)
        turned[...] = first_low.astype(single).T
        keep_left(1, turned)
        turned[...] = dot(first_low, full[1]).T
        cq_ref[...] = turned[...].astype(bfloat)
        def attend(h, carry):
            rows_h = pl.ds(aligned(h * HEAD, 8), HEAD)
            keys = pair_s[rows_h, :].astype(bfloat)
            values = pair_s[pl.ds(aligned(D + h * HEAD, 8), HEAD), :].astype(bfloat)
            scores = dot(keys, turned[rows_h, :].astype(bfloat), (0, 0)) * scaling
            top = jnp.max(scores, axis=0, keepdims=True)
            exponent = jnp.exp(scores - top)
            weights = exponent * (1.0 / jnp.sum(exponent, axis=0, keepdims=True))
            p_ref[h] = weights
            mixed[rows_h, :] = dot(values, weights.astype(bfloat)).astype(bfloat).astype(single)
            return carry

        lax.fori_loop(0, HEADS, attend, 0, unroll=4)
        second = first + dot(mixed[...].T.astype(bfloat), full[2])
        second_ref[...] = second
        normed, _ = layer_norm(second)
        x_two_ref[...] = (normed * (1.0 + scale_two) + shift_two).astype(bfloat)
        keep_left(2, mixed)

    return call(
        body,
        [
            shape((tok, D)),
            shape((tok, D), single),
            shape((tok, D), single),
            shape((HEADS, TEXT, tok), single),
            shape((D, tok)),
            shape((3, D // 2, tok)),
            shape((3, D // 2, tok)),
            shape((2 * D, TEXT), single),
        ],
        [ids, x, modulation] + list(got) + list(pair_parts) + list(pieces),
        [SMEM] + [VMEM] * (2 + n_got + n_pairs) + piece_specs(kinds),
        [
            pltpu.VMEM((3, D, D), bfloat),
            pltpu.VMEM((D, tok), single),
            pltpu.VMEM((2 * D, TEXT), single),
            pltpu.VMEM((D, tok), single),
            pltpu.VMEM((2, D // 2, tok), single),
            pltpu.SemaphoreType.DMA((n_pieces,)),
        ],
        megabytes=28,
        micros=7.0,
    )


def feed_forward(ids, x_parts, grad_hidden, pieces, kinds, ff, f_size):
    count = f_size
    n_parts = len(x_parts)
    tok = x_parts[0].shape[0]
    tile = 384 if ff % 384 == 0 else ff
    rows = D // f_size
    n_pieces = len(pieces)

    def body(*refs):
        ids_ref = refs[0]
        x_refs = refs[1 : 1 + n_parts]
        gh_ref = refs[1 + n_parts]
        piece_refs = refs[2 + n_parts : 2 + n_parts + n_pieces]
        rest = refs[2 + n_parts + n_pieces :]
        hidden_ref, pre_ref, keep_ref, send_ref = rest[:4]
        x_all, full, sems = rest[4:]
        up_ref = full.at[0]
        copies = weight_copies(piece_refs, kinds, full, sems, ids_ref[0], ids_ref[2], rows)
        for copy in copies:
            copy.start()
        x_all[0:tok, :] = x_refs[0][...]
        at = tok
        for ref in x_refs[1:]:
            for i in range(ref.shape[0]):
                x_all[at : at + tok, :] = ref[i]
                at += tok
        for copy in copies:
            copy.wait()

        def step(j, carry):
            place = pl.ds(aligned(j * tile, 128), tile) if ff > tile else pl.ds(0, tile)
            u = dot(x_all[...], up_ref[:, place])
            square = u * u
            t = jnp.tanh(0.7978845608028654 * u * (1.0 + 0.044715 * square))
            half = 0.5 * (1.0 + t)
            hidden_ref[:, place] = (u * half).astype(bfloat)
            slope = half + 0.5 * u * (1.0 - t * t) * (
                0.7978845608028654 * (1.0 + 0.134145 * square)
            )
            pre_ref[:, place] = (gh_ref[:, place] * slope).astype(bfloat)
            return carry

        if ff > tile:
            lax.fori_loop(0, ff // tile, step, 0)
        else:
            step(0, 0)
        part = dot(pre_ref[...], up_ref[...], (1, 1))
        for i in range(count):
            piece = part[i * tok : (i + 1) * tok]
            if i < count // 2:
                keep_ref[i] = piece
            else:
                send_ref[i - count // 2] = piece.astype(bfloat)

    total = count * tok
    return call(
        body,
        [
            shape((total, ff)),
            shape((total, ff)),
            shape((count // 2, tok, D), single),
            shape((count // 2, tok, D)),
        ],
        [ids] + list(x_parts) + [grad_hidden] + list(pieces),
        [SMEM] + [VMEM] * (n_parts + 1) + piece_specs(kinds),
        [
            pltpu.VMEM((total, D), bfloat),
            pltpu.VMEM((1, D, ff), bfloat),
            pltpu.SemaphoreType.DMA((n_pieces,)),
        ],
        megabytes=24,
        micros=7.0,
    )


def feed_forward_turn(ids, x_parts, hidden, f_size, z_size):
    n_parts = len(x_parts)
    tok = x_parts[0].shape[0]
    total, ff = hidden.shape
    own = D // (2 * f_size * z_size)
    own_down = ff // (2 * z_size)

    def body(*refs):
        ids_ref, hidden_ref = refs[:2]
        x_refs = refs[2 : 2 + n_parts]
        hk_ref, hs_ref, xk_ref, xs_ref, flat, halves, flat_down, halves_down = refs[2 + n_parts :]
        b = ids_ref[2]
        flat_down[...] = hidden_ref[...].T.astype(single)
        permute_rows(flat_down, halves_down, z_size, own_down)
        hk_ref[...] = halves_down[b].astype(bfloat)
        hs_ref[...] = halves_down[1 - b].astype(bfloat)
        flat[:, 0:tok] = x_refs[0][...].T.astype(single)
        at = tok
        for ref in x_refs[1:]:
            for i in range(ref.shape[0]):
                flat[:, at : at + tok] = ref[i].T.astype(single)
                at += tok
        permute_rows(flat, halves, f_size * z_size, own)
        xk_ref[...] = halves[b].astype(bfloat)
        xs_ref[...] = halves[1 - b].astype(bfloat)

    return call(
        body,
        [shape((ff // 2, total))] * 2 + [shape((D // 2, total))] * 2,
        [ids, hidden] + list(x_parts),
        [SMEM] + [VMEM] * (1 + n_parts),
        [
            pltpu.VMEM((D, total), single),
            pltpu.VMEM((2, D // 2, total), single),
            pltpu.VMEM((ff, total), single),
            pltpu.VMEM((2, ff // 2, total), single),
        ],
        megabytes=20,
        micros=0.1,
    )


def feed_forward_out(ids, hidden, down, count):
    total = hidden.shape[0]
    tok = total // count

    def body(_, hidden_ref, down_ref, keep_ref, send_ref):
        part = dot(hidden_ref[...], down_ref[...])
        for i in range(count):
            piece = part[i * tok : (i + 1) * tok]
            if i < count // 2:
                keep_ref[i] = piece
            else:
                send_ref[i - count // 2] = piece.astype(bfloat)

    return call(
        body,
        [shape((count // 2, tok, D), single), shape((count // 2, tok, D))],
        [ids, hidden, down],
        [SMEM, VMEM, VMEM],
        megabytes=12,
        micros=0.1,
    )


def chip_grads(ids, index, left, left_far, right, right_far, count, direct):
    rows, tok = left.shape
    cols = right.shape[1]
    part = rows // count
    held = 1 if direct else count // 2

    def body(*refs):
        ids_ref, left_ref, lf_ref, right_ref, rf_ref, keep_ref, send_ref = refs[:7]
        left_s, right_s, flat = refs[7:]
        i, b = ids_ref[index], ids_ref[2]
        left_s[:, 0:tok] = left_ref[...]
        left_s[:, tok : 2 * tok] = lf_ref[...]
        right_s[0:tok, :] = right_ref[...]
        right_s[tok : 2 * tok, :] = rf_ref[...]
        value = dot(left_s[...], right_s[...])
        for k in range(count):
            flat[k] = value[k * part : (k + 1) * part]
        for q in range(count):
            piece = flat[i ^ step_of(q, b, count)]
            if q < held:
                keep_ref[q] = piece
            else:
                send_ref[q - held] = piece.astype(bfloat)

    return call(
        body,
        [shape((held, part, cols), single), shape((count - held, part, cols))],
        [ids, left, left_far, right, right_far],
        [SMEM] + [VMEM] * 4,
        [
            pltpu.VMEM((rows, 2 * tok), bfloat),
            pltpu.VMEM((2 * tok, cols), bfloat),
            pltpu.VMEM((count, part, cols), single),
        ],
        megabytes=24,
        micros=0.1,
    )


def token_backward(
    ids, own, got, second, branch, cotangent, modulation, p, cq, pairs, pieces, kinds, f_size, z_size
):
    tok = second.shape[0]
    heads_here = HEADS // (2 * z_size)
    rows = D // f_size
    kv_wide = D // z_size
    n_got, n_pieces = len(got), len(pieces)

    def body(*refs):
        ids_ref, own_ref, second_ref, branch_ref, cot_ref, mod_ref, p_ref, cq_ref, pairs_ref = refs[:9]
        got_refs = refs[9 : 9 + n_got]
        piece_refs = refs[9 + n_got : 9 + n_got + n_pieces]
        rest = refs[9 + n_got + n_pieces :]
        near_ref, far_ref, right_ref, first_ref, stat_ref, pair_keep, pair_send = rest[:7]
        full, turned, grads, low, sems = rest[7:]
        pair_s = pairs_ref
        f, z, b = ids_ref[0], ids_ref[1], ids_ref[2]
        copies = weight_copies(piece_refs, kinds, full, sems, f, b, rows)
        for copy in copies:
            copy.start()
        gate_one, scale_two = mod_ref[2:3], mod_ref[4:5]
        grad_mod = own_ref[...]
        for ref in got_refs:
            grad_mod = grad_mod + ref[...].astype(single)
        normed, inverse = layer_norm(second_ref[...])
        stat_ref[1:2] = jnp.sum(grad_mod, axis=0, keepdims=True)
        stat_ref[2:3] = jnp.sum(grad_mod * normed, axis=0, keepdims=True)
        grad_second = cot_ref[...].astype(single) + norm_back(
            grad_mod * (1.0 + scale_two), normed, inverse
        )
        grad_low = grad_second.astype(bfloat)
        right_ref[2] = grad_low
        for copy in copies:
            copy.wait()
        turned[...] = dot(full[2], grad_low, (1, 1))
        low[...] = cq_ref[...].astype(single)
        def attend(h, carry):
            rows_h = pl.ds(aligned(h * HEAD, 8), HEAD)
            rows_v = pl.ds(aligned(D + h * HEAD, 8), HEAD)
            keys = pair_s[rows_h, :].astype(bfloat)
            values = pair_s[rows_v, :].astype(bfloat)
            grad_h = turned[rows_h, :].astype(bfloat)
            weights = p_ref[h]
            grad_weights = dot(values, grad_h, (0, 0))
            grads[rows_v, :] = dot(grad_h, weights.astype(bfloat), (1, 1))
            inner = jnp.sum(weights * grad_weights, axis=0, keepdims=True)
            grad_scores = (weights * (grad_weights - inner)).astype(bfloat)
            turned[rows_h, :] = scaling * dot(keys, grad_scores)
            grads[rows_h, :] = scaling * dot(low[rows_h, :].astype(bfloat), grad_scores, (1, 1))
            return carry

        lax.fori_loop(0, HEADS, attend, 0, unroll=4)
        for q in range(z_size):
            here = 2 * (z ^ step_of(q, b, z_size)) + b
            there = 2 * (z ^ step_of(q, 1 - b, z_size)) + 1 - b
            pair_keep[q] = grads[pl.ds(aligned(here * kv_wide, 8), kv_wide), :]
            place = pl.ds(aligned(there * kv_wide, 8), kv_wide)
            pair_send[q] = grads[place, :].astype(bfloat)
        grad_query = turned[...].T.astype(bfloat)
        right_ref[1] = grad_query
        grad_first = grad_second + dot(grad_query, full[1], (1, 1))
        first_ref[...] = grad_first
        stat_ref[0:1] = jnp.sum(grad_first * branch_ref[...], axis=0, keepdims=True)
        grad_branch = (gate_one * grad_first).astype(bfloat)
        right_ref[0] = grad_branch
        turned[...] = dot(full[0], grad_branch, (1, 1))
        for q in range(z_size):
            for core in range(2):
                target = near_ref if core == 0 else far_ref
                g = 2 * (z ^ step_of(q, b ^ core, z_size)) + (b ^ core)
                for h in range(heads_here):
                    place = pl.ds(aligned((g * heads_here + h) * HEAD, 8), HEAD)
                    target[q, h] = turned[place, :].astype(bfloat)

    return call(
        body,
        [
            shape((z_size, heads_here, HEAD, tok)),
            shape((z_size, heads_here, HEAD, tok)),
            shape((3, tok, D)),
            shape((tok, D), single),
            shape((3, D), single),
            shape((z_size, kv_wide, TEXT), single),
            shape((z_size, kv_wide, TEXT)),
        ],
        [ids, own, second, branch, cotangent, modulation, p, cq, pairs] + list(got) + list(pieces),
        [SMEM] + [VMEM] * (8 + n_got) + piece_specs(kinds),
        [
            pltpu.VMEM((3, D, D), bfloat),
            pltpu.VMEM((D, tok), single),
            pltpu.VMEM((2 * D, TEXT), single),
            pltpu.VMEM((D, tok), single),
            pltpu.SemaphoreType.DMA((n_pieces,)),
        ],
        megabytes=28,
        micros=0.1,
    )


def square_grads(ids, left, left_far, right, right_far, f_size):
    count, half, tok = left.shape
    part = half // f_size

    def body(*refs):
        ids_ref, left_ref, lf_ref, right_ref, rf_ref, keep_ref, send_ref = refs[:7]
        left_s, right_s, flat = refs[7:]
        f, b = ids_ref[0], ids_ref[2]
        for i in range(count):
            left_s[:, 0:tok] = left_ref[i]
            left_s[:, tok : 2 * tok] = lf_ref[i]
            right_s[0:tok, :] = right_ref[i]
            right_s[tok : 2 * tok, :] = rf_ref[i]
            value = dot(left_s[...], right_s[...])
            for k in range(f_size):
                flat[k] = value[k * part : (k + 1) * part]
            for q in range(f_size):
                value = flat[f ^ step_of(q, b, f_size)]
                if q < f_size // 2:
                    keep_ref[q, i] = value
                else:
                    send_ref[q - f_size // 2, i] = value.astype(bfloat)

    return call(
        body,
        [
            shape((f_size // 2, count, part, D), single),
            shape((f_size // 2, count, part, D)),
        ],
        [ids, left, left_far, right, right_far],
        [SMEM] + [VMEM] * 4,
        [
            pltpu.VMEM((half, 2 * tok), bfloat),
            pltpu.VMEM((2 * tok, D), bfloat),
            pltpu.VMEM((f_size, part, D), single),
        ],
        megabytes=20,
        micros=0.1,
    )


def sum_split(ids, index, own, got, count, add):
    lead, rows, cols = own.shape
    part = rows // count
    n_got = len(got)
    groups = lead if add else lead * (1 + n_got)

    def body(*refs):
        ids_ref, own_ref = refs[:2]
        got_refs = refs[2 : 2 + n_got]
        keep_ref, send_ref, flat, chunks = refs[2 + n_got :]
        i, b = ids_ref[index], ids_ref[2]

        for k in range(lead):
            if add:
                value = own_ref[k]
                for ref in got_refs:
                    value = value + ref[k].astype(single)
                flat[k] = value
            else:
                flat[k] = own_ref[k]
                for j, ref in enumerate(got_refs):
                    flat[(j + 1) * lead + k] = ref[k].astype(single)
        for k in range(groups):
            for c in range(count):
                chunks[c, pl.ds(k * part, part), :] = flat[k, pl.ds(c * part, part), :]
        for q in range(count):
            value = chunks[i ^ step_of(q, b, count)]
            if q < count // 2:
                keep_ref[q] = value
            else:
                send_ref[q - count // 2] = value.astype(bfloat)

    return call(
        body,
        [
            shape((count // 2, groups * part, cols), single),
            shape((count // 2, groups * part, cols)),
        ],
        [ids, own] + list(got),
        [SMEM] + [VMEM] * (1 + n_got),
        [
            pltpu.VMEM((groups, rows, cols), single),
            pltpu.VMEM((count, groups * part, cols), single),
        ],
        megabytes=24,
        micros=0.1,
    )


def attend_backward(ids, h, qkv, norm, got, z_size):
    heads_here, _, tok = got[0].shape[1:]
    count = 2 * z_size
    total = count * tok
    width = 256 if total % 256 == 0 else tok
    n_got = len(got)

    def body(*refs):
        _, qkv_ref, norm_ref = refs[:3]
        got_refs = refs[3 : 3 + n_got]
        out_ref, grad, flat_k, flat_v = refs[3 + n_got :]
        for core in range(2):
            for q in range(z_size):
                at = (core * z_size + q) * tok
                place = q if core == 0 else back_of(q, z_size)
                grad[:, at : at + tok] = got_refs[place][core, h]
        flat_k[...] = jnp.zeros_like(flat_k)
        flat_v[...] = jnp.zeros_like(flat_v)
        keys = qkv_ref[heads_here + h]
        values = qkv_ref[2 * heads_here + h]

        def block(j, carry):
            place = pl.ds(aligned(j * width, width), width)
            query = qkv_ref[h, :, place]
            grad_h = grad[:, place]
            scores = dot(keys, query, (0, 0)) * scaling
            weights = jnp.exp(scores - norm_ref[h, :, place])
            grad_weights = dot(values, grad_h, (0, 0))
            inner = jnp.sum(weights * grad_weights, axis=0, keepdims=True)
            grad_scores = (weights * (grad_weights - inner)).astype(bfloat)
            flat_v[...] += dot(grad_h, weights.astype(bfloat), (1, 1))
            out_ref[0, :, place] = (scaling * dot(keys, grad_scores)).astype(bfloat)
            flat_k[...] += scaling * dot(query, grad_scores, (1, 1))
            return carry

        lax.fori_loop(0, total // width, block, 0)
        out_ref[1] = flat_k[...].astype(bfloat)
        out_ref[2] = flat_v[...].astype(bfloat)

    return call(
        body,
        [shape((3, HEAD, total))],
        [ids, qkv, norm] + list(got),
        [SMEM] + [VMEM] * (2 + n_got),
        [
            pltpu.VMEM((HEAD, total), bfloat),
            pltpu.VMEM((HEAD, total), single),
            pltpu.VMEM((HEAD, total), single),
        ],
        megabytes=20,
        micros=0.1,
    )


def attend_project(ids, grads, w_t, z_size):
    heads_here = len(grads)
    total = grads[0].shape[-1]
    tok = total // (2 * z_size)
    wide3 = 3 * heads_here * HEAD
    width = z_size * tok

    def body(*refs):
        w_ref = refs[1]
        grad_refs = refs[2 : 2 + heads_here]
        close_ref, away_ref, low, flat = refs[2 + heads_here :]
        for h in range(heads_here):
            for i in range(3):
                place = pl.ds((i * heads_here + h) * HEAD, HEAD)
                flat[place, :] = grad_refs[h][i].astype(single)
        low[...] = flat[...].astype(bfloat)
        for core in (1, 0):
            part = dot(low[:, core * width : (core + 1) * width], w_ref[...], (0, 0))
            for q in range(z_size):
                piece = part[q * tok : (q + 1) * tok]
                if core == 0:
                    close_ref[q] = piece
                else:
                    away_ref[q] = piece.astype(bfloat)

    return call(
        body,
        [
            shape((z_size, tok, D), single),
            shape((z_size, tok, D)),
            shape((wide3, total)),
        ],
        [ids, w_t] + list(grads),
        [SMEM] + [VMEM] * (1 + heads_here),
        [pltpu.VMEM((wide3, total), single)],
        megabytes=24,
        micros=0.1,
    )


def text_grads(ids, own, got, kv_t):
    def body(ids_ref, own_ref, got_ref, kv_ref, pairs_ref, keep_ref, send_ref, flat):
        b = ids_ref[2]
        pairs = (own_ref[...] + got_ref[...].astype(single)).astype(bfloat)
        pairs_ref[...] = pairs
        part = dot(kv_ref[...], pairs, (0, 0))
        flat[0] = part[: D // 2]
        flat[1] = part[D // 2 :]
        keep_ref[...] = flat[b]
        send_ref[...] = flat[1 - b]

    return call(
        body,
        [
            shape(own.shape),
            shape((D // 2, TEXT), single),
            shape((D // 2, TEXT), single),
        ],
        [ids, own, got, kv_t],
        [SMEM] + [VMEM] * 3,
        [pltpu.VMEM((2, D // 2, TEXT), single)],
        megabytes=16,
        micros=0.1,
    )


def split_columns(ids, own, got, z_size):
    rows, cols = own.shape
    part = rows // z_size

    def body(ids_ref, own_ref, got_ref, out_ref, chunks):
        z, b = ids_ref[1], ids_ref[2]
        value = own_ref[...] + got_ref[...].astype(single)
        for k in range(z_size):
            chunks[k] = value[k * part : (k + 1) * part]
        for q in range(z_size):
            out_ref[q] = chunks[z ^ step_of(q, b, z_size)].astype(bfloat)

    return call(
        body,
        [shape((z_size, part, cols))],
        [ids, own, got],
        [SMEM] + [VMEM] * 2,
        [pltpu.VMEM((z_size, part, cols), single)],
        megabytes=16,
        micros=0.1,
    )


def place_columns(ids, near, far, wide, z_size):
    part, cols = near[0].shape[0] // 2, near[0].shape[1]
    kv_wide = cols - 3 * wide

    def body(*refs):
        ids_ref = refs[0]
        in_ref, kv_ref, blocks, pair = refs[1 + 2 * z_size :]
        z, b = ids_ref[1], ids_ref[2]
        for core in range(2):
            for q in range(z_size):
                both = refs[1 + core * z_size + q][...].astype(single)
                pair[0] = both[:part]
                pair[1] = both[part:]
                blocks[z ^ step_of(q, b ^ core, z_size), b ^ core] = pair[b]
        for k in range(z_size):
            for core in range(2):
                g = 2 * k + core
                block = blocks[k, core]
                for i in range(3):
                    at = i * D + g * wide
                    in_ref[:, at : at + wide] = block[:, i * wide : (i + 1) * wide]
                kv_ref[:, g * kv_wide : (g + 1) * kv_wide] = block[:, 3 * wide :]

    return call(
        body,
        [shape((part, 3 * D), single), shape((part, 2 * D), single)],
        [ids] + list(near) + list(far),
        [SMEM] + [VMEM] * (2 * z_size),
        [pltpu.VMEM((z_size, 2, part, cols), single), pltpu.VMEM((2, part, cols), single)],
        megabytes=16,
        micros=0.1,
    )


def column_grads(ids, joined, x_all, text, grad_pairs, f_size):
    wide3 = joined.shape[0]
    kv_wide = grad_pairs.shape[0]
    rows = D // f_size
    cols = wide3 + kv_wide

    def body(ids_ref, joined_ref, x_ref, text_ref, pairs_ref, keep_ref, send_ref, turned, kv_s):
        f, b = ids_ref[0], ids_ref[2]
        turned[...] = dot(joined_ref[...], x_ref[...]).T
        kv_s[...] = dot(text_ref[...], pairs_ref[...], (0, 1))
        held = f_size // 2
        for q in range(f_size):
            place = pl.ds(aligned((f ^ step_of(q, b, f_size)) * rows, 8), rows)
            if q < held:
                keep_ref[q, :, 0:wide3] = turned[place, :]
                keep_ref[q, :, wide3:cols] = kv_s[place, :]
            else:
                send_ref[q - held, :, 0:wide3] = turned[place, :].astype(bfloat)
                send_ref[q - held, :, wide3:cols] = kv_s[place, :].astype(bfloat)

    return call(
        body,
        [
            shape((f_size // 2, rows, cols), single),
            shape((f_size // 2, rows, cols)),
        ],
        [ids, joined, x_all, text, grad_pairs],
        [SMEM] + [VMEM] * 4,
        [pltpu.VMEM((D, wide3), single), pltpu.VMEM((D, kv_wide), single)],
        megabytes=24,
        micros=1.5,
    )


def finish(ids, own, got, x, modulation, grad_first):
    tok = x.shape[0]
    n_got = len(got)

    def body(*refs):
        _, own_ref, x_ref, mod_ref, first_ref = refs[:5]
        got_refs = refs[5 : 5 + n_got]
        out_ref, stat_ref = refs[5 + n_got :]
        grad_mod = own_ref[...]
        for ref in got_refs:
            grad_mod = grad_mod + ref[...].astype(single)
        normed, inverse = layer_norm(x_ref[...].astype(single))
        stat_ref[0:1] = jnp.sum(grad_mod, axis=0, keepdims=True)
        stat_ref[1:2] = jnp.sum(grad_mod * normed, axis=0, keepdims=True)
        out_ref[...] = first_ref[...] + norm_back(grad_mod * (1.0 + mod_ref[1:2]), normed, inverse)

    return call(
        body,
        [shape((tok, D), single), shape((2, D), single)],
        [ids, own, x, modulation, grad_first] + list(got),
        [SMEM] + [VMEM] * (4 + n_got),
        micros=0.1,
    )


class Summing:
    def __init__(self, clock, value, axes):
        self.clock, self.value = clock, value
        self.axes = list(axes)

    def start(self):
        axis = self.axes.pop(0)
        size = lax.axis_size(axis)
        self.got = [self.clock.swap(self.value, axis, step) for step in range(1, size)]

    def wait(self):
        parts = self.clock.wait(self.value, *self.got)
        self.value = tree_sum(list(parts))

    def finish(self):
        self.wait()
        while self.axes:
            self.start()
            self.wait()


def shards(
    latents,
    text_embed,
    timestep,
    ada_table,
    w_attn_in,
    w_attn_out,
    w_cross_q,
    w_cross_kv,
    w_cross_out,
    w_mlp_up,
    w_mlp_down,
    grad_out,
):
    f_size = lax.axis_size("fsdp")
    z_size = lax.axis_size("ctx")
    group = 2 * z_size
    f = lax.axis_index("fsdp")
    z = lax.axis_index("ctx")
    b = lax.axis_index("blk")
    g = 2 * z + b
    ids = jnp.stack([f, z, b]).astype(jnp.int32)
    heads_here = HEADS // group
    wide = heads_here * HEAD
    kv_wide = 2 * D // group
    rows_f = D // f_size
    half_f = rows_f // 2
    own = D // (f_size * group)
    ff = w_mlp_up.shape[1] // f_size
    m_half = z_size // 2

    x = latents[0]
    cotangent = grad_out[0]
    text = text_embed[0]
    squares = [w_attn_out, w_cross_q, w_cross_out]
    clock = Clock(ids)
    run, swap_at, wait = clock.run, clock.swap, clock.wait

    def assemble(pieces, kinds):
        if half_f % 16 == 0:
            return pieces, kinds
        count = sum(kind[0] == "own" for kind in kinds)
        whole = jnp.zeros((count, f_size, rows_f, pieces[0].shape[-1]), bfloat)
        for part, kind in zip(pieces, kinds):
            if kind[0] == "own":
                whole = lax.dynamic_update_slice(whole, part[None, None], (kind[1], f, 0, 0))
            else:
                core = b if kind[0] == "near" else 1 - b
                part = part if kind[1] is None else part[kind[1]]
                whole = lax.dynamic_update_slice(
                    whole, part[:, None], (0, f ^ kind[2](core), core * half_f, 0)
                )
        return [whole.reshape(count, D, -1)], [("whole",)]

    class Events:
        def x0(self):
            self.x_z = Doubling(clock, x, "ctx")
            self.x_z.start()

        def x1(self):
            self.x_z.wait()
            self.x_z.start()

        def xc(self):
            self.x_far = [swap_at(part, "blk", 1) for part in (x, self.x_z.arrays[0])]

        def x2(self):
            self.x_z.finish()

        def xd0(self):
            self.x_far += [swap_at(part, "blk", 1) for part in self.x_z.arrays[1:]]

        def xd(self):
            *self.x_far, self.w_far[0] = wait(*self.x_far, self.w_far[0])

        def in0(self):
            self.own_in = jnp.concatenate(
                [
                    lax.dynamic_slice(w_attn_in, (0, i * D + g * wide), (rows_f, wide))
                    for i in range(3)
                ]
                + [lax.dynamic_slice(w_cross_kv, (0, g * kv_wide), (rows_f, kv_wide)), ada_table.T],
                axis=1,
            )
            self.in_f = Doubling(clock, self.own_in, "fsdp")
            self.in_f.start()

        def in1(self):
            self.in_f.wait()
            self.in_f.start()

        def in2(self):
            self.in_f.finish()

        def proj(self):
            self.w_t, self.kv_t, self.pairs_here, table = run(
                project_text, self.own_in, self.in_f.arrays, text, 3 * wide, kv_wide, f_size
            )
            self.modulation = table + timestep.reshape(6, D)

        def pz0(self):
            self.pair_z = Doubling(clock, self.pairs_here, "ctx")
            self.pair_z.start()

        def pz1(self):
            self.pair_z.wait()
            self.pair_z.start()

        def pc(self):
            self.pair_far = [
                swap_at(part, "blk", 1) for part in [self.pairs_here] + self.pair_z.arrays[:1]
            ]

        def pz2(self):
            self.pair_z.finish()
            self.pair_far += [swap_at(part, "blk", 1) for part in self.pair_z.arrays[1:]]

        def pd(self):
            self.pair_far = list(wait(*self.pair_far))

        def w0(self):
            half = jnp.stack(
                [lax.dynamic_slice(w, (b * half_f, 0), (half_f, D)) for w in squares], 0
            )
            self.w_f = Doubling(clock, half, "fsdp")
            self.w_f.start()

        def w1(self):
            self.w_f.wait()
            self.w_f.start()
            self.w_far = [swap_at(part, "blk", 1) for part in self.w_f.arrays]

        def w2(self):
            self.w_f.finish()
            self.w_far += [swap_at(part, "blk", 1) for part in self.w_f.arrays[1:]]

        def wd(self):
            self.w_far = self.w_far[:1] + list(wait(*self.w_far[1:], self.mixed[0])[:-1])
            pieces, kinds = list(squares), [("own", i) for i in range(3)]
            for name, arrays in (("near", self.w_f.arrays), ("far", self.w_far)):
                place = 1
                for part in arrays:
                    for i in range(part.shape[0]):
                        pieces.append(part)
                        kinds.append((name, i, functools.partial(step_of, place, size=f_size)))
                        place += 1
            self.pieces, self.kinds = assemble(pieces, kinds)

        def up0(self):
            up_half = lax.dynamic_slice(w_mlp_up, (b * half_f, 0), (half_f, f_size * ff))
            parts = [None] + [
                lax.dynamic_slice(up_half, (0, (f ^ step_of(q, b, f_size)) * ff), (half_f, ff))
                for q in range(1, f_size)
            ]
            self.up_f = Transposing(clock, parts, "fsdp")
            self.up_f.start()

        def upw(self):
            self.up_f.wait()

        def up1(self):
            self.up_f.start()

        def up2(self):
            self.up_f.finish()

        def upc(self):
            self.up_far = [
                swap_at(self.up_f.pieces[q][None], "blk", 1) for q in range(1, f_size)
            ]

        def upd(self):
            far = wait(*self.up_far)
            pieces = [lax.dynamic_slice(w_mlp_up, (0, f * ff), (rows_f, ff))]
            kinds = [("own", 0)]
            for q in range(1, f_size):
                place = functools.partial(step_of, q, size=f_size)
                got, i = self.up_f.found[q]
                pieces += [got[i][None], far[q - 1]]
                kinds += [("near", None, place), ("far", None, place)]
            self.up_pieces, self.up_kinds = assemble(pieces, kinds)

        def gb0(self):
            grad = (self.modulation[5:6] * cotangent.astype(single)).astype(bfloat)
            self.grad_f = Doubling(clock, grad, "fsdp")
            self.grad_f.start()

        def gbw(self):
            self.grad_f.wait()

        def gb1(self):
            self.grad_f.start()

        def gb2(self):
            self.grad_f.finish()
            self.branch_all = jnp.concatenate(self.grad_f.pieces, 0)

        def gbc(self):
            self.branch_far = swap_at(self.branch_all, "blk", 1)

        def gh(self):
            self.grad_hidden = wait(dot(self.branch_all, w_mlp_down, (1, 1)))

        def attn(self):
            parts = [x] + self.x_z.arrays + self.x_far
            kinds, at = [], 0
            for part in parts:
                n = 1 if part.ndim == 2 else part.shape[0]
                kinds.append(list(range(at, at + n)))
                at += n
            near, far, self.qkv, self.norm, self.x_all = run(
                attend_forward, self.w_t, self.modulation, parts, kinds, heads_here, z_size
            )
            self.mixed = (near, far)

        def ex0(self):
            self.to_owner = Exchange(clock, *self.mixed)

        def ex1(self):
            self.to_owner.cross()

        def ex2(self):
            self.to_owner.wait()

        def ex3(self):
            self.to_owner.finish()

        def tok(self):
            (
                self.x_two,
                self.second,
                self.branch_one,
                self.p,
                self.cq,
                self.left,
                self.left_send,
                self.pairs,
            ) = run(
                token_forward,
                self.to_owner.pieces,
                x,
                self.modulation,
                [self.pairs_here] + self.pair_z.arrays + self.pair_far,
                self.pieces,
                self.kinds,
                f_size,
                z_size,
            )

        def lc(self):
            self.left_far = swap_at(self.left_send, "blk", 1)

        def xt0(self):
            self.x_two_f = Doubling(clock, self.x_two, "fsdp")
            self.x_two_f.start()

        def xt1(self):
            self.x_two_f.wait()
            self.x_two_f.start()

        def xt2(self):
            self.x_two_f.finish()
            self.x_two_parts = [self.x_two] + self.x_two_f.arrays

        def ff(self):
            self.hidden, self.pre, keep, send = run(
                feed_forward,
                self.x_two_parts,
                self.grad_hidden,
                self.up_pieces,
                self.up_kinds,
                ff,
                f_size,
            )
            self.gm = Halving(clock, keep, send, "fsdp")

        def gm0(self):
            self.gm.start()

        def gm1(self):
            self.gm.wait()
            self.gm.start()

        def gm2(self):
            self.gm.finish()

        def prc(self):
            self.pre_far = swap_at(self.pre, "blk", 1)

        def turn(self):
            self.hk, self.hs, self.xk, self.xs = run(
                feed_forward_turn, self.x_two_parts, self.hidden, f_size, z_size
            )

        def hsc(self):
            self.hs = swap_at(self.hs, "blk", 1)

        def xsc(self):
            self.xs = swap_at(self.xs, "blk", 1)

        def hsd(self):
            self.hs, self.branch_far = wait(self.hs, self.branch_far)

        def down(self):
            terms = run(
                chip_grads, 1, self.hk, self.hs, self.branch_all, self.branch_far, z_size, False
            )
            self.d = Halving(clock, *terms, "ctx")

        def d0(self):
            self.d.start()

        def d1(self):
            self.d.wait()
            self.d.start()

        def d2(self):
            self.d.finish()

        def xsd(self):
            self.xs, self.pre_far = wait(self.xs, self.pre_far)

        def upg(self):
            self.u_own, send = run(
                chip_grads, 0, self.xk, self.xs, self.pre, self.pre_far, f_size, True
            )
            self.u_f = Direct(clock, [None] + [send[q - 1] for q in range(1, f_size)], "fsdp")

        def u0(self):
            self.u_f.start()

        def u2(self):
            self.u_f.finish()

        def us(self):
            got = [self.u_f.pieces[q][None] for q in range(1, f_size)]
            terms = run(sum_split, 1, self.u_own, got, z_size, False)
            self.u = Halving(clock, *terms, "ctx")

        def uz0(self):
            self.u.start()

        def uz1(self):
            self.u.wait()
            self.u.start()

        def uz2(self):
            self.u.finish()

        def out(self):
            terms = run(feed_forward_out, self.hidden, w_mlp_down, f_size)
            self.branch = Halving(clock, *terms, "fsdp")

        def br0(self):
            self.branch.start()

        def br1(self):
            self.branch.wait()
            self.branch.start()

        def br2(self):
            self.branch.finish()
            mlp_branch = self.branch.sum()
            self.block_out = (self.second + self.modulation[5:6] * mlp_branch).astype(bfloat)
            self.stat_gate = jnp.sum(cotangent.astype(single) * mlp_branch, axis=0, keepdims=True)

        def tb(self):
            (
                near,
                far,
                self.right,
                self.grad_first,
                self.stat_mid,
                self.pair_keep,
                self.pair_send,
            ) = run(
                token_backward,
                self.gm.own,
                [self.gm.last],
                self.second,
                self.branch_one,
                cotangent,
                self.modulation,
                self.p,
                self.cq,
                self.pairs,
                self.pieces,
                self.kinds,
                f_size,
                z_size,
            )
            self.grad_mixed = (near, far)

        def hx0(self):
            self.to_heads = Exchange(clock, *self.grad_mixed)

        def hx1(self):
            self.to_heads.cross()

        def hx2(self):
            self.to_heads.wait()

        def hx3(self):
            self.to_heads.finish()

        def rc(self):
            self.right_far = swap_at(self.right, "blk", 1)

        def rd(self):
            self.right_far, self.left_far = wait(self.right_far, self.left_far)

        def sq(self):
            terms = run(
                square_grads, self.left, self.left_far, self.right, self.right_far, f_size
            )
            self.s = Halving(clock, *terms, "fsdp")

        def s0(self):
            self.s.start()

        def s1(self):
            self.s.wait()
            self.s.start()

        def s2(self):
            self.s.finish()

        def ss(self):
            terms = run(sum_split, 1, self.s.own, [self.s.last], z_size, True)
            self.s = Halving(clock, *terms, "ctx")

        def sz0(self):
            self.s.start()

        def sz1(self):
            self.s.wait()
            self.s.start()

        def sz2(self):
            self.s.finish()

        def pg0(self):
            self.pair_back = swap_at(self.pair_send, "blk", 1)

        def pgd(self):
            value = self.pair_keep + wait(self.pair_back).astype(single)
            self.pair = Halving(clock, value[:m_half], value[m_half:].astype(bfloat), "ctx")

        def pp0(self):
            self.pair.start()

        def pp1(self):
            self.pair.wait()
            self.pair.start()

        def pp2(self):
            self.pair.finish()

        def tg(self):
            self.grad_pairs, self.text_keep, self.text_send = run(
                text_grads, self.pair.own, self.pair.last, self.kv_t
            )

        def tc0(self):
            self.text_got = swap_at(self.text_send, "blk", 1)

        def td0(self):
            self.grad_text = (self.text_keep + wait(self.text_got)).astype(bfloat)

        def tz0(self):
            self.text_got = cross(clock.gate(self.grad_text), "ctx", 0)
            self.text_stage = 1

        def tz1(self):
            value = self.grad_text.astype(single) + wait(self.text_got).astype(single)
            self.grad_text = value.astype(bfloat)
            self.text_got = cross(clock.gate(self.grad_text), "ctx", self.text_stage)
            self.text_stage += 1

        def tz2(self):
            while self.text_stage < bits_of(z_size):
                self.tz1()
            self.grad_text = self.grad_text.astype(single) + wait(self.text_got).astype(single)
            self.text_got = swap_at(self.grad_text, "blk", 1)

        def td1(self):
            self.text_got = wait(self.text_got)

        def h0(self):
            self.grads = list(
                run(attend_backward, 0, self.qkv, self.norm, self.to_heads.pieces, z_size)
            )

        def h1(self):
            for h in range(1, heads_here):
                self.grads += run(
                    attend_backward, h, self.qkv, self.norm, self.to_heads.pieces, z_size
                )

        def pj(self):
            self.close, self.away, self.joined = run(
                attend_project, self.grads, self.w_t, z_size
            )

        def ac(self):
            self.away = swap_at(self.away, "blk", 1)

        def ad(self):
            value = self.close + wait(self.away).astype(single)
            self.m = Halving(clock, value[:m_half], value[m_half:].astype(bfloat), "ctx")

        def m0(self):
            self.m.start()

        def m1(self):
            self.m.wait()
            self.m.start()

        def m2(self):
            self.m.finish()

        def col(self):
            terms = run(
                column_grads, self.joined, self.x_all, text, self.grad_pairs, f_size
            )
            self.c = Halving(clock, *terms, "fsdp")

        def c0(self):
            self.c.start()

        def c1(self):
            self.c.wait()
            self.c.start()

        def c2(self):
            self.c.finish()

        def sp(self):
            (rows,) = run(split_columns, self.c.own, self.c.last, z_size)
            self.to_rows = Transposing(clock, [rows[q] for q in range(z_size)], "ctx")

        def cx0(self):
            self.to_rows.start()

        def cx1(self):
            self.to_rows.wait()
            self.to_rows.start()

        def cx2(self):
            self.to_rows.finish()

        def cc(self):
            self.c_far = [swap_at(part, "blk", 1) for part in self.to_rows.pieces]

        def cd(self):
            self.c_far = list(wait(*self.c_far))

        def pl(self):
            self.grad_attn_in, self.grad_cross_kv = run(
                place_columns, self.to_rows.pieces, self.c_far, wide, z_size
            )

        def fin(self):
            self.grad_latents, self.stat_last = run(
                finish, self.m.own, [self.m.last], x, self.modulation, self.grad_first
            )

        def st0(self):
            rows = [self.stat_last, self.stat_mid, self.stat_gate]
            self.stamp = Summing(clock, jnp.concatenate(rows, axis=0), ("blk", "ctx"))
            self.stamp.start()

        def st1(self):
            self.stamp.wait()
            self.stamp.start()

        def st3(self):
            self.stamp.finish()
            self.table = Summing(clock, self.stamp.value, ("fsdp",))
            self.table.start()

        def st4(self):
            self.table.finish()

    e = Events()
    for event in (
        e.w0, e.x0, e.in0, e.up0, e.x1, e.xc, e.in1, e.w1, e.x2, e.xd0, e.in2, e.proj, e.pz0,
        e.gb0, e.xd, e.attn, e.ex0, e.gbw, e.pz1, e.ex1, e.upw, e.w2, e.ex2, e.pc, e.pz2, e.gb1,
        e.up1, e.pd, e.wd, e.ex3, e.tok, e.xt0, e.lc, e.gb2, e.gbc, e.xt1, e.up2, e.upc, e.gh,
        e.upd, e.xt2, e.ff, e.gm0, e.prc, e.turn, e.hsc, e.xsc, e.hsd, e.down, e.d0, e.gm1, e.xsd,
        e.upg, e.out, e.gm2, e.u0, e.tb, e.hx0, e.rc, e.hx1, e.rd, e.d1, e.sq, e.s0, e.hx2, e.u2,
        e.br0, e.us, e.pg0, e.hx3, e.pgd, e.pp0, e.uz0, e.h0, e.h1, e.br1, e.pp1, e.pj, e.s1, e.ac,
        e.d2, e.uz1, e.pp2, e.tg, e.tc0, e.br2, e.ad, e.m0, e.col, e.c0, e.td0, e.tz0, e.s2, e.ss,
        e.c1, e.uz2, e.tz1, e.m1, e.sz0, e.c2, e.sp, e.m2, e.fin, e.st0, e.st1, e.cx0, e.sz1,
        e.cx1, e.tz2, e.st3, e.cx2, e.cc, e.cd, e.pl, e.td1, e.st4, e.sz2,
    ):
        event()

    grad_table = lax.dynamic_slice(e.table.value, (0, (f * group + g) * own), (6, own))
    square_sum = e.s.sum().reshape(3, own, D)
    up = e.u.sum().reshape(f_size, own, ff)
    back = [up[back_of(q, f_size)] for q in range(f_size)]
    steps = [jnp.where(b == 0, up[q], back[q]) for q in range(f_size)]
    grad_text = jnp.concatenate(reorder([e.grad_text, e.text_got], b), axis=0).T

    return (
        e.block_out[None],
        e.grad_latents[None],
        grad_text[None],
        e.stamp.value.reshape(1, 6 * D),
        grad_table,
        e.grad_attn_in,
        square_sum[0],
        square_sum[1],
        e.grad_cross_kv,
        square_sum[2],
        jnp.concatenate(reorder(steps, f), axis=1),
        e.d.sum(),
        grad_table[3],
    )


def solution(mesh):
    placed = (
        P("fsdp", ("ctx", "blk"), None),
        P("fsdp", None, None),
        P("fsdp", None),
        P(None, "fsdp"),
        P("fsdp", None),
        P("fsdp", None),
        P("fsdp", None),
        P("fsdp", None),
        P("fsdp", None),
        P("fsdp", None),
        P("fsdp", None),
        P("fsdp", ("ctx", "blk"), None),
    )
    owned = P(("fsdp", "ctx", "blk"), None)
    return jax.shard_map(
        shards,
        mesh=mesh,
        in_specs=placed,
        out_specs=(
            P("fsdp", ("ctx", "blk"), None),
            P("fsdp", ("ctx", "blk"), None),
            P("fsdp", None, None),
            P("fsdp", None),
            P(None, ("fsdp", "ctx", "blk")),
            owned,
            owned,
            owned,
            owned,
            owned,
            owned,
            owned,
            P(("fsdp", "ctx", "blk")),
        ),
        check_vma=False,
    )
```
